32 devices in a mesh: dp: 16 (over z, y, core), tensor: 2 (over x).
Axes of the slice: x: 2, y: 2, z: 4, core: 2. Of those that a mesh axis runs over, the one named last changes fastest.
Arguments:
- hidden_in: bfloat16 [24576, 768], P(('dp', 'tensor')), may hold values from -6 to 6
- seq_lens: int32 [16], P('dp'), may hold values from 864 to 1536, as said below
- ln1_gain: float32 [768], replicated, may hold values from 0.5 to 1.5
- ln1_bias: float32 [768], replicated, may hold values from -4 to 4
- w_qkv: bfloat16 [3, 768, 768], P(None, 'dp', 'tensor'), may hold values from -0.21875 to 0.21875
- bias_qv: float32 [2, 768], replicated, may hold values from -4 to 4
- w_out: bfloat16 [768, 768], P('tensor', 'dp'), may hold values from -2 to 2
- bias_out: float32 [768], replicated, may hold values from -4 to 4
- ln2_gain: float32 [768], replicated, may hold values from 0.5 to 1.5
- ln2_bias: float32 [768], replicated, may hold values from -4 to 4
- w_up: bfloat16 [768, 3072], P('dp', 'tensor'), may hold values from -0.21875 to 0.21875
- bias_up: float32 [3072], replicated, may hold values from -4 to 4
- w_down: bfloat16 [3072, 768], P('tensor', 'dp'), may hold values from -0.109375 to 0.109375
- bias_down: float32 [768], replicated, may hold values from -4 to 4
- grad_out: bfloat16 [24576, 768], P(('dp', 'tensor')), may hold values from -6 to 6
Outputs:
- out: bfloat16 [24576, 768], P(('dp', 'tensor'))
- grad_in: float32 [24576, 768], P(('dp', 'tensor'))
- grad_ln1_gain: float32 [768], replicated
- grad_ln1_bias: float32 [768], replicated
- grad_w_qkv: float32 [3, 768, 768], P(None, 'dp', 'tensor')
- grad_bias_qv: float32 [2, 768], replicated
- grad_w_out: float32 [768, 768], P('tensor', 'dp')
- grad_bias_out: float32 [768], replicated
- grad_ln2_gain: float32 [768], replicated
- grad_ln2_bias: float32 [768], replicated
- grad_w_up: float32 [768, 3072], P('dp', 'tensor')
- grad_bias_up: float32 [3072], replicated
- grad_w_down: float32 [3072, 768], P('tensor', 'dp')
- grad_bias_down: float32 [768], replicated
The draws below stay inside these ranges and needn't reach their ends.
Inputs may be any that keep to these rules, and one draw needn't show every extreme that they name: Each index of dp holds one sequence in its first seq_lens slots, the rest being padding; some index holds exactly 1536 tokens in every draw.
All inputs are finite; a program needn't handle non-finite values.
Results may differ from the reference program's by a relative error of at most 0.02.
Values may be sent and summed in bfloat16 or wider, within the bound.
No kernel may reach another device: no remote copies, remote signals or barrier semaphores. Data moves between devices by JAX's collectives and lax.ppermute only.
A program may use at most 192 MiB of HBM per device.

```python
import jax
import jax.numpy as jnp
from jax import lax

H = 12
HD = 64
D = 768
FF = 3072
CAP = 1536
LEN_MIN = 864
TOKENS = 24576
N_DP = 16


def draw_seq_lens(key, part):
    key = jax.random.fold_in(key, 7)
    first_key, second_key = jax.random.split(key)
    lengths = jax.random.randint(first_key, (N_DP,), LEN_MIN, CAP + 1, dtype=jnp.int32)
    longest = jax.random.randint(second_key, (), 0, N_DP, dtype=jnp.int32)
    return jnp.where(jnp.arange(N_DP, dtype=jnp.int32) == longest, CAP, lengths).astype(jnp.int32)


def level_of(rng, extent, cuts, smallest, largest):
    factor_of = 1.0
    for position, parts in cuts:
        draws = jax.random.uniform(jax.random.fold_in(jax.random.fold_in(rng, 6), position), (parts,), jnp.float32, smallest / len(cuts), largest / len(cuts))
        factor_of = factor_of * jnp.repeat(jnp.exp(draws), extent[position] // parts).reshape((-1,) + (1,) * (len(extent) - 1 - position))
    return factor_of


def normal_values(stream_key, shape, scale, most, cuts=(), held_as=jnp.bfloat16):
    drawn = scale * jax.random.normal(stream_key, shape, jnp.float32)
    if cuts:
        drawn = drawn * level_of(stream_key, shape, cuts, -0.22, 0.18)
    return jnp.clip(drawn, -most, most).astype(held_as)


def setup_inputs(seed: int = 0) -> dict:
    key_of = jax.random.split(jax.random.key(seed), 16)
    return {
        "hidden_in": normal_values(key_of[0], (TOKENS, D), 1.0, 6.0, ((0, 32),)),
        "seq_lens": draw_seq_lens(jax.random.fold_in(key_of[15], 71), 0),
        "ln1_gain": jnp.clip(1.0 + 0.1 * jax.random.normal(key_of[2], (D,), jnp.float32), 0.5, 1.5),
        "ln1_bias": normal_values(key_of[3], (D,), 0.3, 4.0, (), jnp.float32),
        "w_qkv": normal_values(key_of[4], (3, D, D), D ** -0.5, 0.21875, ((1, 16), (2, 2))),
        "bias_qv": normal_values(key_of[5], (2, D), 0.3, 4.0, (), jnp.float32),
        "w_out": normal_values(key_of[6], (D, D), (max(D * 16 // CAP, 1)) ** -0.5, 2.0, ((0, 2), (1, 16))),
        "bias_out": normal_values(key_of[7], (D,), 0.3, 4.0, (), jnp.float32),
        "ln2_gain": jnp.clip(1.0 + 0.1 * jax.random.normal(key_of[8], (D,), jnp.float32), 0.5, 1.5),
        "ln2_bias": normal_values(key_of[9], (D,), 0.3, 4.0, (), jnp.float32),
        "w_up": normal_values(key_of[10], (D, FF), D ** -0.5, 0.21875, ((0, 16), (1, 2))),
        "bias_up": normal_values(key_of[11], (FF,), 0.3, 4.0, (), jnp.float32),
        "w_down": normal_values(key_of[12], (FF, D), FF ** -0.5, 0.109375, ((0, 2), (1, 16))),
        "bias_down": normal_values(key_of[13], (D,), 0.3, 4.0, (), jnp.float32),
        "grad_out": normal_values(key_of[14], (TOKENS, D), 1.0, 6.0, ((0, 32),)),
    }


@jax.custom_vjp
def low(v):
    return lax.optimization_barrier(v.astype(jnp.bfloat16)).astype(jnp.float32)

@jax.custom_vjp
def low_back(v):
    return v

def low_keep(v):
    return (low(v), None)

def low_pass(kept, grad):
    return (grad,)

def back_keep(v):
    return (v, None)

def back_low(kept, grad):
    return (low(grad),)
low.defvjp(low_keep, low_pass)
low_back.defvjp(back_keep, back_low)
epsilon = 1e-05
highest = lax.Precision.HIGHEST

def layer_norm(values, gain, shift):
    center = values - lax.optimization_barrier(jnp.mean(values, axis=-1, keepdims=True))
    spread = lax.optimization_barrier(jnp.mean(center * center, axis=-1, keepdims=True))
    return center * lax.rsqrt(spread + epsilon) * gain + shift

def attend_rows(queries, keys_all, values_all, length, begin_row):
    block_rows = min(512, CAP)
    query_block = lax.dynamic_slice_in_dim(queries, begin_row, block_rows, 0)
    scores = jnp.einsum('qhd,khd->hqk', query_block, keys_all, precision=highest) / jnp.sqrt(jnp.float32(HD))
    query_slots = begin_row + jnp.arange(block_rows, dtype=jnp.int32)
    key_slots = jnp.arange(CAP, dtype=jnp.int32)
    allowed = (key_slots[None, :] <= query_slots[:, None]) & (key_slots[None, :] < length)
    scores = low_back(jnp.where(allowed[None], scores, -1000000000.0))
    weights = low(jax.nn.softmax(scores, axis=-1))
    mixed = jnp.einsum('hqk,khd->qhd', weights, values_all, precision=highest)
    return mixed.reshape(block_rows, D)

def group_forward(residual_in, length, params):
    gain_one, shift_one, qkv_weight, qv_bias, out_weight, out_bias, gain_two, shift_two, up_weight, up_bias, down_weight, down_bias = params
    normed = low(layer_norm(residual_in, gain_one, shift_one))
    qkv_bias = jnp.stack([qv_bias[0], jnp.zeros_like(qv_bias[0]), qv_bias[1]])
    projected = jnp.einsum('rd,cde->cre', normed, qkv_weight, precision=highest) + qkv_bias[:, None, :]
    projected = low(low_back(projected))
    queries = projected[0].reshape(CAP, H, HD)
    keys_all = projected[1].reshape(CAP, H, HD)
    values_all = projected[2].reshape(CAP, H, HD)
    block_rows = min(512, CAP)
    checked = jax.checkpoint(attend_rows)
    starts = jnp.arange(CAP // block_rows, dtype=jnp.int32) * block_rows
    mixed = lax.map(lambda begin_row: checked(queries, keys_all, values_all, length, begin_row), starts)
    mixed = low(low_back(mixed.reshape(CAP, D)))
    hidden_one = residual_in + low_back(jnp.dot(mixed, out_weight, precision=highest) + out_bias)
    normed_two = low(layer_norm(hidden_one, gain_two, shift_two))
    pre_act = low_back(jnp.dot(normed_two, up_weight, precision=highest) + up_bias)
    activated = low(jax.nn.gelu(pre_act))
    return hidden_one + low_back(jnp.dot(activated, down_weight, precision=highest) + down_bias)

def reference(hidden_in, seq_lens, ln1_gain, ln1_bias, w_qkv, bias_qv, w_out, bias_out, ln2_gain, ln2_bias, w_up, bias_up, w_down, bias_down, grad_out):
    params = tuple((item.astype(jnp.float32) for item in (ln1_gain, ln1_bias, w_qkv, bias_qv, w_out, bias_out, ln2_gain, ln2_bias, w_up, bias_up, w_down, bias_down)))
    inputs = hidden_in.astype(jnp.float32).reshape(N_DP, CAP, D)

    def forward(inputs, params):
        checked_group = jax.checkpoint(group_forward)
        return lax.map(lambda pair: checked_group(pair[0], pair[1], params), (inputs, seq_lens))
    outputs, pullback = jax.vjp(forward, inputs, params)
    slots = jnp.arange(CAP, dtype=jnp.int32)
    valid = (slots[None, :] < seq_lens[:, None]).astype(jnp.float32)
    cotangent = grad_out.astype(jnp.float32).reshape(N_DP, CAP, D) * valid[:, :, None]
    grad_inputs, grad_params = pullback(cotangent)
    g_gain_one, g_shift_one, g_qkv, g_qv_bias, g_out, g_out_bias, g_gain_two, g_shift_two, g_up, g_up_bias, g_down, g_down_bias = grad_params
    return (outputs.reshape(TOKENS, D).astype(jnp.bfloat16), grad_inputs.reshape(TOKENS, D), g_gain_one, g_shift_one, g_qkv, g_qv_bias, g_out, g_out_bias, g_gain_two, g_shift_two, g_up, g_up_bias, g_down, g_down_bias)
```

```python
import functools
import math

import jax
import jax.numpy as jnp
from jax import lax
from jax.experimental import pallas as pl
from jax.experimental.pallas import tpu as pltpu
from jax.sharding import Mesh, PartitionSpec as P

HD = 64
LEN_MIN = 864
EPS = 1e-05
LANES = 128
BLOCK = 256
MASKED = -1000000000.0
F32 = jnp.float32
BF16 = jnp.bfloat16
NN = (((1,), (0,)), ((), ()))
NT = (((1,), (1,)), ((), ()))
TN = (((0,), (0,)), ((), ()))


def dot(left, right, dims=NN):
    return lax.dot_general(left, right, dims, preferred_element_type=F32)


def norm_stats(values):
    center = values - jnp.mean(values, axis=-1, keepdims=True)
    inverse = lax.rsqrt(jnp.mean(center * center, axis=-1, keepdims=True) + EPS)
    return center * inverse, inverse


def norm_back(grad, normed, inverse, gain):
    scaled = grad * gain
    back = inverse * (
        scaled
        - jnp.mean(scaled, axis=-1, keepdims=True)
        - normed * jnp.mean(scaled * normed, axis=-1, keepdims=True)
    )
    return back, jnp.sum(grad * normed, axis=0), jnp.sum(grad, axis=0)


def head_part(values, head):
    lane = lax.broadcasted_iota(jnp.int32, (1, LANES), 1)
    keep = (lane < HD) if head == 0 else (lane >= HD)
    return jnp.where(keep, values, jnp.zeros_like(values))


def lane_block(first):
    return pl.ds(pl.multiple_of(first, LANES), LANES)


def row_half(index, rows):
    return pl.ds(pl.multiple_of(index * rows, rows), rows)


def attend_forward_kernel(info, qkv_own, qkv_other, out_own, out_other, qkv, out):
    pair = pl.program_id(0)
    length, core = info[0], info[1]
    rows, width = qkv_own.shape[0], out_own.shape[1]
    blocks = 2 * rows // BLOCK

    @pl.when(pair == 0)
    def _():
        qkv[row_half(core, rows), :] = qkv_own[...]
        qkv[row_half(1 - core, rows), :] = qkv_other[...]

    first = pair * LANES

    def part(block, which):
        return qkv[block * BLOCK : (block + 1) * BLOCK, lane_block(which * width + first)]

    column = lax.broadcasted_iota(jnp.int32, (1, BLOCK), 1)
    row = lax.broadcasted_iota(jnp.int32, (BLOCK, 1), 0)

    def score(block, head):
        query = head_part(part(block, 0), head) * jnp.asarray(0.125, BF16)
        last = jnp.minimum(row + block * BLOCK, length - 1)
        scores = []
        for other in range(block + 1):
            piece = dot(query, part(other, 1), NT)
            if other == block or (other + 1) * BLOCK > LEN_MIN:
                piece = jnp.where(column + other * BLOCK <= last, piece, MASKED)
            scores.append(piece)
        return scores

    tasks = [(block, head) for block in range(blocks) for head in range(2)]
    upcoming = score(*tasks[0])
    kept = None
    for place, (block, head) in enumerate(tasks):
        scores = upcoming
        if place + 1 < len(tasks):
            upcoming = score(*tasks[place + 1])
        top = functools.reduce(jnp.maximum, scores)
        top = jnp.max(top, axis=1, keepdims=True)
        weights = [jnp.exp(piece - top) for piece in scores]
        total = jnp.sum(functools.reduce(jnp.add, weights), axis=1, keepdims=True)
        mixed = functools.reduce(
            jnp.add,
            [
                dot(weight.astype(BF16), head_part(part(other, 2), head))
                for other, weight in enumerate(weights)
            ],
        )
        mixed = mixed / total
        if head == 0:
            kept = mixed
        else:
            out[block * BLOCK : (block + 1) * BLOCK, lane_block(first)] = (kept + mixed).astype(BF16)

    @pl.when(pair == pl.num_programs(0) - 1)
    def _():
        out_own[...] = out[row_half(core, rows), :]
        out_other[...] = out[row_half(1 - core, rows), :]


def attend_forward(info, qkv_own, qkv_other):
    rows, width = qkv_own.shape[0], qkv_own.shape[1] // 3
    whole = pl.BlockSpec(memory_space=pltpu.VMEM)
    shape = jax.ShapeDtypeStruct((rows, width), BF16)
    return pl.pallas_call(
        attend_forward_kernel,
        grid=(width // LANES,),
        in_specs=[pl.BlockSpec(memory_space=pltpu.SMEM), whole, whole],
        out_specs=[whole, whole],
        out_shape=[shape, shape],
        scratch_shapes=[
            pltpu.VMEM((2 * rows, 3 * width), BF16),
            pltpu.VMEM((2 * rows, width), BF16),
        ],
        compiler_params=pltpu.CompilerParams(vmem_limit_bytes=48 * 1024 * 1024),
        name="attend_forward",
    )(info, qkv_own, qkv_other)


def attend_backward_kernel(
    info, qkv_own, qkv_other, grad_own, grad_other, back_own, back_other, qkv, grad, back, key_sum, value_sum
):
    pair = pl.program_id(0)
    length, core = info[0], info[1]
    rows, width = grad_own.shape
    blocks = 2 * rows // BLOCK

    @pl.when(pair == 0)
    def _():
        qkv[row_half(core, rows), :] = qkv_own[...]
        qkv[row_half(1 - core, rows), :] = qkv_other[...]
        grad[row_half(core, rows), :] = grad_own[...]
        grad[row_half(1 - core, rows), :] = grad_other[...]

    key_sum[...] = jnp.zeros_like(key_sum)
    value_sum[...] = jnp.zeros_like(value_sum)
    first = pair * LANES
    eighth = jnp.asarray(0.125, BF16)

    def span(block):
        return slice(block * BLOCK, (block + 1) * BLOCK)

    def part(block, which):
        return qkv[span(block), lane_block(which * width + first)]

    column = lax.broadcasted_iota(jnp.int32, (1, BLOCK), 1)
    row = lax.broadcasted_iota(jnp.int32, (BLOCK, 1), 0)

    def products(block, head):
        query = head_part(part(block, 0), head) * eighth
        mixed = head_part(grad[span(block), lane_block(first)], head)
        last = jnp.minimum(column + block * BLOCK, length - 1)
        scores, grads = [], []
        for other in range(block + 1):
            piece = dot(part(other, 1), query, NT)
            if other == block or (other + 1) * BLOCK > LEN_MIN:
                piece = jnp.where(row + other * BLOCK <= last, piece, MASKED)
            scores.append(piece)
            grads.append(dot(part(other, 2), mixed, NT))
        return query, mixed, scores, grads

    tasks = [(block, head) for block in range(blocks) for head in range(2)]
    upcoming = products(*tasks[0])
    kept = None
    for place, (block, head) in enumerate(tasks):
        query, mixed, scores, grads = upcoming
        if place + 1 < len(tasks):
            upcoming = products(*tasks[place + 1])
        top = jnp.max(functools.reduce(jnp.maximum, scores), axis=0, keepdims=True)
        weights = [jnp.exp(piece - top) for piece in scores]
        total = jnp.sum(functools.reduce(jnp.add, weights), axis=0, keepdims=True)
        inverse = 1.0 / total
        weights = [weight * inverse for weight in weights]
        products_sum = functools.reduce(jnp.add, [w * g for w, g in zip(weights, grads)])
        inner = jnp.sum(products_sum, axis=0, keepdims=True)
        query_sum = None
        for other in range(block + 1):
            weight = weights[other]
            change = (weight * (grads[other] - inner)).astype(BF16)
            value_sum[span(other), :] += dot(weight.astype(BF16), mixed)
            key_sum[span(other), :] += dot(change, query)
            piece = dot(change, head_part(part(other, 1), head) * eighth, TN)
            query_sum = piece if query_sum is None else query_sum + piece
        if head == 0:
            kept = query_sum
        else:
            back[span(block), lane_block(first)] = (kept + query_sum).astype(BF16)
    back[:, lane_block(width + first)] = key_sum[...].astype(BF16)
    back[:, lane_block(2 * width + first)] = value_sum[...].astype(BF16)

    @pl.when(pair == pl.num_programs(0) - 1)
    def _():
        back_own[...] = back[row_half(core, rows), :]
        back_other[...] = back[row_half(1 - core, rows), :]


def attend_backward(info, qkv_own, qkv_other, grad_own, grad_other):
    rows, width = grad_own.shape
    whole = pl.BlockSpec(memory_space=pltpu.VMEM)
    shape = jax.ShapeDtypeStruct((rows, 3 * width), BF16)
    return pl.pallas_call(
        attend_backward_kernel,
        grid=(width // LANES,),
        in_specs=[pl.BlockSpec(memory_space=pltpu.SMEM), whole, whole, whole, whole],
        out_specs=[whole, whole],
        out_shape=[shape, shape],
        scratch_shapes=[
            pltpu.VMEM((2 * rows, 3 * width), BF16),
            pltpu.VMEM((2 * rows, width), BF16),
            pltpu.VMEM((2 * rows, 3 * width), BF16),
            pltpu.VMEM((2 * rows, LANES), F32),
            pltpu.VMEM((2 * rows, LANES), F32),
        ],
        compiler_params=pltpu.CompilerParams(vmem_limit_bytes=48 * 1024 * 1024),
        name="attend_backward",
    )(info, qkv_own, qkv_other, grad_own, grad_other)


def swap(values):
    return lax.ppermute(values, ("core", "x"), [(0, 0), (1, 2), (2, 1), (3, 3)])


def exchange(values):
    return lax.ppermute(values, "core", [(0, 1), (1, 0)])


def gelu_parts(pre):
    slope = math.sqrt(2.0 / math.pi)
    bent = jnp.tanh(slope * (pre + 0.044715 * (pre * pre * pre)))
    value = 0.5 * pre * (1.0 + bent)
    change = 0.5 * (1.0 + bent) + 0.5 * pre * (1.0 - bent * bent) * slope * (1.0 + 3 * 0.044715 * pre * pre)
    return value, change


def shards(
    hidden_in,
    seq_lens,
    ln1_gain,
    ln1_bias,
    w_qkv,
    bias_qv,
    w_out,
    bias_out,
    ln2_gain,
    ln2_bias,
    w_up,
    bias_up,
    w_down,
    bias_down,
    grad_out,
):
    core = lax.axis_index("core")
    group = ("zy", "x")
    rows, width = hidden_in.shape
    shard_rows = w_up.shape[0]
    head_cols = w_qkv.shape[2]
    hidden_cols = w_up.shape[1]
    qkv_cols = 3 * head_cols

    residual_low = swap(hidden_in)
    length = swap(seq_lens)[0]
    attn_shard = swap(
        jnp.concatenate([w_qkv.transpose(1, 0, 2).reshape(shard_rows, qkv_cols), w_out.T], axis=1)
    )
    mlp_shard = swap(jnp.concatenate([w_up, w_down.T], axis=1))
    attn_weights = lax.all_gather(attn_shard, group, axis=0, tiled=True)
    mlp_weights = lax.all_gather(mlp_shard, group, axis=0, tiled=True)
    grad_low = swap(grad_out)

    qkv_weight, out_weight = attn_weights[:, :qkv_cols], attn_weights[:, qkv_cols:]
    up_weight, down_weight = mlp_weights[:, :hidden_cols], mlp_weights[:, hidden_cols:]
    info = jnp.stack([length, core.astype(jnp.int32)])

    residual = residual_low.astype(F32)
    unit_one, inverse_one = norm_stats(residual)
    norm_own = (unit_one * ln1_gain + ln1_bias).astype(BF16)
    norm_other = exchange(norm_own)
    bias_here = lax.dynamic_slice_in_dim(bias_qv, core * head_cols, head_cols, 1)
    qkv_bias = jnp.concatenate([bias_here[0], jnp.zeros((head_cols,), F32), bias_here[1]])
    qkv_own = (dot(norm_own, qkv_weight) + qkv_bias).astype(BF16)
    qkv_other = (dot(norm_other, qkv_weight) + qkv_bias).astype(BF16)
    mixed_own, mixed_other = attend_forward(info, qkv_own, qkv_other)
    attn_received = exchange(dot(mixed_other, out_weight, NT).astype(BF16))
    hidden = residual + (dot(mixed_own, out_weight, NT) + attn_received.astype(F32)) + bias_out
    unit_two, inverse_two = norm_stats(hidden)
    two_own = (unit_two * ln2_gain + ln2_bias).astype(BF16)
    two_other = exchange(two_own)
    bias_up_here = lax.dynamic_slice_in_dim(bias_up, core * hidden_cols, hidden_cols, 0)

    slots = core * rows + jnp.arange(rows, dtype=jnp.int32)
    grad_own = jnp.where((slots < length)[:, None], grad_low, jnp.zeros_like(grad_low))
    grad_other = exchange(grad_own)

    def feed(two, grad):
        pre = dot(two, up_weight) + bias_up_here
        value, change = gelu_parts(pre)
        active = value.astype(BF16)
        grad_pre = (dot(grad, down_weight) * change).astype(BF16)
        return active, grad_pre

    active_other, grad_pre_other = feed(two_other, grad_other)
    back_two_received = exchange(dot(grad_pre_other, up_weight, NT).astype(BF16))
    mlp_received = exchange(dot(active_other, down_weight, NT).astype(BF16))
    active_own, grad_pre_own = feed(two_own, grad_own)
    back_two = dot(grad_pre_own, up_weight, NT) + back_two_received.astype(F32)
    layer_out = hidden + (dot(active_own, down_weight, NT) + mlp_received.astype(F32)) + bias_down
    layer_out = swap(layer_out.astype(BF16))

    grad_up = dot(two_own, grad_pre_own, TN) + dot(two_other, grad_pre_other, TN)
    grad_down = dot(grad_own, active_own, TN) + dot(grad_other, active_other, TN)
    mlp_grads = jnp.concatenate([grad_up.astype(BF16), grad_down.astype(BF16)], axis=1)
    mlp_grads = swap(lax.psum_scatter(mlp_grads, group, scatter_dimension=0, tiled=True))

    back_hidden, gain_two_sum, shift_two_sum = norm_back(back_two, unit_two, inverse_two, ln2_gain)
    grad_hidden = grad_own.astype(F32) + back_hidden
    attn_grad_own = grad_hidden.astype(BF16)
    attn_grad_other = exchange(attn_grad_own)
    grad_mixed_own = dot(attn_grad_own, out_weight).astype(BF16)
    grad_mixed_other = dot(attn_grad_other, out_weight).astype(BF16)
    grad_outproj = dot(attn_grad_own, mixed_own, TN) + dot(attn_grad_other, mixed_other, TN)

    back_own, back_other = attend_backward(info, qkv_own, qkv_other, grad_mixed_own, grad_mixed_other)
    back_one_received = exchange(dot(back_other, qkv_weight, NT).astype(BF16))
    grad_qkv = dot(norm_own, back_own, TN) + dot(norm_other, back_other, TN)
    attn_grads = jnp.concatenate([grad_qkv.astype(BF16), grad_outproj.astype(BF16)], axis=1)
    attn_grads = swap(lax.psum_scatter(attn_grads, group, scatter_dimension=0, tiled=True))
    back_one = dot(back_own, qkv_weight, NT) + back_one_received.astype(F32)
    back_input, gain_one_sum, shift_one_sum = norm_back(back_one, unit_one, inverse_one, ln1_gain)
    grad_input = swap((grad_hidden + back_input).astype(BF16)).astype(F32)

    def place(values, full):
        return lax.dynamic_update_slice_in_dim(
            jnp.zeros(values.shape[:-1] + (full,), F32), values, core * values.shape[-1], values.ndim - 1
        )

    up_bias_sum = jnp.sum(grad_pre_own.astype(F32), axis=0) + jnp.sum(grad_pre_other.astype(F32), axis=0)
    back_sum = jnp.sum(back_own.astype(F32), axis=0) + jnp.sum(back_other.astype(F32), axis=0)
    qv_sum = jnp.stack([back_sum[:head_cols], back_sum[2 * head_cols :]])
    early = jnp.concatenate(
        [
            jnp.sum(grad_own.astype(F32), axis=0),
            gain_two_sum,
            shift_two_sum,
            jnp.sum(attn_grad_own.astype(F32), axis=0),
            place(up_bias_sum, bias_up.shape[0]),
        ]
    )
    late = jnp.concatenate([gain_one_sum, shift_one_sum, place(qv_sum, width).reshape(-1)])
    everyone = ("zy", "core", "x")
    early = lax.psum(early, everyone)
    late = lax.psum(late, everyone)
    down_bias, gain_two, shift_two, out_bias, up_bias = jnp.split(early, [width * n for n in range(1, 5)])
    gain_one, shift_one, qv_bias = jnp.split(late, [width, 2 * width])

    grad_w_qkv = attn_grads[:, :qkv_cols].reshape(shard_rows, 3, head_cols).transpose(1, 0, 2).astype(F32)
    grad_w_out = attn_grads[:, qkv_cols:].T.astype(F32)
    grad_w_up = mlp_grads[:, :hidden_cols].astype(F32)
    grad_w_down = mlp_grads[:, hidden_cols:].T.astype(F32)
    return (
        layer_out,
        grad_input,
        gain_one,
        shift_one,
        grad_w_qkv,
        qv_bias.reshape(2, width),
        grad_w_out,
        out_bias,
        gain_two,
        shift_two,
        grad_w_up,
        up_bias,
        grad_w_down,
        down_bias,
    )


def solution(mesh):
    cores = 2
    devices = mesh.devices
    inner = Mesh(devices.reshape(devices.shape[0] // cores, cores, devices.shape[1]), ("zy", "core", "x"))
    dp = ("zy", "core")
    token = P(("zy", "core", "x"), None)
    in_specs = (
        token,
        P(dp),
        P(),
        P(),
        P(None, dp, "x"),
        P(),
        P("x", dp),
        P(),
        P(),
        P(),
        P(dp, "x"),
        P(),
        P("x", dp),
        P(),
        token,
    )
    out_specs = (
        token,
        token,
        P(),
        P(),
        P(None, dp, "x"),
        P(),
        P("x", dp),
        P(),
        P(),
        P(),
        P(dp, "x"),
        P(),
        P("x", dp),
        P(),
    )
    return jax.shard_map(shards, mesh=inner, in_specs=in_specs, out_specs=out_specs, check_vma=False)
```

```python
import functools
import math

import jax
import jax.numpy as jnp
from jax import lax
from jax.experimental import pallas as pl
from jax.experimental.pallas import tpu as pltpu
from jax.sharding import Mesh, PartitionSpec as P

HD = 64
LEN_MIN = 864
EPS = 1e-05
LANES = 128
BLOCK = 256
MASKED = -1000000000.0
F32 = jnp.float32
BF16 = jnp.bfloat16
NN = (((1,), (0,)), ((), ()))
NT = (((1,), (1,)), ((), ()))
TN = (((0,), (0,)), ((), ()))


def dot(left, right, dims=NN):
    return lax.dot_general(left, right, dims, preferred_element_type=F32)


def norm_stats(values):
    center = values - jnp.mean(values, axis=-1, keepdims=True)
    inverse = lax.rsqrt(jnp.mean(center * center, axis=-1, keepdims=True) + EPS)
    return center * inverse, inverse


def norm_back(grad, normed, inverse, gain):
    scaled = grad * gain
    back = inverse * (
        scaled
        - jnp.mean(scaled, axis=-1, keepdims=True)
        - normed * jnp.mean(scaled * normed, axis=-1, keepdims=True)
    )
    return back, jnp.sum(grad * normed, axis=0), jnp.sum(grad, axis=0)


def head_part(values, head):
    lane = lax.broadcasted_iota(jnp.int32, (1, LANES), 1)
    keep = (lane < HD) if head == 0 else (lane >= HD)
    return jnp.where(keep, values, jnp.zeros_like(values))


def lane_block(first):
    return pl.ds(pl.multiple_of(first, LANES), LANES)


def row_half(index, rows):
    return pl.ds(pl.multiple_of(index * rows, rows), rows)


def span(block, size=BLOCK):
    return slice(block * size, (block + 1) * size)


def vmem():
    return pl.BlockSpec(memory_space=pltpu.VMEM)


def smem():
    return pl.BlockSpec(memory_space=pltpu.SMEM)


def limit(mib):
    return pltpu.CompilerParams(vmem_limit_bytes=mib * 1024 * 1024)


def fill_halves(target, core, own, other):
    rows = own.shape[0]
    target[row_half(core, rows), :] = own[...]
    target[row_half(1 - core, rows), :] = other[...]


def split_halves(source, core, own, other):
    rows = own.shape[0]
    own[...] = source[row_half(core, rows), :]
    other[...] = source[row_half(1 - core, rows), :]


def attend_forward_kernel(info, qkv_own, qkv_other, out_own, out_other, qkv, out):
    length, core = info[0], info[1]
    blocks = qkv.shape[0] // BLOCK
    fill_halves(qkv, core, qkv_own, qkv_other)

    def part(block, which):
        return qkv[span(block), span(which, LANES)]

    column = lax.broadcasted_iota(jnp.int32, (1, BLOCK), 1)
    row = lax.broadcasted_iota(jnp.int32, (BLOCK, 1), 0)

    def score(block, head):
        query = head_part(part(block, 0), head) * jnp.asarray(0.125, BF16)
        last = jnp.minimum(row + block * BLOCK, length - 1)
        scores = []
        for other in range(block + 1):
            piece = dot(query, part(other, 1), NT)
            if other == block or (other + 1) * BLOCK > LEN_MIN:
                piece = jnp.where(column + other * BLOCK <= last, piece, MASKED)
            scores.append(piece)
        return scores

    tasks = [(block, head) for block in range(blocks) for head in range(2)]
    upcoming = score(*tasks[0])
    kept = None
    for place, (block, head) in enumerate(tasks):
        scores = upcoming
        if place + 1 < len(tasks):
            upcoming = score(*tasks[place + 1])
        top = functools.reduce(jnp.maximum, scores)
        top = jnp.max(top, axis=1, keepdims=True)
        weights = [jnp.exp(piece - top) for piece in scores]
        total = jnp.sum(functools.reduce(jnp.add, weights), axis=1, keepdims=True)
        mixed = functools.reduce(
            jnp.add,
            [
                dot(weight.astype(BF16), head_part(part(other, 2), head))
                for other, weight in enumerate(weights)
            ],
        )
        mixed = mixed / total
        if head == 0:
            kept = mixed
        else:
            out[span(block), :] = (kept + mixed).astype(BF16)
    split_halves(out, core, out_own, out_other)


def attend_forward(info, qkv_own, qkv_other):
    rows, width = qkv_own.shape[0], qkv_own.shape[1] // 3
    taken = pl.BlockSpec((rows, 3 * LANES), lambda pair: (0, pair))
    given = pl.BlockSpec((rows, LANES), lambda pair: (0, pair))
    shape = jax.ShapeDtypeStruct((rows, width), BF16)
    return pl.pallas_call(
        attend_forward_kernel,
        grid=(width // LANES,),
        in_specs=[smem(), taken, taken],
        out_specs=[given, given],
        out_shape=[shape, shape],
        scratch_shapes=[
            pltpu.VMEM((2 * rows, 3 * LANES), BF16),
            pltpu.VMEM((2 * rows, LANES), BF16),
        ],
        compiler_params=limit(32),
        name="attend_forward",
    )(info, qkv_own, qkv_other)


def attend_backward_kernel(
    info, qkv_own, qkv_other, grad_own, grad_other, back_own, back_other, qkv, grad, back, key_sum, value_sum
):
    length, core = info[0], info[1]
    blocks = qkv.shape[0] // BLOCK
    fill_halves(qkv, core, qkv_own, qkv_other)
    fill_halves(grad, core, grad_own, grad_other)
    key_sum[...] = jnp.zeros_like(key_sum)
    value_sum[...] = jnp.zeros_like(value_sum)
    eighth = jnp.asarray(0.125, BF16)

    def part(block, which):
        return qkv[span(block), span(which, LANES)]

    column = lax.broadcasted_iota(jnp.int32, (1, BLOCK), 1)
    row = lax.broadcasted_iota(jnp.int32, (BLOCK, 1), 0)

    def products(block, head):
        query = head_part(part(block, 0), head) * eighth
        mixed = head_part(grad[span(block), :], head)
        last = jnp.minimum(column + block * BLOCK, length - 1)
        scores, grads = [], []
        for other in range(block + 1):
            piece = dot(part(other, 1), query, NT)
            if other == block or (other + 1) * BLOCK > LEN_MIN:
                piece = jnp.where(row + other * BLOCK <= last, piece, MASKED)
            scores.append(piece)
            grads.append(dot(part(other, 2), mixed, NT))
        return query, mixed, scores, grads

    tasks = [(block, head) for block in range(blocks) for head in range(2)]
    upcoming = products(*tasks[0])
    kept = None
    for place, (block, head) in enumerate(tasks):
        query, mixed, scores, grads = upcoming
        if place + 1 < len(tasks):
            upcoming = products(*tasks[place + 1])
        top = jnp.max(functools.reduce(jnp.maximum, scores), axis=0, keepdims=True)
        weights = [jnp.exp(piece - top) for piece in scores]
        total = jnp.sum(functools.reduce(jnp.add, weights), axis=0, keepdims=True)
        inverse = 1.0 / total
        weights = [weight * inverse for weight in weights]
        products_sum = functools.reduce(jnp.add, [w * g for w, g in zip(weights, grads)])
        inner = jnp.sum(products_sum, axis=0, keepdims=True)
        query_sum = None
        for other in range(block + 1):
            weight = weights[other]
            change = (weight * (grads[other] - inner)).astype(BF16)
            value_sum[span(other), :] += dot(weight.astype(BF16), mixed)
            key_sum[span(other), :] += dot(change, query)
            piece = dot(change, head_part(part(other, 1), head) * eighth, TN)
            query_sum = piece if query_sum is None else query_sum + piece
        if head == 0:
            kept = query_sum
        else:
            back[span(block), span(0, LANES)] = (kept + query_sum).astype(BF16)
    back[:, span(1, LANES)] = key_sum[...].astype(BF16)
    back[:, span(2, LANES)] = value_sum[...].astype(BF16)
    split_halves(back, core, back_own, back_other)


def attend_backward(pair, info, qkv_own, qkv_other, grad_own, grad_other):
    rows = grad_own.shape[0]
    qkv_spec = pl.BlockSpec((rows, 3 * LANES), lambda step: (0, pair))
    grad_spec = pl.BlockSpec((rows, LANES), lambda step: (0, pair))
    shape = jax.ShapeDtypeStruct((rows, 3 * LANES), BF16)
    return pl.pallas_call(
        attend_backward_kernel,
        grid=(1,),
        in_specs=[smem(), qkv_spec, qkv_spec, grad_spec, grad_spec],
        out_specs=[vmem(), vmem()],
        out_shape=[shape, shape],
        scratch_shapes=[
            pltpu.VMEM((2 * rows, 3 * LANES), BF16),
            pltpu.VMEM((2 * rows, LANES), BF16),
            pltpu.VMEM((2 * rows, 3 * LANES), BF16),
            pltpu.VMEM((2 * rows, LANES), F32),
            pltpu.VMEM((2 * rows, LANES), F32),
        ],
        compiler_params=limit(32),
        name=f"attend_backward_{pair}",
    )(info, qkv_own, qkv_other, grad_own, grad_other)


def feed_kernel(two, grad, weight, bias, active, grad_pre, mlp, back, bias_sum):
    hidden = active.shape[1]
    slope = math.sqrt(2.0 / math.pi)
    cubic = slope * 0.044715
    for chunk in range(hidden // BLOCK):
        here = span(chunk)
        there = slice(hidden + chunk * BLOCK, hidden + (chunk + 1) * BLOCK)
        pre = dot(two[...], weight[:, here]) + bias[:, here]
        grad_active = dot(grad[...], weight[:, there])
        square = pre * pre
        half = 0.5 + 0.5 * jnp.tanh(pre * (slope + cubic * square))
        value = pre * half
        change = half + (value - value * half) * (2.0 * slope + (6.0 * cubic) * square)
        active[:, here] = value.astype(BF16)
        low = (grad_active * change).astype(BF16)
        grad_pre[:, here] = low
        bias_sum[:, here] = jnp.sum(low.astype(F32), axis=0, keepdims=True)
    for chunk in range(mlp.shape[1] // BLOCK):
        here = span(chunk)
        back[:, here] = dot(grad_pre[...], weight[here, :hidden], NT).astype(back.dtype)
        mlp[:, here] = dot(active[...], weight[here, hidden:], NT).astype(mlp.dtype)


def feed(two, grad, weight, bias, result, name):
    rows, width = two.shape
    hidden = weight.shape[1] // 2
    low = jax.ShapeDtypeStruct((rows, hidden), BF16)
    terms = jax.ShapeDtypeStruct((rows, width), result)
    return pl.pallas_call(
        feed_kernel,
        in_specs=[vmem()] * 4,
        out_specs=[vmem()] * 5,
        out_shape=[low, low, terms, terms, jax.ShapeDtypeStruct((1, hidden), F32)],
        compiler_params=limit(24),
        name=name,
    )(two, grad, weight, bias)


def weight_grads_kernel(count, shard, order, *refs):
    lefts_own, lefts_other = refs[:count], refs[count : 2 * count]
    rights_own, rights_other = refs[2 * count : 3 * count], refs[3 * count : 4 * count]
    out, total = refs[4 * count], refs[4 * count + 1]
    first = 0
    for term in range(count):
        columns = rights_own[term].shape[1]
        for chunk in range(total.shape[0] // BLOCK):
            here = span(chunk)
            piece = dot(lefts_own[term][:, here], rights_own[term][...], TN)
            piece += dot(lefts_other[term][:, here], rights_other[term][...], TN)
            total[here, first : first + columns] = piece.astype(BF16)
        first += columns
    for place in range(total.shape[0] // shard):
        start = pl.multiple_of(order[place] * shard, 16)
        out[span(place, shard), :] = total[pl.ds(start, shard), :]


def weight_grads(order, terms, name):
    width = terms[0][0].shape[1]
    columns = sum(term[2].shape[1] for term in terms)
    shard = width // order.shape[0]
    operands = [term[kind] for kind in range(4) for term in terms]
    return pl.pallas_call(
        functools.partial(weight_grads_kernel, len(terms), shard),
        in_specs=[smem()] + [vmem()] * len(operands),
        out_specs=vmem(),
        out_shape=jax.ShapeDtypeStruct((width, columns), BF16),
        scratch_shapes=[pltpu.VMEM((width, columns), BF16)],
        compiler_params=limit(24),
        name=name,
    )(order, *operands)


def place_kernel(shard, order, *refs):
    pieces, out = refs[:-1], refs[-1]
    place = 0
    for piece in pieces:
        for step in range(piece.shape[0] // shard):
            start = pl.multiple_of(order[place] * shard, 16)
            out[pl.ds(start, shard), :] = piece[span(step, shard), :]
            place += 1


def place_blocks(order, pieces):
    shard, columns = pieces[0].shape
    return pl.pallas_call(
        functools.partial(place_kernel, shard),
        in_specs=[smem()] + [vmem()] * len(pieces),
        out_specs=vmem(),
        out_shape=jax.ShapeDtypeStruct((shard * order.shape[0], columns), BF16),
        name="place_blocks",
    )(order, *pieces)


class Cube:
    def __init__(self, shard_rows):
        self.shard_rows = shard_rows
        self.zy = lax.axis_size("zy")
        self.cores = lax.axis_size("core")
        self.size = self.zy * lax.axis_size("x")
        self.bits = self.size.bit_length() - 1
        self.direct = self.size == 1 << self.bits and self.bits >= 2 and shard_rows % 16 == 0
        outer = list(range(self.bits - 1, 1, -1))
        self.dims = [outer + [0, 1], outer + [1, 0]]
        if self.direct:
            masks = [
                [sum(1 << dims[step] for step in range(self.bits) if place >> step & 1) for place in range(self.size)]
                for dims in self.dims
            ]
            mine = lax.axis_index("zy") * 2 + lax.axis_index("x")
            core = lax.axis_index("core")
            chosen = jnp.where(core == 0, jnp.array(masks[0], jnp.int32), jnp.array(masks[1], jnp.int32))
            self.order = jnp.bitwise_xor(mine.astype(jnp.int32), chosen)
        else:
            blocks = shard_rows * self.size // 48
            self.order = jnp.arange(blocks, dtype=jnp.int32)

    def send(self, values, step):
        pairs = []
        for zy in range(self.zy):
            for core in range(self.cores):
                for x in range(2):
                    other = (zy * 2 + x) ^ (1 << self.dims[core][step])
                    pairs.append(((zy * 2 + core) * 2 + x, (other // 2 * 2 + core) * 2 + other % 2))
        return lax.ppermute(values, ("zy", "core", "x"), pairs)

    def gather(self, shard):
        if not self.direct:
            return lax.all_gather(shard, ("zy", "x"), axis=0, tiled=True)
        pieces = [shard]
        for step in range(self.bits):
            payload = pieces[0] if step == 0 else jnp.concatenate(pieces, axis=0)
            pieces.append(self.send(payload, step))
        return place_blocks(self.order, pieces)

    def steps(self):
        return self.bits if self.direct else 1

    def reduce_step(self, values, step):
        if not self.direct:
            return lax.psum_scatter(values, ("zy", "x"), scatter_dimension=0, tiled=True)
        half = values.shape[0] // 2
        received = self.send(values[half:], self.bits - 1 - step)
        return (values[:half].astype(F32) + received.astype(F32)).astype(BF16)


def swap_small(values):
    return lax.ppermute(values, ("core", "x"), [(0, 0), (1, 2), (2, 1), (3, 3)])


def swap(values):
    received = lax.ppermute(values, ("core", "x"), [(1, 2), (2, 1)])
    return jnp.where(lax.axis_index("core") == lax.axis_index("x"), values, received)


def exchange(values):
    return lax.ppermute(values, "core", [(0, 1), (1, 0)])


def tie(values, other):
    return lax.optimization_barrier((values, other))


def shards(
    hidden_in,
    seq_lens,
    ln1_gain,
    ln1_bias,
    w_qkv,
    bias_qv,
    w_out,
    bias_out,
    ln2_gain,
    ln2_bias,
    w_up,
    bias_up,
    w_down,
    bias_down,
    grad_out,
):
    core = lax.axis_index("core")
    group = ("zy", "x")
    everyone = ("zy", "core", "x")
    rows, width = hidden_in.shape
    shard_rows = w_up.shape[0]
    head_cols = w_qkv.shape[2]
    hidden_cols = w_up.shape[1]
    pairs = head_cols // LANES
    qkv_cols = 3 * head_cols
    cube = Cube(shard_rows)

    qkv_shard = w_qkv.reshape(3, shard_rows, pairs, LANES).transpose(1, 2, 0, 3).reshape(shard_rows, qkv_cols)
    attn_shard = swap_small(jnp.concatenate([qkv_shard, w_out.T], axis=1))
    length = swap_small(seq_lens)[0]
    residual_low = swap(hidden_in)
    mlp_shard = swap_small(jnp.concatenate([w_up, w_down.T], axis=1))
    attn_weights = cube.gather(attn_shard)
    mlp_weights = lax.all_gather(mlp_shard, group, axis=0, tiled=True)
    grad_low = swap(grad_out)

    qkv_weight, out_weight = attn_weights[:, :qkv_cols], attn_weights[:, qkv_cols:]
    info = jnp.stack([length, core.astype(jnp.int32)])

    residual = residual_low.astype(F32)
    unit_one, inverse_one = norm_stats(residual)
    norm_own = (unit_one * ln1_gain + ln1_bias).astype(BF16)
    norm_other = exchange(norm_own)
    bias_here = lax.dynamic_slice_in_dim(bias_qv, core * head_cols, head_cols, 1)
    qkv_bias = jnp.stack([bias_here[0], jnp.zeros((head_cols,), F32), bias_here[1]])
    qkv_bias = qkv_bias.reshape(3, pairs, LANES).transpose(1, 0, 2).reshape(qkv_cols)
    qkv_own = (dot(norm_own, qkv_weight) + qkv_bias).astype(BF16)
    qkv_other = (dot(norm_other, qkv_weight) + qkv_bias).astype(BF16)
    mixed_own, mixed_other = attend_forward(info, qkv_own, qkv_other)
    attn_received = exchange(dot(mixed_other, out_weight, NT).astype(BF16))
    hidden = residual + (dot(mixed_own, out_weight, NT) + attn_received.astype(F32)) + bias_out
    unit_two, inverse_two = norm_stats(hidden)
    two_own = (unit_two * ln2_gain + ln2_bias).astype(BF16)
    two_other = exchange(two_own)
    bias_up_here = lax.dynamic_slice_in_dim(bias_up, core * hidden_cols, hidden_cols, 0)[None]

    slots = core * rows + jnp.arange(rows, dtype=jnp.int32)
    grad_own = jnp.where((slots < length)[:, None], grad_low, jnp.zeros_like(grad_low))
    grad_other = exchange(grad_own)

    active_other, grad_pre_other, mlp_other, back_two_other, up_sum_other = feed(
        two_other, grad_other, mlp_weights, bias_up_here, BF16, "feed_other"
    )
    back_two_received = exchange(back_two_other)
    mlp_received = exchange(mlp_other)
    active_own, grad_pre_own, mlp_own, back_two_own, up_sum_own = feed(
        two_own, grad_own, mlp_weights, bias_up_here, F32, "feed_own"
    )
    layer_out = swap((hidden + (mlp_own + mlp_received.astype(F32)) + bias_down).astype(BF16))

    back_two = back_two_own + back_two_received.astype(F32)
    back_hidden, gain_two_sum, shift_two_sum = norm_back(back_two, unit_two, inverse_two, ln2_gain)
    grad_hidden = grad_own.astype(F32) + back_hidden
    attn_grad_own = grad_hidden.astype(BF16)
    attn_grad_other = exchange(attn_grad_own)
    first_grads = weight_grads(
        cube.order,
        [
            (two_own, two_other, grad_pre_own, grad_pre_other),
            (grad_own, grad_other, active_own, active_other),
            (attn_grad_own, attn_grad_other, mixed_own, mixed_other),
        ],
        "first_weight_grads",
    )
    grad_mixed_own = dot(attn_grad_own, out_weight).astype(BF16)
    grad_mixed_other = dot(attn_grad_other, out_weight).astype(BF16)

    def place(values, full):
        return lax.dynamic_update_slice_in_dim(
            jnp.zeros(values.shape[:-1] + (full,), F32), values, core * values.shape[-1], values.ndim - 1
        )

    early = jnp.concatenate(
        [
            jnp.sum(grad_own.astype(F32), axis=0),
            gain_two_sum,
            shift_two_sum,
            jnp.sum(attn_grad_own.astype(F32), axis=0),
            place((up_sum_own + up_sum_other)[0], bias_up.shape[0]),
        ]
    )
    early = jnp.sum(lax.all_gather(early, everyone), axis=0)

    backs_own, backs_other = [], []
    grad_pair = (grad_mixed_own, grad_mixed_other)
    for pair in range(pairs):
        if pair < cube.steps():
            first_grads, grad_pair = tie(first_grads, grad_pair)
            first_grads = cube.reduce_step(first_grads, pair)
        back_own, back_other = attend_backward(pair, info, qkv_own, qkv_other, *grad_pair)
        backs_own.append(back_own)
        backs_other.append(back_other)
    for step in range(pairs, cube.steps()):
        first_grads = cube.reduce_step(first_grads, step)
    back_own = jnp.concatenate(backs_own, axis=1)
    back_other = jnp.concatenate(backs_other, axis=1)

    last_grads = weight_grads(
        cube.order, [(norm_own, norm_other, back_own, back_other)], "last_weight_grads"
    )
    for step in range(cube.steps()):
        last_grads = cube.reduce_step(last_grads, step)
    back_one_received = exchange(dot(back_other, qkv_weight, NT).astype(BF16))
    back_one = dot(back_own, qkv_weight, NT) + back_one_received.astype(F32)
    back_input, gain_one_sum, shift_one_sum = norm_back(back_one, unit_one, inverse_one, ln1_gain)
    grad_input = swap((grad_hidden + back_input).astype(BF16)).astype(F32)

    back_sum = jnp.sum(back_own.astype(F32), axis=0) + jnp.sum(back_other.astype(F32), axis=0)
    back_sum = back_sum.reshape(pairs, 3, LANES).transpose(1, 0, 2).reshape(3, head_cols)
    qv_sum = jnp.stack([back_sum[0], back_sum[2]])
    late = jnp.concatenate([gain_one_sum, shift_one_sum, place(qv_sum, width).reshape(-1)])
    late = jnp.sum(lax.all_gather(late, everyone), axis=0)
    down_bias, gain_two, shift_two, out_bias, up_bias = jnp.split(early, [width * n for n in range(1, 5)])
    gain_one, shift_one, qv_bias = jnp.split(late, [width, 2 * width])

    first_grads = swap_small(first_grads)
    last_grads = swap_small(last_grads)
    grad_w_qkv = last_grads.reshape(shard_rows, pairs, 3, LANES).transpose(2, 0, 1, 3)
    grad_w_qkv = grad_w_qkv.reshape(3, shard_rows, head_cols).astype(F32)
    grad_w_up = first_grads[:, :hidden_cols].astype(F32)
    grad_w_down = first_grads[:, hidden_cols : 2 * hidden_cols].T.astype(F32)
    grad_w_out = first_grads[:, 2 * hidden_cols :].T.astype(F32)
    return (
        layer_out,
        grad_input,
        gain_one,
        shift_one,
        grad_w_qkv,
        qv_bias.reshape(2, width),
        grad_w_out,
        out_bias,
        gain_two,
        shift_two,
        grad_w_up,
        up_bias,
        grad_w_down,
        down_bias,
    )


def solution(mesh):
    cores = 2
    devices = mesh.devices
    inner = Mesh(devices.reshape(devices.shape[0] // cores, cores, devices.shape[1]), ("zy", "core", "x"))
    dp = ("zy", "core")
    token = P(("zy", "core", "x"), None)
    in_specs = (
        token,
        P(dp),
        P(),
        P(),
        P(None, dp, "x"),
        P(),
        P("x", dp),
        P(),
        P(),
        P(),
        P(dp, "x"),
        P(),
        P("x", dp),
        P(),
        token,
    )
    out_specs = (
        token,
        token,
        P(),
        P(),
        P(None, dp, "x"),
        P(),
        P("x", dp),
        P(),
        P(),
        P(),
        P(dp, "x"),
        P(),
        P("x", dp),
        P(),
    )
    return jax.shard_map(shards, mesh=inner, in_specs=in_specs, out_specs=out_specs, check_vma=False)
```

```python
import functools
import math

import jax
import jax.numpy as jnp
from jax import lax
from jax.experimental import pallas as pl
from jax.experimental.pallas import tpu as pltpu
from jax.sharding import Mesh, PartitionSpec as P

HD = 64
LEN_MIN = 864
EPS = 1e-05
LANES = 128
BLOCK = 256
MASKED = -1000000000.0
F32 = jnp.float32
BF16 = jnp.bfloat16
NN = (((1,), (0,)), ((), ()))
NT = (((1,), (1,)), ((), ()))
TN = (((0,), (0,)), ((), ()))


def dot(left, right, dims=NN):
    return lax.dot_general(left, right, dims, preferred_element_type=F32)


def norm_stats(values):
    center = values - jnp.mean(values, axis=-1, keepdims=True)
    inverse = lax.rsqrt(jnp.mean(center * center, axis=-1, keepdims=True) + EPS)
    return center * inverse, inverse


def norm_back(grad, normed, inverse, gain):
    scaled = grad * gain
    back = inverse * (
        scaled
        - jnp.mean(scaled, axis=-1, keepdims=True)
        - normed * jnp.mean(scaled * normed, axis=-1, keepdims=True)
    )
    return back, jnp.sum(grad * normed, axis=0), jnp.sum(grad, axis=0)


def head_part(values, head):
    lane = lax.broadcasted_iota(jnp.int32, (1, LANES), 1)
    keep = (lane < HD) if head == 0 else (lane >= HD)
    return jnp.where(keep, values, jnp.zeros_like(values))


def lane_block(first):
    return pl.ds(pl.multiple_of(first, LANES), LANES)


def row_half(index, rows):
    return pl.ds(pl.multiple_of(index * rows, rows), rows)


def span(block, size=BLOCK):
    return slice(block * size, (block + 1) * size)


def vmem():
    return pl.BlockSpec(memory_space=pltpu.VMEM)


def smem():
    return pl.BlockSpec(memory_space=pltpu.SMEM)


def limit(mib):
    return pltpu.CompilerParams(vmem_limit_bytes=mib * 1024 * 1024)


def cost(microseconds):
    return pl.CostEstimate(flops=int(microseconds * 1.1e9), transcendentals=0, bytes_accessed=1)


def fill_halves(target, core, own, other):
    rows = own.shape[0]
    target[row_half(core, rows), :] = own[...]
    target[row_half(1 - core, rows), :] = other[...]


def split_halves(source, core, own, other):
    rows = own.shape[0]
    own[...] = source[row_half(core, rows), :]
    other[...] = source[row_half(1 - core, rows), :]


def attend_forward_kernel(info, qkv_own, qkv_other, out_own, out_other, qkv, out):
    length, core = info[0], info[1]
    blocks = qkv.shape[0] // BLOCK
    fill_halves(qkv, core, qkv_own, qkv_other)

    def part(block, which):
        return qkv[span(block), span(which, LANES)]

    column = lax.broadcasted_iota(jnp.int32, (1, BLOCK), 1)
    row = lax.broadcasted_iota(jnp.int32, (BLOCK, 1), 0)

    def score(block, head):
        query = head_part(part(block, 0), head) * jnp.asarray(0.125, BF16)
        last = jnp.minimum(row + block * BLOCK, length - 1)
        scores = []
        for other in range(block + 1):
            piece = dot(query, part(other, 1), NT)
            if other == block or (other + 1) * BLOCK > LEN_MIN:
                piece = jnp.where(column + other * BLOCK <= last, piece, MASKED)
            scores.append(piece)
        return scores

    tasks = [(block, head) for block in range(blocks) for head in range(2)]
    upcoming = score(*tasks[0])
    kept = None
    for place, (block, head) in enumerate(tasks):
        scores = upcoming
        if place + 1 < len(tasks):
            upcoming = score(*tasks[place + 1])
        top = functools.reduce(jnp.maximum, scores)
        top = jnp.max(top, axis=1, keepdims=True)
        weights = [jnp.exp(piece - top) for piece in scores]
        total = jnp.sum(functools.reduce(jnp.add, weights), axis=1, keepdims=True)
        mixed = functools.reduce(
            jnp.add,
            [
                dot(weight.astype(BF16), head_part(part(other, 2), head))
                for other, weight in enumerate(weights)
            ],
        )
        mixed = mixed / total
        if head == 0:
            kept = mixed
        else:
            out[span(block), :] = (kept + mixed).astype(BF16)
    split_halves(out, core, out_own, out_other)


def attend_forward(info, qkv_own, qkv_other):
    rows, width = qkv_own.shape[0], qkv_own.shape[1] // 3
    taken = pl.BlockSpec((rows, 3 * LANES), lambda pair: (0, pair))
    given = pl.BlockSpec((rows, LANES), lambda pair: (0, pair))
    shape = jax.ShapeDtypeStruct((rows, width), BF16)
    return pl.pallas_call(
        attend_forward_kernel,
        grid=(width // LANES,),
        in_specs=[smem(), taken, taken],
        out_specs=[given, given],
        out_shape=[shape, shape],
        scratch_shapes=[
            pltpu.VMEM((2 * rows, 3 * LANES), BF16),
            pltpu.VMEM((2 * rows, LANES), BF16),
        ],
        compiler_params=limit(32),
        cost_estimate=cost(15),
        name="attend_forward",
    )(info, qkv_own, qkv_other)


def attend_backward_kernel(
    info, qkv_own, qkv_other, grad_own, grad_other, back_own, back_other, qkv, grad, back, key_sum, value_sum
):
    length, core = info[0], info[1]
    blocks = qkv.shape[0] // BLOCK
    fill_halves(qkv, core, qkv_own, qkv_other)
    fill_halves(grad, core, grad_own, grad_other)
    key_sum[...] = jnp.zeros_like(key_sum)
    value_sum[...] = jnp.zeros_like(value_sum)
    eighth = jnp.asarray(0.125, BF16)

    def part(block, which):
        return qkv[span(block), span(which, LANES)]

    column = lax.broadcasted_iota(jnp.int32, (1, BLOCK), 1)
    row = lax.broadcasted_iota(jnp.int32, (BLOCK, 1), 0)

    def products(block, head):
        query = head_part(part(block, 0), head) * eighth
        mixed = head_part(grad[span(block), :], head)
        last = jnp.minimum(column + block * BLOCK, length - 1)
        scores, grads = [], []
        for other in range(block + 1):
            piece = dot(part(other, 1), query, NT)
            if other == block or (other + 1) * BLOCK > LEN_MIN:
                piece = jnp.where(row + other * BLOCK <= last, piece, MASKED)
            scores.append(piece)
            grads.append(dot(part(other, 2), mixed, NT))
        return query, mixed, scores, grads

    tasks = [(block, head) for block in range(blocks) for head in range(2)]
    upcoming = products(*tasks[0])
    kept = None
    for place, (block, head) in enumerate(tasks):
        query, mixed, scores, grads = upcoming
        if place + 1 < len(tasks):
            upcoming = products(*tasks[place + 1])
        top = jnp.max(functools.reduce(jnp.maximum, scores), axis=0, keepdims=True)
        weights = [jnp.exp(piece - top) for piece in scores]
        total = jnp.sum(functools.reduce(jnp.add, weights), axis=0, keepdims=True)
        inverse = 1.0 / total
        weights = [weight * inverse for weight in weights]
        products_sum = functools.reduce(jnp.add, [w * g for w, g in zip(weights, grads)])
        inner = jnp.sum(products_sum, axis=0, keepdims=True)
        query_sum = None
        for other in range(block + 1):
            weight = weights[other]
            change = (weight * (grads[other] - inner)).astype(BF16)
            value_sum[span(other), :] += dot(weight.astype(BF16), mixed)
            key_sum[span(other), :] += dot(change, query)
            piece = dot(change, head_part(part(other, 1), head) * eighth, TN)
            query_sum = piece if query_sum is None else query_sum + piece
        if head == 0:
            kept = query_sum
        else:
            back[span(block), span(0, LANES)] = (kept + query_sum).astype(BF16)
    back[:, span(1, LANES)] = key_sum[...].astype(BF16)
    back[:, span(2, LANES)] = value_sum[...].astype(BF16)
    split_halves(back, core, back_own, back_other)


def attend_backward(pair, info, qkv_own, qkv_other, grad_own, grad_other):
    rows = grad_own.shape[0]
    qkv_spec = pl.BlockSpec((rows, 3 * LANES), lambda step: (0, pair))
    grad_spec = pl.BlockSpec((rows, LANES), lambda step: (0, pair))
    shape = jax.ShapeDtypeStruct((rows, 3 * LANES), BF16)
    return pl.pallas_call(
        attend_backward_kernel,
        grid=(1,),
        in_specs=[smem(), qkv_spec, qkv_spec, grad_spec, grad_spec],
        out_specs=[vmem(), vmem()],
        out_shape=[shape, shape],
        scratch_shapes=[
            pltpu.VMEM((2 * rows, 3 * LANES), BF16),
            pltpu.VMEM((2 * rows, LANES), BF16),
            pltpu.VMEM((2 * rows, 3 * LANES), BF16),
            pltpu.VMEM((2 * rows, LANES), F32),
            pltpu.VMEM((2 * rows, LANES), F32),
        ],
        compiler_params=limit(32),
        cost_estimate=cost(13),
        name=f"attend_backward_{pair}",
    )(info, qkv_own, qkv_other, grad_own, grad_other)


def feed_kernel(two, grad, weight, bias, active, grad_pre, mlp, back, bias_sum):
    hidden = active.shape[1]
    slope = math.sqrt(2.0 / math.pi)
    cubic = slope * 0.044715
    for chunk in range(hidden // BLOCK):
        here = span(chunk)
        there = slice(hidden + chunk * BLOCK, hidden + (chunk + 1) * BLOCK)
        pre = dot(two[...], weight[:, here]) + bias[:, here]
        grad_active = dot(grad[...], weight[:, there])
        square = pre * pre
        half = 0.5 + 0.5 * jnp.tanh(pre * (slope + cubic * square))
        value = pre * half
        change = half + (value - value * half) * (2.0 * slope + (6.0 * cubic) * square)
        active[:, here] = value.astype(BF16)
        low = (grad_active * change).astype(BF16)
        grad_pre[:, here] = low
        bias_sum[:, here] = jnp.sum(low.astype(F32), axis=0, keepdims=True)
    for chunk in range(mlp.shape[1] // BLOCK):
        here = span(chunk)
        back[:, here] = dot(grad_pre[...], weight[here, :hidden], NT).astype(back.dtype)
        mlp[:, here] = dot(active[...], weight[here, hidden : 2 * hidden], NT).astype(mlp.dtype)


def feed(two, grad, weight, bias, result, name):
    rows, width = two.shape
    hidden = bias.shape[1]
    low = jax.ShapeDtypeStruct((rows, hidden), BF16)
    terms = jax.ShapeDtypeStruct((rows, width), result)
    return pl.pallas_call(
        feed_kernel,
        in_specs=[vmem()] * 4,
        out_specs=[vmem()] * 5,
        out_shape=[low, low, terms, terms, jax.ShapeDtypeStruct((1, hidden), F32)],
        compiler_params=limit(24),
        cost_estimate=cost(12),
        name=name,
    )(two, grad, weight, bias)


def weight_grads_kernel(count, shard, order, *refs):
    lefts_own, lefts_other = refs[:count], refs[count : 2 * count]
    rights_own, rights_other = refs[2 * count : 3 * count], refs[3 * count : 4 * count]
    out, total = refs[4 * count], refs[4 * count + 1]
    first = 0
    for term in range(count):
        columns = rights_own[term].shape[1]
        for chunk in range(total.shape[0] // BLOCK):
            here = span(chunk)
            piece = dot(lefts_own[term][:, here], rights_own[term][...], TN)
            piece += dot(lefts_other[term][:, here], rights_other[term][...], TN)
            total[here, first : first + columns] = piece.astype(BF16)
        first += columns
    if shard is None:
        out[...] = total[...]
        return
    for place in range(total.shape[0] // shard):
        start = pl.multiple_of(order[place] * shard, 16)
        out[span(place, shard), :] = total[pl.ds(start, shard), :]


def weight_grads(order, terms, name):
    width = terms[0][0].shape[1]
    columns = sum(term[2].shape[1] for term in terms)
    shard = None if order is None else width // order.shape[0]
    order = jnp.zeros((1,), jnp.int32) if order is None else order
    operands = [term[kind] for kind in range(4) for term in terms]
    return pl.pallas_call(
        functools.partial(weight_grads_kernel, len(terms), shard),
        in_specs=[smem()] + [vmem()] * len(operands),
        out_specs=vmem(),
        out_shape=jax.ShapeDtypeStruct((width, columns), BF16),
        scratch_shapes=[pltpu.VMEM((width, columns), BF16)],
        compiler_params=limit(24),
        cost_estimate=cost(columns / 300),
        name=name,
    )(order, *operands)


def place_kernel(shard, order, *refs):
    pieces, out = refs[:-1], refs[-1]
    place = 0
    for piece in pieces:
        for step in range(piece.shape[0] // shard):
            start = pl.multiple_of(order[place] * shard, 16)
            out[pl.ds(start, shard), :] = piece[span(step, shard), :]
            place += 1


def place_blocks(order, pieces):
    shard, columns = pieces[0].shape
    return pl.pallas_call(
        functools.partial(place_kernel, shard),
        in_specs=[smem()] + [vmem()] * len(pieces),
        out_specs=vmem(),
        out_shape=jax.ShapeDtypeStruct((shard * order.shape[0], columns), BF16),
        name="place_blocks",
    )(order, *pieces)


class Cube:
    def __init__(self, shard_rows):
        self.shard_rows = shard_rows
        self.zy = lax.axis_size("zy")
        self.cores = lax.axis_size("core")
        self.size = self.zy * lax.axis_size("x")
        self.bits = self.size.bit_length() - 1
        self.direct = self.size == 1 << self.bits and self.bits >= 2 and shard_rows % 16 == 0
        outer = list(range(self.bits - 1, 1, -1))
        self.dims = [outer + [0, 1], outer + [1, 0]]
        if self.direct:
            masks = [
                [sum(1 << dims[step] for step in range(self.bits) if place >> step & 1) for place in range(self.size)]
                for dims in self.dims
            ]
            mine = lax.axis_index("zy") * 2 + lax.axis_index("x")
            core = lax.axis_index("core")
            chosen = jnp.where(core == 0, jnp.array(masks[0], jnp.int32), jnp.array(masks[1], jnp.int32))
            self.order = jnp.bitwise_xor(mine.astype(jnp.int32), chosen)
        else:
            blocks = shard_rows * self.size // 48
            self.order = jnp.arange(blocks, dtype=jnp.int32)

    def send(self, values, step):
        pairs = []
        for zy in range(self.zy):
            for core in range(self.cores):
                for x in range(2):
                    other = (zy * 2 + x) ^ (1 << self.dims[core][step])
                    pairs.append(((zy * 2 + core) * 2 + x, (other // 2 * 2 + core) * 2 + other % 2))
        return lax.ppermute(values, ("zy", "core", "x"), pairs)

    def gather(self, shard):
        if not self.direct:
            return lax.all_gather(shard, ("zy", "x"), axis=0, tiled=True)
        pieces = [shard]
        for step in range(self.bits):
            payload = pieces[0] if step == 0 else jnp.concatenate(pieces, axis=0)
            pieces.append(self.send(payload, step))
        return place_blocks(self.order, pieces)

    def payload(self, values):
        return values[values.shape[0] // 2 :]

    def reduce_send(self, payload, step):
        return self.send(payload, self.bits - 1 - step)

    def merge(self, values, received):
        return (values[: values.shape[0] // 2].astype(F32) + received.astype(F32)).astype(BF16)

    def scatter(self, values):
        return lax.psum_scatter(values, ("zy", "x"), scatter_dimension=0, tiled=True)

    def total(self, values):
        if not self.direct:
            return lax.psum(values, ("zy", "core", "x"))
        for step in range(self.bits):
            values = values + self.send(values, step)
        return values + exchange(values)


def swap_small(values):
    return lax.ppermute(values, ("core", "x"), [(0, 0), (1, 2), (2, 1), (3, 3)])


def swap(values):
    received = lax.ppermute(values, ("core", "x"), [(1, 2), (2, 1)])
    return jnp.where(lax.axis_index("core") == lax.axis_index("x"), values, received)


def exchange(values):
    return lax.ppermute(values, "core", [(0, 1), (1, 0)])


def tie(values, other):
    return lax.optimization_barrier((values, other))


def shards(
    hidden_in,
    seq_lens,
    ln1_gain,
    ln1_bias,
    w_qkv,
    bias_qv,
    w_out,
    bias_out,
    ln2_gain,
    ln2_bias,
    w_up,
    bias_up,
    w_down,
    bias_down,
    grad_out,
):
    core = lax.axis_index("core")
    group = ("zy", "x")
    rows, width = hidden_in.shape
    shard_rows = w_up.shape[0]
    head_cols = w_qkv.shape[2]
    hidden_cols = w_up.shape[1]
    pairs = head_cols // LANES
    qkv_cols = 3 * head_cols
    cube = Cube(shard_rows)

    qkv_shard = w_qkv.reshape(3, shard_rows, pairs, LANES).transpose(1, 2, 0, 3).reshape(shard_rows, qkv_cols)
    first_low = swap(jnp.concatenate([hidden_in, qkv_shard.reshape(-1, width)], axis=0))
    residual_low = first_low[:rows]
    rest_shard = swap(jnp.concatenate([w_up, w_down.T, w_out.T], axis=1))
    length = swap_small(seq_lens)[0]
    qkv_weight = cube.gather(first_low[rows:].reshape(shard_rows, qkv_cols))
    rest_weights = lax.all_gather(rest_shard, group, axis=0, tiled=True)
    grad_low = swap(grad_out)

    out_weight = rest_weights[:, 2 * hidden_cols :]
    info = jnp.stack([length, core.astype(jnp.int32)])

    residual = residual_low.astype(F32)
    unit_one, inverse_one = norm_stats(residual)
    norm_own = (unit_one * ln1_gain + ln1_bias).astype(BF16)
    norm_other = exchange(norm_own)
    bias_here = lax.dynamic_slice_in_dim(bias_qv, core * head_cols, head_cols, 1)
    qkv_bias = jnp.stack([bias_here[0], jnp.zeros((head_cols,), F32), bias_here[1]])
    qkv_bias = qkv_bias.reshape(3, pairs, LANES).transpose(1, 0, 2).reshape(qkv_cols)
    qkv_own = (dot(norm_own, qkv_weight) + qkv_bias).astype(BF16)
    qkv_other = (dot(norm_other, qkv_weight) + qkv_bias).astype(BF16)
    mixed_own, mixed_other = attend_forward(info, qkv_own, qkv_other)
    attn_received = exchange(dot(mixed_other, out_weight, NT).astype(BF16))
    hidden = residual + (dot(mixed_own, out_weight, NT) + attn_received.astype(F32)) + bias_out
    unit_two, inverse_two = norm_stats(hidden)
    two_own = (unit_two * ln2_gain + ln2_bias).astype(BF16)
    two_other = exchange(two_own)
    bias_up_here = lax.dynamic_slice_in_dim(bias_up, core * hidden_cols, hidden_cols, 0)[None]

    slots = core * rows + jnp.arange(rows, dtype=jnp.int32)
    grad_own = jnp.where((slots < length)[:, None], grad_low, jnp.zeros_like(grad_low))
    grad_other = exchange(grad_own)

    active_other, grad_pre_other, mlp_other, back_two_other, up_sum_other = feed(
        two_other, grad_other, rest_weights, bias_up_here, BF16, "feed_other"
    )
    back_two_received = exchange(back_two_other)
    mlp_received = exchange(mlp_other)
    active_own, grad_pre_own, mlp_own, back_two_own, up_sum_own = feed(
        two_own, grad_own, rest_weights, bias_up_here, F32, "feed_own"
    )
    layer_out = swap((hidden + (mlp_own + mlp_received.astype(F32)) + bias_down).astype(BF16))

    down_grads = weight_grads(None, [(grad_own, grad_other, active_own, active_other)], "down_grads")
    down_grads = cube.scatter(down_grads)

    back_two = back_two_own + back_two_received.astype(F32)
    back_hidden, gain_two_sum, shift_two_sum = norm_back(back_two, unit_two, inverse_two, ln2_gain)
    grad_hidden = grad_own.astype(F32) + back_hidden
    attn_grad_own = grad_hidden.astype(BF16)
    attn_grad_other = exchange(attn_grad_own)
    first_grads = weight_grads(
        cube.order,
        [
            (two_own, two_other, grad_pre_own, grad_pre_other),
            (attn_grad_own, attn_grad_other, mixed_own, mixed_other),
        ],
        "first_weight_grads",
    )
    grad_mixed_own = dot(attn_grad_own, out_weight).astype(BF16)
    grad_mixed_other = dot(attn_grad_other, out_weight).astype(BF16)

    def place(values):
        empty = jnp.zeros_like(values)
        return jnp.where(
            core == 0,
            jnp.concatenate([values, empty], axis=-1),
            jnp.concatenate([empty, values], axis=-1),
        )

    early = jnp.concatenate(
        [
            jnp.sum(grad_own.astype(F32), axis=0),
            gain_two_sum,
            shift_two_sum,
            jnp.sum(attn_grad_own.astype(F32), axis=0),
            place((up_sum_own + up_sum_other)[0]),
        ]
    )
    early_size = early.shape[0]
    if cube.direct:
        early = early.reshape(16, -1).astype(BF16)
        early = jnp.pad(early, ((0, 0), (0, first_grads.shape[1] - early.shape[1])))
    else:
        early = cube.total(early)
        first_grads = cube.scatter(first_grads)

    backs_own, backs_other = [], []
    grad_pair = (grad_mixed_own, grad_mixed_other)
    steps = cube.bits if cube.direct else 0
    for pair in range(max(pairs, steps)):
        received = None
        if pair < steps:
            payload = jnp.concatenate([cube.payload(first_grads), early], axis=0)
            payload, grad_pair = tie(payload, grad_pair)
            received = cube.reduce_send(payload, pair)
        if pair < pairs:
            back_own, back_other = attend_backward(pair, info, qkv_own, qkv_other, *grad_pair)
            if received is not None:
                received, back_own = tie(received, back_own)
            backs_own.append(back_own)
            backs_other.append(back_other)
        if received is not None:
            first_grads = cube.merge(first_grads, received[:-16])
            early = (early.astype(F32) + received[-16:].astype(F32)).astype(BF16)
    if cube.direct:
        early = early[:, : early_size // 16].reshape(-1).astype(F32)
        early = early + exchange(early)
    back_own = jnp.concatenate(backs_own, axis=1)
    back_other = jnp.concatenate(backs_other, axis=1)

    back_one_received = exchange(dot(back_other, qkv_weight, NT).astype(BF16))
    last_grads = weight_grads(
        cube.order, [(norm_own, norm_other, back_own, back_other)], "last_weight_grads"
    )
    if cube.direct:
        for step in range(steps):
            last_grads = cube.merge(last_grads, cube.reduce_send(cube.payload(last_grads), step))
    else:
        last_grads = cube.scatter(last_grads)
    back_one = dot(back_own, qkv_weight, NT) + back_one_received.astype(F32)
    back_input, gain_one_sum, shift_one_sum = norm_back(back_one, unit_one, inverse_one, ln1_gain)
    grad_input = swap((grad_hidden + back_input).astype(BF16)).astype(F32)

    back_sum = jnp.sum(back_own.astype(F32), axis=0) + jnp.sum(back_other.astype(F32), axis=0)
    back_sum = back_sum.reshape(pairs, 3, LANES).transpose(1, 0, 2).reshape(3, head_cols)
    qv_sum = jnp.stack([back_sum[0], back_sum[2]])
    late = cube.total(jnp.concatenate([gain_one_sum, shift_one_sum, place(qv_sum).reshape(-1)]))
    down_bias, gain_two, shift_two, out_bias, up_bias = jnp.split(early, [width * n for n in range(1, 5)])
    gain_one, shift_one, qv_bias = jnp.split(late, [width, 2 * width])

    done_grads = swap(jnp.concatenate([first_grads, down_grads, last_grads], axis=1))
    done_grads, last_grads = done_grads[:, :-qkv_cols], done_grads[:, -qkv_cols:]
    grad_w_qkv = last_grads.reshape(shard_rows, pairs, 3, LANES).transpose(2, 0, 1, 3)
    grad_w_qkv = grad_w_qkv.reshape(3, shard_rows, head_cols).astype(F32)
    grad_w_up = done_grads[:, :hidden_cols].astype(F32)
    grad_w_out = done_grads[:, hidden_cols : hidden_cols + head_cols].T.astype(F32)
    grad_w_down = done_grads[:, hidden_cols + head_cols :].T.astype(F32)
    return (
        layer_out,
        grad_input,
        gain_one,
        shift_one,
        grad_w_qkv,
        qv_bias.reshape(2, width),
        grad_w_out,
        out_bias,
        gain_two,
        shift_two,
        grad_w_up,
        up_bias,
        grad_w_down,
        down_bias,
    )


def solution(mesh):
    cores = 2
    devices = mesh.devices
    inner = Mesh(devices.reshape(devices.shape[0] // cores, cores, devices.shape[1]), ("zy", "core", "x"))
    dp = ("zy", "core")
    token = P(("zy", "core", "x"), None)
    in_specs = (
        token,
        P(dp),
        P(),
        P(),
        P(None, dp, "x"),
        P(),
        P("x", dp),
        P(),
        P(),
        P(),
        P(dp, "x"),
        P(),
        P("x", dp),
        P(),
        token,
    )
    out_specs = (
        token,
        token,
        P(),
        P(),
        P(None, dp, "x"),
        P(),
        P("x", dp),
        P(),
        P(),
        P(),
        P(dp, "x"),
        P(),
        P("x", dp),
        P(),
    )
    return jax.shard_map(shards, mesh=inner, in_specs=in_specs, out_specs=out_specs, check_vma=False)
```

```python
import functools
import math

import jax
import jax.numpy as jnp
from jax import lax
from jax.experimental import pallas as pl
from jax.experimental.pallas import tpu as pltpu
from jax.sharding import Mesh, PartitionSpec as P

HD = 64
LEN_MIN = 864
EPS = 1e-05
LANES = 128
BLOCK = 256
MASKED = -1000000000.0
F32 = jnp.float32
BF16 = jnp.bfloat16
NN = (((1,), (0,)), ((), ()))
NT = (((1,), (1,)), ((), ()))
TN = (((0,), (0,)), ((), ()))


def dot(left, right, dims=NN):
    return lax.dot_general(left, right, dims, preferred_element_type=F32)


def norm_stats(values):
    center = values - jnp.mean(values, axis=-1, keepdims=True)
    inverse = lax.rsqrt(jnp.mean(center * center, axis=-1, keepdims=True) + EPS)
    return center * inverse, inverse


def norm_back(grad, normed, inverse, gain):
    scaled = grad * gain
    back = inverse * (
        scaled
        - jnp.mean(scaled, axis=-1, keepdims=True)
        - normed * jnp.mean(scaled * normed, axis=-1, keepdims=True)
    )
    return back, jnp.sum(grad * normed, axis=0), jnp.sum(grad, axis=0)


def head_part(values, head):
    lane = lax.broadcasted_iota(jnp.int32, (1, LANES), 1)
    keep = (lane < HD) if head == 0 else (lane >= HD)
    return jnp.where(keep, values, jnp.zeros_like(values))


def lane_block(first):
    return pl.ds(pl.multiple_of(first, LANES), LANES)


def row_half(index, rows):
    return pl.ds(pl.multiple_of(index * rows, rows), rows)


def span(block, size=BLOCK):
    return slice(block * size, (block + 1) * size)


def vmem():
    return pl.BlockSpec(memory_space=pltpu.VMEM)


def smem():
    return pl.BlockSpec(memory_space=pltpu.SMEM)


def limit(mib):
    return pltpu.CompilerParams(vmem_limit_bytes=mib * 1024 * 1024)


def cost(microseconds):
    return pl.CostEstimate(flops=int(microseconds * 1.1e9), transcendentals=0, bytes_accessed=1)


def fill_halves(target, core, own, other):
    rows = own.shape[0]
    target[row_half(core, rows), :] = own[...]
    target[row_half(1 - core, rows), :] = other[...]


def split_halves(source, core, own, other):
    rows = own.shape[0]
    own[...] = source[row_half(core, rows), :]
    other[...] = source[row_half(1 - core, rows), :]


def attend_forward_kernel(info, qkv_own, qkv_other, out_own, out_other, qkv, out):
    length, core = info[0], info[1]
    blocks = qkv.shape[0] // BLOCK
    fill_halves(qkv, core, qkv_own, qkv_other)

    def part(block, which):
        return qkv[span(block), span(which, LANES)]

    column = lax.broadcasted_iota(jnp.int32, (1, BLOCK), 1)
    row = lax.broadcasted_iota(jnp.int32, (BLOCK, 1), 0)

    def score(block, head):
        query = head_part(part(block, 0), head) * jnp.asarray(0.125, BF16)
        last = jnp.minimum(row + block * BLOCK, length - 1)
        scores = []
        for other in range(block + 1):
            piece = dot(query, part(other, 1), NT)
            if other == block or (other + 1) * BLOCK > LEN_MIN:
                piece = jnp.where(column + other * BLOCK <= last, piece, MASKED)
            scores.append(piece)
        return scores

    tasks = [(block, head) for block in range(blocks) for head in range(2)]
    upcoming = score(*tasks[0])
    kept = None
    for place, (block, head) in enumerate(tasks):
        scores = upcoming
        if place + 1 < len(tasks):
            upcoming = score(*tasks[place + 1])
        top = functools.reduce(jnp.maximum, scores)
        top = jnp.max(top, axis=1, keepdims=True)
        weights = [jnp.exp(piece - top) for piece in scores]
        total = jnp.sum(functools.reduce(jnp.add, weights), axis=1, keepdims=True)
        mixed = functools.reduce(
            jnp.add,
            [
                dot(weight.astype(BF16), head_part(part(other, 2), head))
                for other, weight in enumerate(weights)
            ],
        )
        mixed = mixed / total
        if head == 0:
            kept = mixed
        else:
            out[span(block), :] = (kept + mixed).astype(BF16)
    split_halves(out, core, out_own, out_other)


def attend_forward(first, count, info, qkv_own, qkv_other):
    rows = qkv_own.shape[0]
    taken = pl.BlockSpec((rows, 3 * LANES), lambda pair: (0, first + pair))
    given = pl.BlockSpec((rows, LANES), lambda pair: (0, pair))
    shape = jax.ShapeDtypeStruct((rows, count * LANES), BF16)
    return pl.pallas_call(
        attend_forward_kernel,
        grid=(count,),
        in_specs=[smem(), taken, taken],
        out_specs=[given, given],
        out_shape=[shape, shape],
        scratch_shapes=[
            pltpu.VMEM((2 * rows, 3 * LANES), BF16),
            pltpu.VMEM((2 * rows, LANES), BF16),
        ],
        compiler_params=limit(32),
        cost_estimate=cost(5 * count),
        name=f"attend_forward_{first}",
    )(info, qkv_own, qkv_other)


def attend_backward_kernel(
    info, qkv_own, qkv_other, grad_own, grad_other, back_own, back_other, qkv, grad, back, key_sum, value_sum
):
    length, core = info[0], info[1]
    blocks = qkv.shape[0] // BLOCK
    fill_halves(qkv, core, qkv_own, qkv_other)
    fill_halves(grad, core, grad_own, grad_other)
    key_sum[...] = jnp.zeros_like(key_sum)
    value_sum[...] = jnp.zeros_like(value_sum)
    eighth = jnp.asarray(0.125, BF16)

    def part(block, which):
        return qkv[span(block), span(which, LANES)]

    column = lax.broadcasted_iota(jnp.int32, (1, BLOCK), 1)
    row = lax.broadcasted_iota(jnp.int32, (BLOCK, 1), 0)

    def products(block, head):
        query = head_part(part(block, 0), head) * eighth
        mixed = head_part(grad[span(block), :], head)
        last = jnp.minimum(column + block * BLOCK, length - 1)
        scores, grads = [], []
        for other in range(block + 1):
            piece = dot(part(other, 1), query, NT)
            if other == block or (other + 1) * BLOCK > LEN_MIN:
                piece = jnp.where(row + other * BLOCK <= last, piece, MASKED)
            scores.append(piece)
            grads.append(dot(part(other, 2), mixed, NT))
        return query, mixed, scores, grads

    tasks = [(block, head) for block in range(blocks) for head in range(2)]
    upcoming = products(*tasks[0])
    kept = None
    for place, (block, head) in enumerate(tasks):
        query, mixed, scores, grads = upcoming
        if place + 1 < len(tasks):
            upcoming = products(*tasks[place + 1])
        top = jnp.max(functools.reduce(jnp.maximum, scores), axis=0, keepdims=True)
        weights = [jnp.exp(piece - top) for piece in scores]
        total = jnp.sum(functools.reduce(jnp.add, weights), axis=0, keepdims=True)
        inverse = 1.0 / total
        weights = [weight * inverse for weight in weights]
        products_sum = functools.reduce(jnp.add, [w * g for w, g in zip(weights, grads)])
        inner = jnp.sum(products_sum, axis=0, keepdims=True)
        query_sum = None
        for other in range(block + 1):
            weight = weights[other]
            change = (weight * (grads[other] - inner)).astype(BF16)
            value_sum[span(other), :] += dot(weight.astype(BF16), mixed)
            key_sum[span(other), :] += dot(change, query)
            piece = dot(change, head_part(part(other, 1), head) * eighth, TN)
            query_sum = piece if query_sum is None else query_sum + piece
        if head == 0:
            kept = query_sum
        else:
            back[span(block), span(0, LANES)] = (kept + query_sum).astype(BF16)
    back[:, span(1, LANES)] = key_sum[...].astype(BF16)
    back[:, span(2, LANES)] = value_sum[...].astype(BF16)
    split_halves(back, core, back_own, back_other)


def attend_backward(pair, info, qkv_own, qkv_other, grad_own, grad_other):
    rows = grad_own.shape[0]
    qkv_spec = pl.BlockSpec((rows, 3 * LANES), lambda step: (0, pair))
    grad_spec = pl.BlockSpec((rows, LANES), lambda step: (0, pair))
    shape = jax.ShapeDtypeStruct((rows, 3 * LANES), BF16)
    return pl.pallas_call(
        attend_backward_kernel,
        grid=(1,),
        in_specs=[smem(), qkv_spec, qkv_spec, grad_spec, grad_spec],
        out_specs=[vmem(), vmem()],
        out_shape=[shape, shape],
        scratch_shapes=[
            pltpu.VMEM((2 * rows, 3 * LANES), BF16),
            pltpu.VMEM((2 * rows, LANES), BF16),
            pltpu.VMEM((2 * rows, 3 * LANES), BF16),
            pltpu.VMEM((2 * rows, LANES), F32),
            pltpu.VMEM((2 * rows, LANES), F32),
        ],
        compiler_params=limit(32),
        cost_estimate=cost(13),
        name=f"attend_backward_{pair}",
    )(info, qkv_own, qkv_other, grad_own, grad_other)


def feed_kernel(two, grad, weight, bias, active, grad_pre, mlp, back, bias_sum):
    hidden = active.shape[1]
    slope = math.sqrt(2.0 / math.pi)
    cubic = slope * 0.044715
    for chunk in range(hidden // BLOCK):
        here = span(chunk)
        there = slice(hidden + chunk * BLOCK, hidden + (chunk + 1) * BLOCK)
        pre = dot(two[...], weight[:, here]) + bias[:, here]
        grad_active = dot(grad[...], weight[:, there])
        square = pre * pre
        half = 0.5 + 0.5 * jnp.tanh(pre * (slope + cubic * square))
        value = pre * half
        change = half + (value - value * half) * (2.0 * slope + (6.0 * cubic) * square)
        active[:, here] = value.astype(BF16)
        low = (grad_active * change).astype(BF16)
        grad_pre[:, here] = low
        bias_sum[:, here] = jnp.sum(low.astype(F32), axis=0, keepdims=True)
    for chunk in range(mlp.shape[1] // BLOCK):
        here = span(chunk)
        back[:, here] = dot(grad_pre[...], weight[here, :hidden], NT).astype(back.dtype)
        mlp[:, here] = dot(active[...], weight[here, hidden : 2 * hidden], NT).astype(mlp.dtype)


def feed(two, grad, weight, bias, result, name):
    rows, width = two.shape
    hidden = bias.shape[1]
    low = jax.ShapeDtypeStruct((rows, hidden), BF16)
    terms = jax.ShapeDtypeStruct((rows, width), result)
    return pl.pallas_call(
        feed_kernel,
        in_specs=[vmem()] * 4,
        out_specs=[vmem()] * 5,
        out_shape=[low, low, terms, terms, jax.ShapeDtypeStruct((1, hidden), F32)],
        compiler_params=limit(24),
        cost_estimate=cost(12),
        name=name,
    )(two, grad, weight, bias)


def weight_grads_kernel(count, shard, order, *refs):
    lefts_own, lefts_other = refs[:count], refs[count : 2 * count]
    rights_own, rights_other = refs[2 * count : 3 * count], refs[3 * count : 4 * count]
    out, total = refs[4 * count], refs[4 * count + 1]
    first = 0
    for term in range(count):
        columns = rights_own[term].shape[1]
        for chunk in range(total.shape[0] // BLOCK):
            here = span(chunk)
            piece = dot(lefts_own[term][:, here], rights_own[term][...], TN)
            piece += dot(lefts_other[term][:, here], rights_other[term][...], TN)
            total[here, first : first + columns] = piece.astype(BF16)
        first += columns
    if shard is None:
        out[...] = total[...]
        return
    for place in range(total.shape[0] // shard):
        start = pl.multiple_of(order[place] * shard, 16)
        out[span(place, shard), :] = total[pl.ds(start, shard), :]


def weight_grads(order, terms, name):
    width = terms[0][0].shape[1]
    columns = sum(term[2].shape[1] for term in terms)
    shard = None if order is None else width // order.shape[0]
    order = jnp.zeros((1,), jnp.int32) if order is None else order
    operands = [term[kind] for kind in range(4) for term in terms]
    return pl.pallas_call(
        functools.partial(weight_grads_kernel, len(terms), shard),
        in_specs=[smem()] + [vmem()] * len(operands),
        out_specs=vmem(),
        out_shape=jax.ShapeDtypeStruct((width, columns), BF16),
        scratch_shapes=[pltpu.VMEM((width, columns), BF16)],
        compiler_params=limit(24),
        cost_estimate=cost(columns / 300),
        name=name,
    )(order, *operands)


def place_kernel(shard, order, *refs):
    pieces, out = refs[:-1], refs[-1]
    place = 0
    for piece in pieces:
        for step in range(piece.shape[0] // shard):
            start = pl.multiple_of(order[place] * shard, 16)
            out[pl.ds(start, shard), :] = piece[span(step, shard), :]
            place += 1


def place_blocks(order, pieces):
    shard, columns = pieces[0].shape
    return pl.pallas_call(
        functools.partial(place_kernel, shard),
        in_specs=[smem()] + [vmem()] * len(pieces),
        out_specs=vmem(),
        out_shape=jax.ShapeDtypeStruct((shard * order.shape[0], columns), BF16),
        name="place_blocks",
    )(order, *pieces)


class Cube:
    def __init__(self, shard_rows):
        self.shard_rows = shard_rows
        self.zy = lax.axis_size("zy")
        self.cores = lax.axis_size("core")
        self.size = self.zy * lax.axis_size("x")
        self.bits = self.size.bit_length() - 1
        self.direct = self.size == 1 << self.bits and self.bits >= 2 and shard_rows % 16 == 0
        outer = list(range(self.bits - 1, 1, -1))
        self.dims = [outer + [0, 1], outer + [1, 0]]
        if self.direct:
            masks = [
                [sum(1 << dims[step] for step in range(self.bits) if place >> step & 1) for place in range(self.size)]
                for dims in self.dims
            ]
            mine = lax.axis_index("zy") * 2 + lax.axis_index("x")
            core = lax.axis_index("core")
            chosen = jnp.where(core == 0, jnp.array(masks[0], jnp.int32), jnp.array(masks[1], jnp.int32))
            self.order = jnp.bitwise_xor(mine.astype(jnp.int32), chosen)
        else:
            blocks = shard_rows * self.size // 48
            self.order = jnp.arange(blocks, dtype=jnp.int32)

    def send(self, values, step):
        pairs = []
        for zy in range(self.zy):
            for core in range(self.cores):
                for x in range(2):
                    other = (zy * 2 + x) ^ (1 << self.dims[core][step])
                    pairs.append(((zy * 2 + core) * 2 + x, (other // 2 * 2 + core) * 2 + other % 2))
        return lax.ppermute(values, ("zy", "core", "x"), pairs)

    def joined(self, pieces):
        return pieces[0] if len(pieces) == 1 else jnp.concatenate(pieces, axis=0)

    def grow(self, pieces, payload=None):
        payload = self.joined(pieces) if payload is None else payload
        return pieces + [self.send(payload, len(pieces) - 1)]

    def finish(self, pieces):
        if not self.direct:
            return lax.all_gather(pieces[0], ("zy", "x"), axis=0, tiled=True)
        return place_blocks(self.order, pieces)

    def payload(self, values):
        return values[values.shape[0] // 2 :]

    def reduce_send(self, payload, step):
        return self.send(payload, self.bits - 1 - step)

    def merge(self, values, received):
        return (values[: values.shape[0] // 2].astype(F32) + received.astype(F32)).astype(BF16)

    def scatter(self, values):
        return lax.psum_scatter(values, ("zy", "x"), scatter_dimension=0, tiled=True)

    def total(self, values):
        if not self.direct:
            return lax.psum(values, ("zy", "core", "x"))
        for step in range(self.bits):
            values = values + self.send(values, step)
        return values + exchange(values)


def swap_small(values):
    return lax.ppermute(values, ("core", "x"), [(0, 0), (1, 2), (2, 1), (3, 3)])


def swap(values):
    received = lax.ppermute(values, ("core", "x"), [(1, 2), (2, 1)])
    return jnp.where(lax.axis_index("core") == lax.axis_index("x"), values, received)


def exchange(values):
    return lax.ppermute(values, "core", [(0, 1), (1, 0)])


def tie(values, other):
    return lax.optimization_barrier((values, other))


def shards(
    hidden_in,
    seq_lens,
    ln1_gain,
    ln1_bias,
    w_qkv,
    bias_qv,
    w_out,
    bias_out,
    ln2_gain,
    ln2_bias,
    w_up,
    bias_up,
    w_down,
    bias_down,
    grad_out,
):
    core = lax.axis_index("core")
    group = ("zy", "x")
    rows, width = hidden_in.shape
    shard_rows = w_up.shape[0]
    head_cols = w_qkv.shape[2]
    hidden_cols = w_up.shape[1]
    pairs = head_cols // LANES
    qkv_cols = 3 * head_cols
    cube = Cube(shard_rows)

    qkv_shard = w_qkv.reshape(3, shard_rows, pairs, LANES).transpose(1, 2, 0, 3).reshape(shard_rows, qkv_cols)
    attn_shard = jnp.concatenate([qkv_shard, w_out.T], axis=1)
    first_low = swap(jnp.concatenate([hidden_in, attn_shard.reshape(-1, width)], axis=0))
    residual_low = first_low[:rows]
    attn_pieces = [first_low[rows:].reshape(shard_rows, qkv_cols + head_cols)]
    rest_shard = jnp.concatenate([w_up, w_down.T], axis=1).reshape(-1, width)
    second_low = jnp.concatenate([grad_out, rest_shard], axis=0)
    second_low, residual_low = tie(second_low, residual_low)
    second_low = swap(second_low)
    grad_low = second_low[:rows]
    rest_pieces = [second_low[rows:].reshape(shard_rows, 2 * hidden_cols)]
    length = swap_small(seq_lens)[0]
    outer = cube.bits - 2
    if cube.direct:
        for step in range(outer):
            attn_pieces = cube.grow(attn_pieces)
        rest_pieces[0], attn_pieces[-1] = tie(rest_pieces[0], attn_pieces[-1])
        for step in range(outer):
            rest_pieces = cube.grow(rest_pieces)
        for step in range(2):
            attn_pieces = cube.grow(attn_pieces)
    attn_weights = cube.finish(attn_pieces)
    qkv_weight, out_weight = attn_weights[:, :qkv_cols], attn_weights[:, qkv_cols:]
    info = jnp.stack([length, core.astype(jnp.int32)])

    residual = residual_low.astype(F32)
    unit_one, inverse_one = norm_stats(residual)
    norm_own = (unit_one * ln1_gain + ln1_bias).astype(BF16)
    norm_other = exchange(norm_own)
    bias_here = lax.dynamic_slice_in_dim(bias_qv, core * head_cols, head_cols, 1)
    qkv_bias = jnp.stack([bias_here[0], jnp.zeros((head_cols,), F32), bias_here[1]])
    qkv_bias = qkv_bias.reshape(3, pairs, LANES).transpose(1, 0, 2).reshape(qkv_cols)
    qkv_own = (dot(norm_own, qkv_weight) + qkv_bias).astype(BF16)
    qkv_other = (dot(norm_other, qkv_weight) + qkv_bias).astype(BF16)
    if cube.direct:
        payload, qkv_other = tie(cube.joined(rest_pieces), qkv_other)
        rest_pieces = cube.grow(rest_pieces, payload)
    early_pairs = max(pairs - 1, 1)
    mixed_own, mixed_other = attend_forward(0, early_pairs, info, qkv_own, qkv_other)
    if cube.direct:
        rest_pieces[-1], mixed_other = tie(rest_pieces[-1], mixed_other)
        payload, qkv_other = tie(cube.joined(rest_pieces), qkv_other)
        rest_pieces = cube.grow(rest_pieces, payload)
    if early_pairs < pairs:
        more_own, more_other = attend_forward(early_pairs, pairs - early_pairs, info, qkv_own, qkv_other)
        mixed_own = jnp.concatenate([mixed_own, more_own], axis=1)
        mixed_other = jnp.concatenate([mixed_other, more_other], axis=1)
    attn_received = exchange(dot(mixed_other, out_weight, NT).astype(BF16))
    hidden = residual + (dot(mixed_own, out_weight, NT) + attn_received.astype(F32)) + bias_out
    unit_two, inverse_two = norm_stats(hidden)
    two_own = (unit_two * ln2_gain + ln2_bias).astype(BF16)
    two_other = exchange(two_own)
    rest_weights = cube.finish(rest_pieces)
    bias_up_here = lax.dynamic_slice_in_dim(bias_up, core * hidden_cols, hidden_cols, 0)[None]

    slots = core * rows + jnp.arange(rows, dtype=jnp.int32)
    grad_own = jnp.where((slots < length)[:, None], grad_low, jnp.zeros_like(grad_low))
    grad_other = exchange(grad_own)

    active_other, grad_pre_other, mlp_other, back_two_other, up_sum_other = feed(
        two_other, grad_other, rest_weights, bias_up_here, BF16, "feed_other"
    )
    back_two_received = exchange(back_two_other)
    mlp_received = exchange(mlp_other)
    active_own, grad_pre_own, mlp_own, back_two_own, up_sum_own = feed(
        two_own, grad_own, rest_weights, bias_up_here, F32, "feed_own"
    )
    layer_out = swap((hidden + (mlp_own + mlp_received.astype(F32)) + bias_down).astype(BF16))

    down_grads = weight_grads(None, [(grad_own, grad_other, active_own, active_other)], "down_grads")
    down_grads = cube.scatter(down_grads)

    back_two = back_two_own + back_two_received.astype(F32)
    back_hidden, gain_two_sum, shift_two_sum = norm_back(back_two, unit_two, inverse_two, ln2_gain)
    grad_hidden = grad_own.astype(F32) + back_hidden
    attn_grad_own = grad_hidden.astype(BF16)
    attn_grad_other = exchange(attn_grad_own)
    first_grads = weight_grads(
        cube.order,
        [
            (two_own, two_other, grad_pre_own, grad_pre_other),
            (attn_grad_own, attn_grad_other, mixed_own, mixed_other),
        ],
        "first_weight_grads",
    )
    grad_mixed_own = dot(attn_grad_own, out_weight).astype(BF16)
    grad_mixed_other = dot(attn_grad_other, out_weight).astype(BF16)

    def place(values):
        empty = jnp.zeros_like(values)
        return jnp.where(
            core == 0,
            jnp.concatenate([values, empty], axis=-1),
            jnp.concatenate([empty, values], axis=-1),
        )

    early = jnp.concatenate(
        [
            jnp.sum(grad_own.astype(F32), axis=0),
            gain_two_sum,
            shift_two_sum,
            jnp.sum(attn_grad_own.astype(F32), axis=0),
            place((up_sum_own + up_sum_other)[0]),
        ]
    )
    early_size = early.shape[0]
    if cube.direct:
        early = early.reshape(16, -1).astype(BF16)
        early = jnp.pad(early, ((0, 0), (0, first_grads.shape[1] - early.shape[1])))
    else:
        early = cube.total(early)
        first_grads = cube.scatter(first_grads)

    backs_own, backs_other = [], []
    grad_pair = (grad_mixed_own, grad_mixed_other)
    steps = cube.bits if cube.direct else 0
    for pair in range(max(pairs, steps)):
        received = None
        if pair < steps:
            payload = jnp.concatenate([cube.payload(first_grads), early], axis=0)
            payload, grad_pair = tie(payload, grad_pair)
            received = cube.reduce_send(payload, pair)
        if pair < pairs:
            back_own, back_other = attend_backward(pair, info, qkv_own, qkv_other, *grad_pair)
            if received is not None:
                received, back_own = tie(received, back_own)
            backs_own.append(back_own)
            backs_other.append(back_other)
        if received is not None:
            first_grads = cube.merge(first_grads, received[:-16])
            early = (early.astype(F32) + received[-16:].astype(F32)).astype(BF16)
    if cube.direct:
        early = early[:, : early_size // 16].reshape(-1).astype(F32)
        early = early + exchange(early)
    back_own = jnp.concatenate(backs_own, axis=1)
    back_other = jnp.concatenate(backs_other, axis=1)

    last_grads = weight_grads(
        cube.order, [(norm_own, norm_other, back_own, back_other)], "last_weight_grads"
    )
    if cube.direct:
        payload, back_other = tie(cube.payload(last_grads), back_other)
        received = cube.reduce_send(payload, 0)
    back_one_received = exchange(dot(back_other, qkv_weight, NT).astype(BF16))
    back_one = dot(back_own, qkv_weight, NT) + back_one_received.astype(F32)
    back_input, gain_one_sum, shift_one_sum = norm_back(back_one, unit_one, inverse_one, ln1_gain)
    grad_input = (grad_hidden + back_input).astype(BF16)
    back_sum = jnp.sum(back_own.astype(F32), axis=0) + jnp.sum(back_other.astype(F32), axis=0)
    back_sum = back_sum.reshape(pairs, 3, LANES).transpose(1, 0, 2).reshape(3, head_cols)
    qv_sum = jnp.stack([back_sum[0], back_sum[2]])
    late = jnp.concatenate([gain_one_sum, shift_one_sum, place(qv_sum).reshape(-1)])
    late_size = late.shape[0]
    if cube.direct:
        received, grad_input = tie(received, grad_input)
        grad_input = swap(grad_input)
        last_grads = cube.merge(last_grads, received)
        late = late.reshape(16, -1).astype(BF16)
        late = jnp.pad(late, ((0, 0), (0, qkv_cols - late.shape[1])))
        for step in range(1, steps):
            payload = jnp.concatenate([cube.payload(last_grads), late], axis=0)
            if step == steps - 1:
                payload, grad_input = tie(payload, grad_input)
            received = cube.reduce_send(payload, step)
            last_grads = cube.merge(last_grads, received[:-16])
            late = (late.astype(F32) + received[-16:].astype(F32)).astype(BF16)
        grad_input = grad_input.astype(F32)
        late = late[:, : late_size // 16].reshape(-1).astype(F32)
        late = late + cube.reduce_send(late, 0)
        late = late + exchange(late)
    else:
        grad_input = swap(grad_input).astype(F32)
        last_grads = cube.scatter(last_grads)
        late = cube.total(late)
    down_bias, gain_two, shift_two, out_bias, up_bias = jnp.split(early, [width * n for n in range(1, 5)])
    gain_one, shift_one, qv_bias = jnp.split(late, [width, 2 * width])

    done_grads = swap(jnp.concatenate([first_grads, down_grads, last_grads], axis=1))
    done_grads, last_grads = done_grads[:, :-qkv_cols], done_grads[:, -qkv_cols:]
    grad_w_qkv = last_grads.reshape(shard_rows, pairs, 3, LANES).transpose(2, 0, 1, 3)
    grad_w_qkv = grad_w_qkv.reshape(3, shard_rows, head_cols).astype(F32)
    grad_w_up = done_grads[:, :hidden_cols].astype(F32)
    grad_w_out = done_grads[:, hidden_cols : hidden_cols + head_cols].T.astype(F32)
    grad_w_down = done_grads[:, hidden_cols + head_cols :].T.astype(F32)
    return (
        layer_out,
        grad_input,
        gain_one,
        shift_one,
        grad_w_qkv,
        qv_bias.reshape(2, width),
        grad_w_out,
        out_bias,
        gain_two,
        shift_two,
        grad_w_up,
        up_bias,
        grad_w_down,
        down_bias,
    )


def solution(mesh):
    cores = 2
    devices = mesh.devices
    inner = Mesh(devices.reshape(devices.shape[0] // cores, cores, devices.shape[1]), ("zy", "core", "x"))
    dp = ("zy", "core")
    token = P(("zy", "core", "x"), None)
    in_specs = (
        token,
        P(dp),
        P(),
        P(),
        P(None, dp, "x"),
        P(),
        P("x", dp),
        P(),
        P(),
        P(),
        P(dp, "x"),
        P(),
        P("x", dp),
        P(),
        token,
    )
    out_specs = (
        token,
        token,
        P(),
        P(),
        P(None, dp, "x"),
        P(),
        P("x", dp),
        P(),
        P(),
        P(),
        P(dp, "x"),
        P(),
        P("x", dp),
        P(),
    )
    return jax.shard_map(shards, mesh=inner, in_specs=in_specs, out_specs=out_specs, check_vma=False)
```

```python
import functools
import math

import jax
import jax.numpy as jnp
from jax import lax
from jax.experimental import pallas as pl
from jax.experimental.pallas import tpu as pltpu
from jax.sharding import Mesh, PartitionSpec as P

HD = 64
LEN_MIN = 864
EPS = 1e-05
LANES = 128
BLOCK = 256
MASKED = -1000000000.0
F32 = jnp.float32
BF16 = jnp.bfloat16
NN = (((1,), (0,)), ((), ()))
NT = (((1,), (1,)), ((), ()))
TN = (((0,), (0,)), ((), ()))


def dot(left, right, dims=NN):
    return lax.dot_general(left, right, dims, preferred_element_type=F32)


def norm_stats(values):
    center = values - jnp.mean(values, axis=-1, keepdims=True)
    inverse = lax.rsqrt(jnp.mean(center * center, axis=-1, keepdims=True) + EPS)
    return center * inverse, inverse


def head_part(values, head):
    lane = lax.broadcasted_iota(jnp.int32, (1, LANES), 1)
    keep = (lane < HD) if head == 0 else (lane >= HD)
    return jnp.where(keep, values, jnp.zeros_like(values))


def lane_block(first):
    return pl.ds(pl.multiple_of(first, LANES), LANES)


def row_half(index, rows):
    return pl.ds(pl.multiple_of(index * rows, rows), rows)


def span(block, size=BLOCK):
    return slice(block * size, (block + 1) * size)


def vmem():
    return pl.BlockSpec(memory_space=pltpu.VMEM)


def smem():
    return pl.BlockSpec(memory_space=pltpu.SMEM)


def limit(mib):
    return pltpu.CompilerParams(vmem_limit_bytes=mib * 1024 * 1024)


def cost(microseconds):
    return pl.CostEstimate(flops=int(microseconds * 1.1e9), transcendentals=0, bytes_accessed=1)


def fill_halves(target, core, own, other):
    rows = own.shape[0]
    target[row_half(core, rows), :] = own[...]
    target[row_half(1 - core, rows), :] = other[...]


def split_halves(source, core, own, other):
    rows = own.shape[0]
    own[...] = source[row_half(core, rows), :]
    other[...] = source[row_half(1 - core, rows), :]


def attend_forward_kernel(info, qkv_own, qkv_other, out_own, out_other, qkv, out):
    length, core = info[0], info[1]
    blocks = qkv.shape[0] // BLOCK
    fill_halves(qkv, core, qkv_own, qkv_other)

    def part(block, which):
        return qkv[span(block), span(which, LANES)]

    column = lax.broadcasted_iota(jnp.int32, (1, BLOCK), 1)
    row = lax.broadcasted_iota(jnp.int32, (BLOCK, 1), 0)

    def score(block, head):
        query = head_part(part(block, 0), head) * jnp.asarray(0.125, BF16)
        last = jnp.minimum(row + block * BLOCK, length - 1)
        scores = []
        for other in range(block + 1):
            piece = dot(query, part(other, 1), NT)
            if other == block or (other + 1) * BLOCK > LEN_MIN:
                piece = jnp.where(column + other * BLOCK <= last, piece, MASKED)
            scores.append(piece)
        return scores

    tasks = [(block, head) for block in range(blocks) for head in range(2)]
    upcoming = score(*tasks[0])
    kept = None
    for place, (block, head) in enumerate(tasks):
        scores = upcoming
        if place + 1 < len(tasks):
            upcoming = score(*tasks[place + 1])
        top = functools.reduce(jnp.maximum, scores)
        top = jnp.max(top, axis=1, keepdims=True)
        weights = [jnp.exp(piece - top) for piece in scores]
        total = jnp.sum(functools.reduce(jnp.add, weights), axis=1, keepdims=True)
        mixed = functools.reduce(
            jnp.add,
            [
                dot(weight.astype(BF16), head_part(part(other, 2), head))
                for other, weight in enumerate(weights)
            ],
        )
        mixed = mixed / total
        if head == 0:
            kept = mixed
        else:
            out[span(block), :] = (kept + mixed).astype(BF16)
    split_halves(out, core, out_own, out_other)


def attend_forward(info, qkv_own, qkv_other):
    rows, width = qkv_own.shape[0], qkv_own.shape[1] // 3
    taken = pl.BlockSpec((rows, 3 * LANES), lambda pair: (0, pair))
    given = pl.BlockSpec((rows, LANES), lambda pair: (0, pair))
    shape = jax.ShapeDtypeStruct((rows, width), BF16)
    return pl.pallas_call(
        attend_forward_kernel,
        grid=(width // LANES,),
        in_specs=[smem(), taken, taken],
        out_specs=[given, given],
        out_shape=[shape, shape],
        scratch_shapes=[
            pltpu.VMEM((2 * rows, 3 * LANES), BF16),
            pltpu.VMEM((2 * rows, LANES), BF16),
        ],
        compiler_params=limit(32),
        cost_estimate=cost(0.1),
        name="attend_forward",
    )(info, qkv_own, qkv_other)


def attend_backward_kernel(
    info,
    qkv_own,
    qkv_other,
    grad_own,
    grad_other,
    back_own,
    back_other,
    sums,
    qkv,
    grad,
    back,
    key_sum,
    value_sum,
):
    length, core = info[0], info[1]
    blocks = qkv.shape[0] // BLOCK
    fill_halves(qkv, core, qkv_own, qkv_other)
    fill_halves(grad, core, grad_own, grad_other)
    key_sum[...] = jnp.zeros_like(key_sum)
    value_sum[...] = jnp.zeros_like(value_sum)
    eighth = jnp.asarray(0.125, BF16)

    def part(block, which):
        return qkv[span(block), span(which, LANES)]

    column = lax.broadcasted_iota(jnp.int32, (1, BLOCK), 1)
    row = lax.broadcasted_iota(jnp.int32, (BLOCK, 1), 0)

    def products(block, head):
        query = head_part(part(block, 0), head) * eighth
        mixed = head_part(grad[span(block), :], head)
        last = jnp.minimum(column + block * BLOCK, length - 1)
        scores, grads = [], []
        for other in range(block + 1):
            piece = dot(part(other, 1), query, NT)
            if other == block or (other + 1) * BLOCK > LEN_MIN:
                piece = jnp.where(row + other * BLOCK <= last, piece, MASKED)
            scores.append(piece)
            grads.append(dot(part(other, 2), mixed, NT))
        return query, mixed, scores, grads

    tasks = [(block, head) for block in range(blocks) for head in range(2)]
    upcoming = products(*tasks[0])
    kept = None
    for place, (block, head) in enumerate(tasks):
        query, mixed, scores, grads = upcoming
        if place + 1 < len(tasks):
            upcoming = products(*tasks[place + 1])
        top = jnp.max(functools.reduce(jnp.maximum, scores), axis=0, keepdims=True)
        weights = [jnp.exp(piece - top) for piece in scores]
        total = jnp.sum(functools.reduce(jnp.add, weights), axis=0, keepdims=True)
        inverse = 1.0 / total
        weights = [weight * inverse for weight in weights]
        products_sum = functools.reduce(jnp.add, [w * g for w, g in zip(weights, grads)])
        inner = jnp.sum(products_sum, axis=0, keepdims=True)
        query_sum = None
        for other in range(block + 1):
            weight = weights[other]
            change = (weight * (grads[other] - inner)).astype(BF16)
            value_sum[span(other), :] += dot(weight.astype(BF16), mixed)
            key_sum[span(other), :] += dot(change, query)
            piece = dot(change, head_part(part(other, 1), head) * eighth, TN)
            query_sum = piece if query_sum is None else query_sum + piece
        if head == 0:
            kept = query_sum
        else:
            back[span(block), span(0, LANES)] = (kept + query_sum).astype(BF16)
    back[:, span(1, LANES)] = key_sum[...].astype(BF16)
    back[:, span(2, LANES)] = value_sum[...].astype(BF16)
    split_halves(back, core, back_own, back_other)
    sums[...] = jnp.sum(back[...].astype(F32), axis=0, keepdims=True)


def attend_backward(pair, info, qkv_own, qkv_other, grad_own, grad_other):
    rows = grad_own.shape[0]
    qkv_spec = pl.BlockSpec((rows, 3 * LANES), lambda step: (0, pair))
    grad_spec = pl.BlockSpec((rows, LANES), lambda step: (0, pair))
    shape = jax.ShapeDtypeStruct((rows, 3 * LANES), BF16)
    return pl.pallas_call(
        attend_backward_kernel,
        grid=(1,),
        in_specs=[smem(), qkv_spec, qkv_spec, grad_spec, grad_spec],
        out_specs=[vmem(), vmem(), vmem()],
        out_shape=[shape, shape, jax.ShapeDtypeStruct((1, 3 * LANES), F32)],
        scratch_shapes=[
            pltpu.VMEM((2 * rows, 3 * LANES), BF16),
            pltpu.VMEM((2 * rows, LANES), BF16),
            pltpu.VMEM((2 * rows, 3 * LANES), BF16),
            pltpu.VMEM((2 * rows, LANES), F32),
            pltpu.VMEM((2 * rows, LANES), F32),
        ],
        compiler_params=limit(32),
        cost_estimate=cost(13),
        name=f"attend_backward_{pair}",
    )(info, qkv_own, qkv_other, grad_own, grad_other)


def feed_kernel(two, grad, weight, bias, active, grad_pre, mlp, back, bias_sum):
    hidden = active.shape[1]
    slope = math.sqrt(2.0 / math.pi)
    cubic = slope * 0.044715
    for chunk in range(hidden // BLOCK):
        here = span(chunk)
        there = slice(hidden + chunk * BLOCK, hidden + (chunk + 1) * BLOCK)
        pre = dot(two[...], weight[:, here]) + bias[:, here]
        grad_active = dot(grad[...], weight[:, there])
        square = pre * pre
        half = 0.5 + 0.5 * jnp.tanh(pre * (slope + cubic * square))
        value = pre * half
        change = half + (value - value * half) * (2.0 * slope + (6.0 * cubic) * square)
        active[:, here] = value.astype(BF16)
        low = (grad_active * change).astype(BF16)
        grad_pre[:, here] = low
        bias_sum[:, here] = jnp.sum(low.astype(F32), axis=0, keepdims=True)
    for chunk in range(mlp.shape[1] // BLOCK):
        here = span(chunk)
        back[:, here] = dot(grad_pre[...], weight[here, :hidden], NT).astype(back.dtype)
        mlp[:, here] = dot(active[...], weight[here, hidden : 2 * hidden], NT).astype(mlp.dtype)


def feed(two, grad, weight, bias, result, name):
    rows, width = two.shape
    hidden = bias.shape[1]
    low = jax.ShapeDtypeStruct((rows, hidden), BF16)
    terms = jax.ShapeDtypeStruct((rows, width), result)
    return pl.pallas_call(
        feed_kernel,
        in_specs=[vmem()] * 4,
        out_specs=[vmem()] * 5,
        out_shape=[low, low, terms, terms, jax.ShapeDtypeStruct((1, hidden), F32)],
        compiler_params=limit(24),
        cost_estimate=cost(12),
        name=name,
    )(two, grad, weight, bias)


def weight_grads_kernel(count, shard, order, *refs):
    lefts_own, lefts_other = refs[:count], refs[count : 2 * count]
    rights_own, rights_other = refs[2 * count : 3 * count], refs[3 * count : 4 * count]
    out, total = refs[4 * count], refs[4 * count + 1]
    first = 0
    for term in range(count):
        columns = rights_own[term].shape[1]
        for chunk in range(total.shape[0] // BLOCK):
            here = span(chunk)
            piece = dot(lefts_own[term][:, here], rights_own[term][...], TN)
            piece += dot(lefts_other[term][:, here], rights_other[term][...], TN)
            total[here, first : first + columns] = piece.astype(BF16)
        first += columns
    if shard is None:
        out[...] = total[...]
        return
    for place in range(total.shape[0] // shard):
        start = pl.multiple_of(order[place] * shard, 16)
        out[span(place, shard), :] = total[pl.ds(start, shard), :]


def weight_grads(order, terms, name):
    width = terms[0][0].shape[1]
    columns = sum(term[2].shape[1] for term in terms)
    shard = None if order is None else width // order.shape[0]
    order = jnp.zeros((1,), jnp.int32) if order is None else order
    operands = [term[kind] for kind in range(4) for term in terms]
    return pl.pallas_call(
        functools.partial(weight_grads_kernel, len(terms), shard),
        in_specs=[smem()] + [vmem()] * len(operands),
        out_specs=vmem(),
        out_shape=jax.ShapeDtypeStruct((width, columns), BF16),
        scratch_shapes=[pltpu.VMEM((width, columns), BF16)],
        compiler_params=limit(24),
        cost_estimate=cost(0.1),
        name=name,
    )(order, *operands)


def norm_back_kernel(values, back_own, back_received, extra, gain, low, sums, *total):
    for chunk in range(values.shape[0] // BLOCK):
        here = span(chunk)
        normed, inverse = norm_stats(values[here, :].astype(F32))
        grad = back_own[here, :].astype(F32) + back_received[here, :].astype(F32)
        scaled = grad * gain[...]
        added = extra[here, :].astype(F32)
        result = added + inverse * (
            scaled
            - jnp.mean(scaled, axis=-1, keepdims=True)
            - normed * jnp.mean(scaled * normed, axis=-1, keepdims=True)
        )
        rounded = result.astype(BF16)
        low[here, :] = rounded
        if total:
            total[0][here, :] = result
        for place, item in enumerate((added, grad * normed, grad, rounded.astype(F32))):
            item = jnp.sum(item, axis=0, keepdims=True)
            if chunk == 0:
                sums[place : place + 1, :] = item
            else:
                sums[place : place + 1, :] += item


def norm_back(values, back_own, back_received, extra, gain, keep, name):
    shapes = [
        jax.ShapeDtypeStruct(values.shape, BF16),
        jax.ShapeDtypeStruct((8, values.shape[1]), F32),
    ]
    if keep:
        shapes.append(jax.ShapeDtypeStruct(values.shape, F32))
    return pl.pallas_call(
        norm_back_kernel,
        in_specs=[vmem()] * 5,
        out_specs=[vmem()] * len(shapes),
        out_shape=shapes,
        compiler_params=limit(16),
        cost_estimate=cost(0.1),
        name=name,
    )(values, back_own, back_received, extra, gain[None])


def early_kernel(info, sums, up_own, up_other, out):
    core = info[1]
    half = out.shape[1]
    for place in range(4):
        for side in range(2):
            out[2 * place + side : 2 * place + side + 1, :] = sums[place : place + 1, span(side, half)]
    for place in range(4):
        item = up_own[:, span(place, half)] + up_other[:, span(place, half)]
        out[8 + place : 9 + place, :] = jnp.where(core == 0, item, 0.0)
        out[12 + place : 13 + place, :] = jnp.where(core == 0, 0.0, item)


def late_kernel(info, sums, *refs):
    core = info[1]
    pairs, out = refs[:-1], refs[-1]
    half = out.shape[1]
    out[...] = jnp.zeros_like(out)
    for place in range(2):
        for side in range(2):
            out[2 * place + side : 2 * place + side + 1, :] = sums[place + 1 : place + 2, span(side, half)]
    for index, pair in enumerate(pairs):
        here = span(index, LANES)
        for place, which in enumerate((0, 2)):
            item = pair[:, span(which, LANES)]
            first = 4 + 2 * place
            out[first : first + 1, here] = jnp.where(core == 0, item, 0.0)
            out[first + 1 : first + 2, here] = jnp.where(core == 0, 0.0, item)


def pack(kernel, info, operands, half, name):
    return pl.pallas_call(
        kernel,
        in_specs=[smem()] + [vmem()] * len(operands),
        out_specs=vmem(),
        out_shape=jax.ShapeDtypeStruct((16, half), F32),
        cost_estimate=cost(0.1),
        name=name,
    )(info, *operands)


def place_kernel(shard, order, *refs):
    pieces, out = refs[:-1], refs[-1]
    place = 0
    for piece in pieces:
        for step in range(piece.shape[0] // shard):
            start = pl.multiple_of(order[place] * shard, 16)
            out[pl.ds(start, shard), :] = piece[span(step, shard), :]
            place += 1


def place_blocks(order, pieces):
    shard, columns = pieces[0].shape
    return pl.pallas_call(
        functools.partial(place_kernel, shard),
        in_specs=[smem()] + [vmem()] * len(pieces),
        out_specs=vmem(),
        out_shape=jax.ShapeDtypeStruct((shard * order.shape[0], columns), BF16),
        name="place_blocks",
    )(order, *pieces)


class Cube:
    def __init__(self, shard_rows):
        self.shard_rows = shard_rows
        self.zy = lax.axis_size("zy")
        self.cores = lax.axis_size("core")
        self.size = self.zy * lax.axis_size("x")
        self.bits = self.size.bit_length() - 1
        self.direct = self.size == 1 << self.bits and self.bits >= 2 and shard_rows % 16 == 0
        outer = list(range(self.bits - 1, 1, -1))
        self.dims = [outer + [0, 1], outer + [1, 0]]
        if self.direct:
            masks = [
                [sum(1 << dims[step] for step in range(self.bits) if place >> step & 1) for place in range(self.size)]
                for dims in self.dims
            ]
            mine = lax.axis_index("zy") * 2 + lax.axis_index("x")
            core = lax.axis_index("core")
            chosen = jnp.where(core == 0, jnp.array(masks[0], jnp.int32), jnp.array(masks[1], jnp.int32))
            self.order = jnp.bitwise_xor(mine.astype(jnp.int32), chosen)
        else:
            blocks = shard_rows * self.size // 48
            self.order = jnp.arange(blocks, dtype=jnp.int32)

    def send(self, values, step):
        pairs = []
        for zy in range(self.zy):
            for core in range(self.cores):
                for x in range(2):
                    other = (zy * 2 + x) ^ (1 << self.dims[core][step])
                    pairs.append(((zy * 2 + core) * 2 + x, (other // 2 * 2 + core) * 2 + other % 2))
        return lax.ppermute(values, ("zy", "core", "x"), pairs)

    def joined(self, pieces):
        return pieces[0] if len(pieces) == 1 else jnp.concatenate(pieces, axis=0)

    def grow(self, pieces, payload=None):
        payload = self.joined(pieces) if payload is None else payload
        return pieces + [self.send(payload, len(pieces) - 1)]

    def finish(self, pieces):
        if not self.direct:
            return lax.all_gather(pieces[0], ("zy", "x"), axis=0, tiled=True)
        return place_blocks(self.order, pieces)

    def payload(self, values):
        return values[values.shape[0] // 2 :]

    def reduce_send(self, payload, step):
        return self.send(payload, self.bits - 1 - step)

    def merge(self, values, received):
        return (values[: values.shape[0] // 2].astype(F32) + received.astype(F32)).astype(BF16)

    def scatter(self, values):
        return lax.psum_scatter(values, ("zy", "x"), scatter_dimension=0, tiled=True)

    def total(self, values):
        if not self.direct:
            return lax.psum(values, ("zy", "core", "x"))
        for step in range(self.bits):
            values = values + self.send(values, step)
        return values + exchange(values)


def swap_small(values):
    return lax.ppermute(values, ("core", "x"), [(0, 0), (1, 2), (2, 1), (3, 3)])


def swap(values):
    received = lax.ppermute(values, ("core", "x"), [(1, 2), (2, 1)])
    return jnp.where(lax.axis_index("core") == lax.axis_index("x"), values, received)


def exchange(values):
    return lax.ppermute(values, "core", [(0, 1), (1, 0)])


def tie(values, other):
    return lax.optimization_barrier((values, other))


def shards(
    hidden_in,
    seq_lens,
    ln1_gain,
    ln1_bias,
    w_qkv,
    bias_qv,
    w_out,
    bias_out,
    ln2_gain,
    ln2_bias,
    w_up,
    bias_up,
    w_down,
    bias_down,
    grad_out,
):
    core = lax.axis_index("core")
    group = ("zy", "x")
    rows, width = hidden_in.shape
    shard_rows = w_up.shape[0]
    head_cols = w_qkv.shape[2]
    hidden_cols = w_up.shape[1]
    pairs = head_cols // LANES
    qkv_cols = 3 * head_cols
    cube = Cube(shard_rows)

    qkv_shard = w_qkv.reshape(3, shard_rows, pairs, LANES).transpose(1, 2, 0, 3).reshape(shard_rows, qkv_cols)
    shard = swap(jnp.concatenate([qkv_shard, w_up, w_down.T, w_out.T], axis=1))
    hidden_in, shard = tie(hidden_in, shard)
    residual_low = swap(hidden_in)
    qkv_pieces = [shard[:, :qkv_cols]]
    rest_weights = lax.all_gather(shard[:, qkv_cols:], group, axis=0, tiled=True)
    length = swap_small(seq_lens)[0]
    if cube.direct:
        for step in range(cube.bits):
            qkv_pieces = cube.grow(qkv_pieces)
    qkv_weight = cube.finish(qkv_pieces)
    grad_low = swap(grad_out)
    out_weight = rest_weights[:, 2 * hidden_cols :]
    info = jnp.stack([length, core.astype(jnp.int32)])

    residual = residual_low.astype(F32)
    unit_one, _ = norm_stats(residual)
    norm_own = (unit_one * ln1_gain + ln1_bias).astype(BF16)
    norm_other = exchange(norm_own)
    bias_here = lax.dynamic_slice_in_dim(bias_qv, core * head_cols, head_cols, 1)
    qkv_bias = jnp.stack([bias_here[0], jnp.zeros((head_cols,), F32), bias_here[1]])
    qkv_bias = qkv_bias.reshape(3, pairs, LANES).transpose(1, 0, 2).reshape(qkv_cols)
    qkv_own = (dot(norm_own, qkv_weight) + qkv_bias).astype(BF16)
    qkv_other = (dot(norm_other, qkv_weight) + qkv_bias).astype(BF16)
    mixed_own, mixed_other = attend_forward(info, qkv_own, qkv_other)
    attn_received = exchange(dot(mixed_other, out_weight, NT).astype(BF16))
    hidden = residual + (dot(mixed_own, out_weight, NT) + attn_received.astype(F32)) + bias_out
    unit_two, _ = norm_stats(hidden)
    two_own = (unit_two * ln2_gain + ln2_bias).astype(BF16)
    two_other = exchange(two_own)
    bias_up_here = lax.dynamic_slice_in_dim(bias_up, core * hidden_cols, hidden_cols, 0)[None]

    slots = core * rows + jnp.arange(rows, dtype=jnp.int32)
    grad_own = jnp.where((slots < length)[:, None], grad_low, jnp.zeros_like(grad_low))
    grad_other = exchange(grad_own)

    active_other, grad_pre_other, mlp_other, back_two_other, up_sum_other = feed(
        two_other, grad_other, rest_weights, bias_up_here, BF16, "feed_other"
    )
    back_two_received = exchange(back_two_other)
    mlp_received = exchange(mlp_other)
    active_own, grad_pre_own, mlp_own, back_two_own, up_sum_own = feed(
        two_own, grad_own, rest_weights, bias_up_here, F32, "feed_own"
    )
    layer_out = swap((hidden + (mlp_own + mlp_received.astype(F32)) + bias_down).astype(BF16))

    up_grads = weight_grads(
        cube.order, [(two_own, two_other, grad_pre_own, grad_pre_other)], "up_grads"
    )
    if cube.direct:
        payload, back_two_own = tie(cube.payload(up_grads), back_two_own)
        up_received = cube.reduce_send(payload, 0)
    attn_grad_own, sums, grad_hidden = norm_back(
        hidden, back_two_own, back_two_received, grad_own, ln2_gain, True, "norm_two_back"
    )
    attn_grad_other = exchange(attn_grad_own)
    first_grads = weight_grads(
        cube.order,
        [
            (grad_own, grad_other, active_own, active_other),
            (attn_grad_own, attn_grad_other, mixed_own, mixed_other),
        ],
        "down_out_grads",
    )
    grad_mixed_own = dot(attn_grad_own, out_weight).astype(BF16)
    grad_mixed_other = dot(attn_grad_other, out_weight).astype(BF16)
    early = pack(early_kernel, info, [sums, up_sum_own, up_sum_other], width // 2, "early_sums")
    if cube.direct:
        up_received, first_grads = tie(up_received, first_grads)
        early = early.astype(BF16)
    else:
        early = cube.total(early)
        first_grads = cube.scatter(first_grads)
        up_grads = cube.scatter(up_grads)

    backs_own, backs_other, back_sums = [], [], []
    grad_pair = (grad_mixed_own, grad_mixed_other)
    steps = cube.bits if cube.direct else 0
    last_grads = None
    for pair in range(max(pairs + 1, steps)):
        received = None
        if pair < steps:
            padding = ((0, 0), (0, first_grads.shape[1] - early.shape[1]))
            payload = jnp.concatenate([cube.payload(first_grads), jnp.pad(early, padding)], axis=0)
            payload, grad_pair = tie(payload, grad_pair)
            received = cube.reduce_send(payload, pair)
        if pair < pairs:
            back_own, back_other, back_sum = attend_backward(pair, info, qkv_own, qkv_other, *grad_pair)
            if received is not None:
                received, back_own = tie(received, back_own)
            backs_own.append(back_own)
            backs_other.append(back_other)
            back_sums.append(back_sum)
        if pair == pairs:
            back_own = jnp.concatenate(backs_own, axis=1)
            back_other = jnp.concatenate(backs_other, axis=1)
            last_grads = weight_grads(
                cube.order, [(norm_own, norm_other, back_own, back_other)], "last_weight_grads"
            )
            if received is not None:
                received, last_grads = tie(received, last_grads)
        if received is not None:
            first_grads = cube.merge(first_grads, received[:-16])
            if pair == 0:
                up_grads = cube.merge(up_grads, up_received)
                first_grads = jnp.concatenate([up_grads, first_grads], axis=1)
            early = (early.astype(F32) + received[-16:, : early.shape[1]].astype(F32)).astype(BF16)
    if cube.direct:
        early = early.astype(F32)
        early = early + exchange(early)
    else:
        first_grads = jnp.concatenate([up_grads, first_grads], axis=1)
    done_grads = first_grads.reshape(-1, width)
    if cube.direct:
        payload, back_other = tie(cube.payload(last_grads), back_other)
        received = cube.reduce_send(payload, 0)
    back_one_received = exchange(dot(back_other, qkv_weight, NT).astype(BF16))
    grad_input, sums = norm_back(
        residual_low,
        dot(back_own, qkv_weight, NT),
        back_one_received,
        grad_hidden,
        ln1_gain,
        False,
        "norm_one_back",
    )
    late = pack(late_kernel, info, [sums] + back_sums, width // 2, "late_sums")
    if cube.direct:
        received, grad_input = tie(received, grad_input)
    final_low = swap(jnp.concatenate([grad_input, done_grads], axis=0))
    if cube.direct:
        last_grads = cube.merge(last_grads, received)
        late = late.astype(BF16)
        for step in range(1, steps):
            padding = ((0, 0), (0, qkv_cols - late.shape[1]))
            payload = jnp.concatenate([cube.payload(last_grads), jnp.pad(late, padding)], axis=0)
            received = cube.reduce_send(payload, step)
            if step == steps - 1:
                received, final_low = tie(received, final_low)
            last_grads = cube.merge(last_grads, received[:-16])
            late = (late.astype(F32) + received[-16:, : late.shape[1]].astype(F32)).astype(BF16)
        late = late.astype(F32)
        late = late + cube.reduce_send(late, 0)
        late = late + exchange(late)
    else:
        last_grads = cube.scatter(last_grads)
        late = cube.total(late)
    last_grads = swap(last_grads)
    grad_input = final_low[:rows].astype(F32)
    done_grads = final_low[rows:].reshape(shard_rows, -1)

    early = early.reshape(-1)
    down_bias, gain_two, shift_two, out_bias, up_bias = jnp.split(early, [width * n for n in range(1, 5)])
    late = late.reshape(-1)[: 4 * width]
    gain_one, shift_one, qv_bias = jnp.split(late, [width, 2 * width])
    grad_w_qkv = last_grads.reshape(shard_rows, pairs, 3, LANES).transpose(2, 0, 1, 3)
    grad_w_qkv = grad_w_qkv.reshape(3, shard_rows, head_cols).astype(F32)
    grad_w_up = done_grads[:, :hidden_cols].astype(F32)
    grad_w_down = done_grads[:, hidden_cols : 2 * hidden_cols].T.astype(F32)
    grad_w_out = done_grads[:, 2 * hidden_cols :].T.astype(F32)
    return (
        layer_out,
        grad_input,
        gain_one,
        shift_one,
        grad_w_qkv,
        qv_bias.reshape(2, width),
        grad_w_out,
        out_bias,
        gain_two,
        shift_two,
        grad_w_up,
        up_bias,
        grad_w_down,
        down_bias,
    )


def solution(mesh):
    cores = 2
    devices = mesh.devices
    inner = Mesh(devices.reshape(devices.shape[0] // cores, cores, devices.shape[1]), ("zy", "core", "x"))
    dp = ("zy", "core")
    token = P(("zy", "core", "x"), None)
    in_specs = (
        token,
        P(dp),
        P(),
        P(),
        P(None, dp, "x"),
        P(),
        P("x", dp),
        P(),
        P(),
        P(),
        P(dp, "x"),
        P(),
        P("x", dp),
        P(),
        token,
    )
    out_specs = (
        token,
        token,
        P(),
        P(),
        P(None, dp, "x"),
        P(),
        P("x", dp),
        P(),
        P(),
        P(),
        P(dp, "x"),
        P(),
        P("x", dp),
        P(),
    )
    return jax.shard_map(shards, mesh=inner, in_specs=in_specs, out_specs=out_specs, check_vma=False)
```

```python
import functools
import math

import jax
import jax.numpy as jnp
from jax import lax
from jax.experimental import pallas as pl
from jax.experimental.pallas import tpu as pltpu
from jax.sharding import Mesh, PartitionSpec as P

HD = 64
LEN_MIN = 864
EPS = 1e-05
LANES = 128
BLOCK = 256
MASKED = -1000000000.0
F32 = jnp.float32
BF16 = jnp.bfloat16
NN = (((1,), (0,)), ((), ()))
NT = (((1,), (1,)), ((), ()))
TN = (((0,), (0,)), ((), ()))


def dot(left, right, dims=NN):
    return lax.dot_general(left, right, dims, preferred_element_type=F32)


def norm_stats(values):
    center = values - jnp.mean(values, axis=-1, keepdims=True)
    inverse = lax.rsqrt(jnp.mean(center * center, axis=-1, keepdims=True) + EPS)
    return center * inverse, inverse


def head_part(values, head):
    lane = lax.broadcasted_iota(jnp.int32, (1, LANES), 1)
    keep = (lane < HD) if head == 0 else (lane >= HD)
    return jnp.where(keep, values, jnp.zeros_like(values))


def lane_block(first):
    return pl.ds(pl.multiple_of(first, LANES), LANES)


def row_half(index, rows):
    return pl.ds(pl.multiple_of(index * rows, rows), rows)


def span(block, size=BLOCK):
    return slice(block * size, (block + 1) * size)


def vmem():
    return pl.BlockSpec(memory_space=pltpu.VMEM)


def smem():
    return pl.BlockSpec(memory_space=pltpu.SMEM)


def limit(mib):
    return pltpu.CompilerParams(vmem_limit_bytes=mib * 1024 * 1024)


def cost(microseconds):
    return pl.CostEstimate(flops=int(microseconds * 1.1e9), transcendentals=0, bytes_accessed=1)


def fill_halves(target, core, own, other):
    rows = own.shape[0]
    target[row_half(core, rows), :] = own[...]
    target[row_half(1 - core, rows), :] = other[...]


def split_halves(source, core, own, other):
    rows = own.shape[0]
    own[...] = source[row_half(core, rows), :]
    other[...] = source[row_half(1 - core, rows), :]


def attend_forward_kernel(info, qkv_own, qkv_other, out_own, out_other, qkv, out):
    length, core = info[0], info[1]
    blocks = qkv.shape[0] // BLOCK
    fill_halves(qkv, core, qkv_own, qkv_other)

    def part(block, which):
        return qkv[span(block), span(which, LANES)]

    column = lax.broadcasted_iota(jnp.int32, (1, BLOCK), 1)
    row = lax.broadcasted_iota(jnp.int32, (BLOCK, 1), 0)

    def score(block, head):
        query = head_part(part(block, 0), head) * jnp.asarray(0.125, BF16)
        last = jnp.minimum(row + block * BLOCK, length - 1)
        scores = []
        for other in range(block + 1):
            piece = dot(query, part(other, 1), NT)
            if other == block or (other + 1) * BLOCK > LEN_MIN:
                piece = jnp.where(column + other * BLOCK <= last, piece, MASKED)
            scores.append(piece)
        return scores

    tasks = [(block, head) for block in range(blocks) for head in range(2)]
    upcoming = score(*tasks[0])
    kept = None
    for place, (block, head) in enumerate(tasks):
        scores = upcoming
        if place + 1 < len(tasks):
            upcoming = score(*tasks[place + 1])
        top = functools.reduce(jnp.maximum, scores)
        top = jnp.max(top, axis=1, keepdims=True)
        weights = [jnp.exp(piece - top) for piece in scores]
        total = jnp.sum(functools.reduce(jnp.add, weights), axis=1, keepdims=True)
        mixed = functools.reduce(
            jnp.add,
            [
                dot(weight.astype(BF16), head_part(part(other, 2), head))
                for other, weight in enumerate(weights)
            ],
        )
        mixed = mixed / total
        if head == 0:
            kept = mixed
        else:
            out[span(block), :] = (kept + mixed).astype(BF16)
    split_halves(out, core, out_own, out_other)


def attend_forward(info, qkv_own, qkv_other):
    rows, width = qkv_own.shape[0], qkv_own.shape[1] // 3
    taken = pl.BlockSpec((rows, 3 * LANES), lambda pair: (0, pair))
    given = pl.BlockSpec((rows, LANES), lambda pair: (0, pair))
    shape = jax.ShapeDtypeStruct((rows, width), BF16)
    return pl.pallas_call(
        attend_forward_kernel,
        grid=(width // LANES,),
        in_specs=[smem(), taken, taken],
        out_specs=[given, given],
        out_shape=[shape, shape],
        scratch_shapes=[
            pltpu.VMEM((2 * rows, 3 * LANES), BF16),
            pltpu.VMEM((2 * rows, LANES), BF16),
        ],
        compiler_params=limit(32),
        cost_estimate=cost(0.1),
        name="attend_forward",
    )(info, qkv_own, qkv_other)


def attend_backward_kernel(
    info,
    qkv_own,
    qkv_other,
    grad_own,
    grad_other,
    back_own,
    back_other,
    sums,
    qkv,
    grad,
    back,
    key_sum,
    value_sum,
):
    length, core = info[0], info[1]
    blocks = qkv.shape[0] // BLOCK
    fill_halves(qkv, core, qkv_own, qkv_other)
    fill_halves(grad, core, grad_own, grad_other)
    key_sum[...] = jnp.zeros_like(key_sum)
    value_sum[...] = jnp.zeros_like(value_sum)
    eighth = jnp.asarray(0.125, BF16)

    def part(block, which):
        return qkv[span(block), span(which, LANES)]

    column = lax.broadcasted_iota(jnp.int32, (1, BLOCK), 1)
    row = lax.broadcasted_iota(jnp.int32, (BLOCK, 1), 0)

    def products(block, head):
        query = head_part(part(block, 0), head) * eighth
        mixed = head_part(grad[span(block), :], head)
        last = jnp.minimum(column + block * BLOCK, length - 1)
        scores, grads = [], []
        for other in range(block + 1):
            piece = dot(part(other, 1), query, NT)
            if other == block or (other + 1) * BLOCK > LEN_MIN:
                piece = jnp.where(row + other * BLOCK <= last, piece, MASKED)
            scores.append(piece)
            grads.append(dot(part(other, 2), mixed, NT))
        return query, mixed, scores, grads

    tasks = [(block, head) for block in range(blocks) for head in range(2)]
    upcoming = products(*tasks[0])
    kept = None
    for place, (block, head) in enumerate(tasks):
        query, mixed, scores, grads = upcoming
        if place + 1 < len(tasks):
            upcoming = products(*tasks[place + 1])
        top = jnp.max(functools.reduce(jnp.maximum, scores), axis=0, keepdims=True)
        weights = [jnp.exp(piece - top) for piece in scores]
        total = jnp.sum(functools.reduce(jnp.add, weights), axis=0, keepdims=True)
        inverse = 1.0 / total
        weights = [weight * inverse for weight in weights]
        products_sum = functools.reduce(jnp.add, [w * g for w, g in zip(weights, grads)])
        inner = jnp.sum(products_sum, axis=0, keepdims=True)
        query_sum = None
        for other in range(block + 1):
            weight = weights[other]
            change = (weight * (grads[other] - inner)).astype(BF16)
            value_sum[span(other), :] += dot(weight.astype(BF16), mixed)
            key_sum[span(other), :] += dot(change, query)
            piece = dot(change, head_part(part(other, 1), head) * eighth, TN)
            query_sum = piece if query_sum is None else query_sum + piece
        if head == 0:
            kept = query_sum
        else:
            back[span(block), span(0, LANES)] = (kept + query_sum).astype(BF16)
    back[:, span(1, LANES)] = key_sum[...].astype(BF16)
    back[:, span(2, LANES)] = value_sum[...].astype(BF16)
    split_halves(back, core, back_own, back_other)
    sums[...] = jnp.sum(back[...].astype(F32), axis=0, keepdims=True)


def attend_backward(pair, info, qkv_own, qkv_other, grad_own, grad_other):
    rows = grad_own.shape[0]
    qkv_spec = pl.BlockSpec((rows, 3 * LANES), lambda step: (0, pair))
    grad_spec = pl.BlockSpec((rows, LANES), lambda step: (0, pair))
    shape = jax.ShapeDtypeStruct((rows, 3 * LANES), BF16)
    return pl.pallas_call(
        attend_backward_kernel,
        grid=(1,),
        in_specs=[smem(), qkv_spec, qkv_spec, grad_spec, grad_spec],
        out_specs=[vmem(), vmem(), vmem()],
        out_shape=[shape, shape, jax.ShapeDtypeStruct((1, 3 * LANES), F32)],
        scratch_shapes=[
            pltpu.VMEM((2 * rows, 3 * LANES), BF16),
            pltpu.VMEM((2 * rows, LANES), BF16),
            pltpu.VMEM((2 * rows, 3 * LANES), BF16),
            pltpu.VMEM((2 * rows, LANES), F32),
            pltpu.VMEM((2 * rows, LANES), F32),
        ],
        compiler_params=limit(32),
        cost_estimate=cost(13),
        name=f"attend_backward_{pair}",
    )(info, qkv_own, qkv_other, grad_own, grad_other)


def feed_kernel(two, grad, weight, bias, active, grad_pre, mlp, back, bias_sum):
    hidden = active.shape[1]
    slope = math.sqrt(2.0 / math.pi)
    cubic = slope * 0.044715
    for chunk in range(hidden // BLOCK):
        here = span(chunk)
        there = slice(hidden + chunk * BLOCK, hidden + (chunk + 1) * BLOCK)
        pre = dot(two[...], weight[:, here]) + bias[:, here]
        grad_active = dot(grad[...], weight[:, there])
        square = pre * pre
        half = 0.5 + 0.5 * jnp.tanh(pre * (slope + cubic * square))
        value = pre * half
        change = half + (value - value * half) * (2.0 * slope + (6.0 * cubic) * square)
        active[:, here] = value.astype(BF16)
        low = (grad_active * change).astype(BF16)
        grad_pre[:, here] = low
        bias_sum[:, here] = jnp.sum(low.astype(F32), axis=0, keepdims=True)
    for chunk in range(mlp.shape[1] // BLOCK):
        here = span(chunk)
        back[:, here] = dot(grad_pre[...], weight[here, :hidden], NT).astype(back.dtype)
        mlp[:, here] = dot(active[...], weight[here, hidden : 2 * hidden], NT).astype(mlp.dtype)


def feed(two, grad, weight, bias, result, name):
    rows, width = two.shape
    hidden = bias.shape[1]
    low = jax.ShapeDtypeStruct((rows, hidden), BF16)
    terms = jax.ShapeDtypeStruct((rows, width), result)
    return pl.pallas_call(
        feed_kernel,
        in_specs=[vmem()] * 4,
        out_specs=[vmem()] * 5,
        out_shape=[low, low, terms, terms, jax.ShapeDtypeStruct((1, hidden), F32)],
        compiler_params=limit(24),
        cost_estimate=cost(12),
        name=name,
    )(two, grad, weight, bias)


def weight_grads_kernel(count, shard, order, *refs):
    lefts_own, lefts_other = refs[:count], refs[count : 2 * count]
    rights_own, rights_other = refs[2 * count : 3 * count], refs[3 * count : 4 * count]
    out, total = refs[4 * count], refs[4 * count + 1]
    first = 0
    for term in range(count):
        columns = rights_own[term].shape[1]
        for chunk in range(total.shape[0] // BLOCK):
            here = span(chunk)
            piece = dot(lefts_own[term][:, here], rights_own[term][...], TN)
            piece += dot(lefts_other[term][:, here], rights_other[term][...], TN)
            total[here, first : first + columns] = piece.astype(BF16)
        first += columns
    if shard is None:
        out[...] = total[...]
        return
    for place in range(total.shape[0] // shard):
        start = pl.multiple_of(order[place] * shard, 16)
        out[span(place, shard), :] = total[pl.ds(start, shard), :]


def weight_grads(order, terms, name):
    width = terms[0][0].shape[1]
    columns = sum(term[2].shape[1] for term in terms)
    shard = None if order is None else width // order.shape[0]
    order = jnp.zeros((1,), jnp.int32) if order is None else order
    operands = [term[kind] for kind in range(4) for term in terms]
    return pl.pallas_call(
        functools.partial(weight_grads_kernel, len(terms), shard),
        in_specs=[smem()] + [vmem()] * len(operands),
        out_specs=vmem(),
        out_shape=jax.ShapeDtypeStruct((width, columns), BF16),
        scratch_shapes=[pltpu.VMEM((width, columns), BF16)],
        compiler_params=limit(24),
        cost_estimate=cost(0.1),
        name=name,
    )(order, *operands)


def norm_back_kernel(values, back_own, back_received, extra, gain, low, sums):
    for chunk in range(values.shape[0] // BLOCK):
        here = span(chunk)
        normed, inverse = norm_stats(values[here, :].astype(F32))
        grad = back_own[here, :].astype(F32) + back_received[here, :].astype(F32)
        scaled = grad * gain[...]
        added = extra[here, :].astype(F32)
        result = added + inverse * (
            scaled
            - jnp.mean(scaled, axis=-1, keepdims=True)
            - normed * jnp.mean(scaled * normed, axis=-1, keepdims=True)
        )
        rounded = result.astype(BF16)
        low[here, :] = rounded
        for place, item in enumerate((added, grad * normed, grad, rounded.astype(F32))):
            item = jnp.sum(item, axis=0, keepdims=True)
            if chunk == 0:
                sums[place : place + 1, :] = item
            else:
                sums[place : place + 1, :] += item


def norm_back(values, back_own, back_received, extra, gain, name):
    shapes = [
        jax.ShapeDtypeStruct(values.shape, BF16),
        jax.ShapeDtypeStruct((8, values.shape[1]), F32),
    ]
    return pl.pallas_call(
        norm_back_kernel,
        in_specs=[vmem()] * 5,
        out_specs=[vmem()] * len(shapes),
        out_shape=shapes,
        compiler_params=limit(16),
        cost_estimate=cost(0.1),
        name=name,
    )(values, back_own, back_received, extra, gain[None])


def early_kernel(info, sums, up_own, up_other, out):
    core = info[1]
    half = out.shape[1]
    for place in range(4):
        for side in range(2):
            out[2 * place + side : 2 * place + side + 1, :] = sums[place : place + 1, span(side, half)]
    for place in range(4):
        item = up_own[:, span(place, half)] + up_other[:, span(place, half)]
        out[8 + place : 9 + place, :] = jnp.where(core == 0, item, 0.0)
        out[12 + place : 13 + place, :] = jnp.where(core == 0, 0.0, item)


def late_kernel(info, sums, *refs):
    core = info[1]
    pairs, out = refs[:-1], refs[-1]
    half = out.shape[1]
    out[...] = jnp.zeros_like(out)
    for place in range(2):
        for side in range(2):
            out[2 * place + side : 2 * place + side + 1, :] = sums[place + 1 : place + 2, span(side, half)]
    for index, pair in enumerate(pairs):
        here = span(index, LANES)
        for place, which in enumerate((0, 2)):
            item = pair[:, span(which, LANES)]
            first = 4 + 2 * place
            out[first : first + 1, here] = jnp.where(core == 0, item, 0.0)
            out[first + 1 : first + 2, here] = jnp.where(core == 0, 0.0, item)


def pack(kernel, info, operands, half, name):
    return pl.pallas_call(
        kernel,
        in_specs=[smem()] + [vmem()] * len(operands),
        out_specs=vmem(),
        out_shape=jax.ShapeDtypeStruct((16, half), F32),
        cost_estimate=cost(0.1),
        name=name,
    )(info, *operands)


def place_kernel(shard, order, *refs):
    pieces, out = refs[:-1], refs[-1]
    place = 0
    for piece in pieces:
        for step in range(piece.shape[0] // shard):
            start = pl.multiple_of(order[place] * shard, 16)
            out[pl.ds(start, shard), :] = piece[span(step, shard), :]
            place += 1


def place_blocks(order, pieces):
    shard, columns = pieces[0].shape
    return pl.pallas_call(
        functools.partial(place_kernel, shard),
        in_specs=[smem()] + [vmem()] * len(pieces),
        out_specs=vmem(),
        out_shape=jax.ShapeDtypeStruct((shard * order.shape[0], columns), BF16),
        cost_estimate=cost(0.1),
        name="place_blocks",
    )(order, *pieces)


class Cube:
    def __init__(self, shard_rows):
        self.shard_rows = shard_rows
        self.zy = lax.axis_size("zy")
        self.cores = lax.axis_size("core")
        self.size = self.zy * lax.axis_size("x")
        self.bits = self.size.bit_length() - 1
        self.direct = self.size == 1 << self.bits and self.bits >= 2 and shard_rows % 16 == 0
        outer = list(range(self.bits - 1, 1, -1))
        self.dims = [outer + [0, 1], outer + [1, 0]]
        if self.direct:
            masks = [
                [sum(1 << dims[step] for step in range(self.bits) if place >> step & 1) for place in range(self.size)]
                for dims in self.dims
            ]
            mine = lax.axis_index("zy") * 2 + lax.axis_index("x")
            core = lax.axis_index("core")
            chosen = jnp.where(core == 0, jnp.array(masks[0], jnp.int32), jnp.array(masks[1], jnp.int32))
            self.order = jnp.bitwise_xor(mine.astype(jnp.int32), chosen)
        else:
            blocks = shard_rows * self.size // 48
            self.order = jnp.arange(blocks, dtype=jnp.int32)

    def send(self, values, step):
        pairs = []
        for zy in range(self.zy):
            for core in range(self.cores):
                for x in range(2):
                    other = (zy * 2 + x) ^ (1 << self.dims[core][step])
                    pairs.append(((zy * 2 + core) * 2 + x, (other // 2 * 2 + core) * 2 + other % 2))
        return lax.ppermute(values, ("zy", "core", "x"), pairs)

    def joined(self, pieces):
        return pieces[0] if len(pieces) == 1 else jnp.concatenate(pieces, axis=0)

    def grow(self, pieces, payload=None):
        payload = self.joined(pieces) if payload is None else payload
        return pieces + [self.send(payload, len(pieces) - 1)]

    def finish(self, pieces):
        if not self.direct:
            return lax.all_gather(pieces[0], ("zy", "x"), axis=0, tiled=True)
        return place_blocks(self.order, pieces)

    def payload(self, values):
        return values[values.shape[0] // 2 :]

    def reduce_send(self, payload, step):
        return self.send(payload, self.bits - 1 - step)

    def merge(self, values, received):
        return (values[: values.shape[0] // 2].astype(F32) + received.astype(F32)).astype(BF16)

    def scatter(self, values):
        return lax.psum_scatter(values, ("zy", "x"), scatter_dimension=0, tiled=True)

    def total(self, values):
        if not self.direct:
            return lax.psum(values, ("zy", "core", "x"))
        for step in range(self.bits):
            values = values + self.send(values, step)
        return values + exchange(values)


def swap_small(values):
    return lax.ppermute(values, ("core", "x"), [(0, 0), (1, 2), (2, 1), (3, 3)])


def swap_send(values):
    return lax.ppermute(values, ("core", "x"), [(1, 2), (2, 1)])


def swap_pick(values, received):
    return jnp.where(lax.axis_index("core") == lax.axis_index("x"), values, received)


def swap(values):
    return swap_pick(values, swap_send(values))


def exchange(values):
    return lax.ppermute(values, "core", [(0, 1), (1, 0)])


def tie(values, other):
    return lax.optimization_barrier((values, other))


def shards(
    hidden_in,
    seq_lens,
    ln1_gain,
    ln1_bias,
    w_qkv,
    bias_qv,
    w_out,
    bias_out,
    ln2_gain,
    ln2_bias,
    w_up,
    bias_up,
    w_down,
    bias_down,
    grad_out,
):
    core = lax.axis_index("core")
    group = ("zy", "x")
    rows, width = hidden_in.shape
    shard_rows = w_up.shape[0]
    head_cols = w_qkv.shape[2]
    hidden_cols = w_up.shape[1]
    pairs = head_cols // LANES
    qkv_cols = 3 * head_cols
    cube = Cube(shard_rows)

    qkv_shard = w_qkv.reshape(3, shard_rows, pairs, LANES).transpose(1, 2, 0, 3).reshape(shard_rows, qkv_cols)
    shard = swap(jnp.concatenate([qkv_shard, w_out.T, w_up, w_down.T], axis=1))
    attn_cols = qkv_cols + head_cols
    hidden_in, shard = tie(hidden_in, shard)
    residual_low = swap(hidden_in)
    attn_pieces = [shard[:, :attn_cols]]
    rest_weights = lax.all_gather(shard[:, attn_cols:], group, axis=0, tiled=True)
    length = swap_small(seq_lens)[0]
    if cube.direct:
        for step in range(cube.bits):
            attn_pieces = cube.grow(attn_pieces)
    attn_weights = cube.finish(attn_pieces)
    qkv_weight, out_weight = attn_weights[:, :qkv_cols], attn_weights[:, qkv_cols:]
    grad_low = swap(grad_out)
    info = jnp.stack([length, core.astype(jnp.int32)])

    residual = residual_low.astype(F32)
    unit_one, _ = norm_stats(residual)
    norm_own = (unit_one * ln1_gain + ln1_bias).astype(BF16)
    norm_other = exchange(norm_own)
    bias_here = lax.dynamic_slice_in_dim(bias_qv, core * head_cols, head_cols, 1)
    qkv_bias = jnp.stack([bias_here[0], jnp.zeros((head_cols,), F32), bias_here[1]])
    qkv_bias = qkv_bias.reshape(3, pairs, LANES).transpose(1, 0, 2).reshape(qkv_cols)
    qkv_own = (dot(norm_own, qkv_weight) + qkv_bias).astype(BF16)
    qkv_other = (dot(norm_other, qkv_weight) + qkv_bias).astype(BF16)
    mixed_own, mixed_other = attend_forward(info, qkv_own, qkv_other)
    attn_received = exchange(dot(mixed_other, out_weight, NT).astype(BF16))
    hidden = residual + (dot(mixed_own, out_weight, NT) + attn_received.astype(F32)) + bias_out
    rest_weights, hidden = tie(rest_weights, hidden)
    unit_two, _ = norm_stats(hidden)
    two_own = (unit_two * ln2_gain + ln2_bias).astype(BF16)
    two_other = exchange(two_own)
    bias_up_here = lax.dynamic_slice_in_dim(bias_up, core * hidden_cols, hidden_cols, 0)[None]

    slots = core * rows + jnp.arange(rows, dtype=jnp.int32)
    grad_own = jnp.where((slots < length)[:, None], grad_low, jnp.zeros_like(grad_low))
    grad_other = exchange(grad_own)

    active_other, grad_pre_other, mlp_other, back_two_other, up_sum_other = feed(
        two_other, grad_other, rest_weights, bias_up_here, BF16, "feed_other"
    )
    back_two_received = exchange(back_two_other)
    mlp_received = exchange(mlp_other)
    active_own, grad_pre_own, mlp_own, back_two_own, up_sum_own = feed(
        two_own, grad_own, rest_weights, bias_up_here, BF16, "feed_own"
    )
    mlp_sum = mlp_own.astype(F32) + mlp_received.astype(F32)
    layer_here = (hidden + mlp_sum + bias_down).astype(BF16)
    layer_there = swap_send(layer_here)

    up_grads = weight_grads(
        cube.order, [(two_own, two_other, grad_pre_own, grad_pre_other)], "up_grads"
    )
    if cube.direct:
        payload, back_two_own = tie(cube.payload(up_grads), back_two_own)
        up_received = cube.reduce_send(payload, 0)
    attn_grad_own, sums = norm_back(
        hidden, back_two_own, back_two_received, grad_own, ln2_gain, "norm_two_back"
    )
    attn_grad_other = exchange(attn_grad_own)
    first_grads = weight_grads(
        cube.order,
        [
            (grad_own, grad_other, active_own, active_other),
            (attn_grad_own, attn_grad_other, mixed_own, mixed_other),
        ],
        "down_out_grads",
    )
    grad_mixed_own = dot(attn_grad_own, out_weight).astype(BF16)
    grad_mixed_other = dot(attn_grad_other, out_weight).astype(BF16)
    early = pack(early_kernel, info, [sums, up_sum_own, up_sum_other], width // 2, "early_sums")
    if cube.direct:
        up_received, first_grads = tie(up_received, first_grads)
        early = early.astype(BF16)
    else:
        early = cube.total(early)
        first_grads = cube.scatter(first_grads)
        up_grads = cube.scatter(up_grads)

    backs_own, backs_other, back_sums = [], [], []
    grad_pair = (grad_mixed_own, grad_mixed_other)
    steps = cube.bits if cube.direct else 0
    last_grads = None
    for pair in range(max(pairs + 1, steps)):
        received = None
        if pair < steps:
            padding = ((0, 0), (0, first_grads.shape[1] - early.shape[1]))
            payload = jnp.concatenate([cube.payload(first_grads), jnp.pad(early, padding)], axis=0)
            payload, grad_pair = tie(payload, grad_pair)
            received = cube.reduce_send(payload, pair)
        if pair < pairs:
            back_own, back_other, back_sum = attend_backward(pair, info, qkv_own, qkv_other, *grad_pair)
            if received is not None:
                received, back_own = tie(received, back_own)
            backs_own.append(back_own)
            backs_other.append(back_other)
            back_sums.append(back_sum)
        if pair == pairs:
            back_own = jnp.concatenate(backs_own, axis=1)
            back_other = jnp.concatenate(backs_other, axis=1)
            last_grads = weight_grads(
                cube.order, [(norm_own, norm_other, back_own, back_other)], "last_weight_grads"
            )
            if cube.direct:
                payload, back_other = tie(cube.payload(last_grads), back_other)
                last_received = cube.reduce_send(payload, 0)
            layer_there, back_other = tie(layer_there, back_other)
            layer_out = swap_pick(layer_here, layer_there)
            back_one_received = exchange(dot(back_other, qkv_weight, NT).astype(BF16))
            grad_input, sums = norm_back(
                residual_low,
                dot(back_own, qkv_weight, NT),
                back_one_received,
                attn_grad_own,
                ln1_gain,
                "norm_one_back",
            )
            if received is not None:
                received, grad_input = tie(received, grad_input)
        if received is not None:
            first_grads = cube.merge(first_grads, received[:-16])
            if pair == 0:
                up_grads = cube.merge(up_grads, up_received)
                first_grads = jnp.concatenate([up_grads, first_grads], axis=1)
            early = (early.astype(F32) + received[-16:, : early.shape[1]].astype(F32)).astype(BF16)
    if cube.direct:
        early = early.astype(F32)
        early = early + exchange(early)
    else:
        first_grads = jnp.concatenate([up_grads, first_grads], axis=1)
    done_grads = first_grads.reshape(-1, width)
    late = pack(late_kernel, info, [sums] + back_sums, width // 2, "late_sums")
    if cube.direct:
        late = late + cube.reduce_send(late, 0)
        last_received, grad_input = tie(last_received, grad_input)
    final_low = swap(jnp.concatenate([grad_input, done_grads], axis=0))
    if cube.direct:
        last_grads = cube.merge(last_grads, last_received)
        late = late.astype(BF16)
        for step in range(1, steps):
            padding = ((0, 0), (0, qkv_cols - late.shape[1]))
            payload = jnp.concatenate([cube.payload(last_grads), jnp.pad(late, padding)], axis=0)
            received = cube.reduce_send(payload, step)
            if step == steps - 1:
                received, final_low = tie(received, final_low)
            last_grads = cube.merge(last_grads, received[:-16])
            late = (late.astype(F32) + received[-16:, : late.shape[1]].astype(F32)).astype(BF16)
        late = late.astype(F32)
        late = late + exchange(late)
    else:
        last_grads = cube.scatter(last_grads)
        late = cube.total(late)
    last_grads = swap(last_grads)
    grad_input = final_low[:rows].astype(F32)
    done_grads = final_low[rows:].reshape(shard_rows, -1)

    early = early.reshape(-1)
    down_bias, gain_two, shift_two, out_bias, up_bias = jnp.split(early, [width * n for n in range(1, 5)])
    late = late.reshape(-1)[: 4 * width]
    gain_one, shift_one, qv_bias = jnp.split(late, [width, 2 * width])
    grad_w_qkv = last_grads.reshape(shard_rows, pairs, 3, LANES).transpose(2, 0, 1, 3)
    grad_w_qkv = grad_w_qkv.reshape(3, shard_rows, head_cols).astype(F32)
    grad_w_up = done_grads[:, :hidden_cols].astype(F32)
    grad_w_down = done_grads[:, hidden_cols : 2 * hidden_cols].T.astype(F32)
    grad_w_out = done_grads[:, 2 * hidden_cols :].T.astype(F32)
    return (
        layer_out,
        grad_input,
        gain_one,
        shift_one,
        grad_w_qkv,
        qv_bias.reshape(2, width),
        grad_w_out,
        out_bias,
        gain_two,
        shift_two,
        grad_w_up,
        up_bias,
        grad_w_down,
        down_bias,
    )


def solution(mesh):
    cores = 2
    devices = mesh.devices
    inner = Mesh(devices.reshape(devices.shape[0] // cores, cores, devices.shape[1]), ("zy", "core", "x"))
    dp = ("zy", "core")
    token = P(("zy", "core", "x"), None)
    in_specs = (
        token,
        P(dp),
        P(),
        P(),
        P(None, dp, "x"),
        P(),
        P("x", dp),
        P(),
        P(),
        P(),
        P(dp, "x"),
        P(),
        P("x", dp),
        P(),
        token,
    )
    out_specs = (
        token,
        token,
        P(),
        P(),
        P(None, dp, "x"),
        P(),
        P("x", dp),
        P(),
        P(),
        P(),
        P(dp, "x"),
        P(),
        P("x", dp),
        P(),
    )
    return jax.shard_map(shards, mesh=inner, in_specs=in_specs, out_specs=out_specs, check_vma=False)
```

```python
import functools
import math

import jax
import jax.numpy as jnp
from jax import lax
from jax.experimental import pallas as pl
from jax.experimental.pallas import tpu as pltpu
from jax.sharding import Mesh, PartitionSpec as P

HD = 64
LEN_MIN = 864
EPS = 1e-05
LANES = 128
BLOCK = 256
MASKED = -1000000000.0
F32 = jnp.float32
BF16 = jnp.bfloat16
NN = (((1,), (0,)), ((), ()))
NT = (((1,), (1,)), ((), ()))
TN = (((0,), (0,)), ((), ()))


def dot(left, right, dims=NN):
    return lax.dot_general(left, right, dims, preferred_element_type=F32)


def norm_stats(values):
    center = values - jnp.mean(values, axis=-1, keepdims=True)
    inverse = lax.rsqrt(jnp.mean(center * center, axis=-1, keepdims=True) + EPS)
    return center * inverse, inverse


def head_part(values, head):
    lane = lax.broadcasted_iota(jnp.int32, (1, LANES), 1)
    keep = (lane < HD) if head == 0 else (lane >= HD)
    return jnp.where(keep, values, jnp.zeros_like(values))


def lane_block(first):
    return pl.ds(pl.multiple_of(first, LANES), LANES)


def row_half(index, rows):
    return pl.ds(pl.multiple_of(index * rows, rows), rows)


def span(block, size=BLOCK):
    return slice(block * size, (block + 1) * size)


def vmem():
    return pl.BlockSpec(memory_space=pltpu.VMEM)


def smem():
    return pl.BlockSpec(memory_space=pltpu.SMEM)


def limit(mib):
    return pltpu.CompilerParams(vmem_limit_bytes=mib * 1024 * 1024)


def project_kernel(left, weight, out):
    out[...] = dot(left[...], weight[...], NT).astype(out.dtype)


def project(left, weight, name):
    return pl.pallas_call(
        project_kernel,
        in_specs=[vmem()] * 2,
        out_specs=vmem(),
        out_shape=jax.ShapeDtypeStruct((left.shape[0], weight.shape[0]), BF16),
        compiler_params=limit(16),
        cost_estimate=cost(0.1),
        name=name,
    )(left, weight)


def cost(microseconds):
    return pl.CostEstimate(flops=int(microseconds * 1.1e9), transcendentals=0, bytes_accessed=1)


def fill_halves(target, core, own, other):
    rows = own.shape[0]
    target[row_half(core, rows), :] = own[...]
    target[row_half(1 - core, rows), :] = other[...]


def split_halves(source, core, own, other):
    rows = own.shape[0]
    own[...] = source[row_half(core, rows), :]
    other[...] = source[row_half(1 - core, rows), :]


def attend_forward_kernel(info, qkv_own, qkv_other, out_own, out_other, qkv, out):
    length, core = info[0], info[1]
    blocks = qkv.shape[0] // BLOCK
    fill_halves(qkv, core, qkv_own, qkv_other)

    def part(block, which):
        return qkv[span(block), span(which, LANES)]

    column = lax.broadcasted_iota(jnp.int32, (1, BLOCK), 1)
    row = lax.broadcasted_iota(jnp.int32, (BLOCK, 1), 0)

    def score(block, head):
        query = head_part(part(block, 0), head) * jnp.asarray(0.125, BF16)
        last = jnp.minimum(row + block * BLOCK, length - 1)
        scores = []
        for other in range(block + 1):
            piece = dot(query, part(other, 1), NT)
            if other == block or (other + 1) * BLOCK > LEN_MIN:
                piece = jnp.where(column + other * BLOCK <= last, piece, MASKED)
            scores.append(piece)
        return scores

    tasks = [(block, head) for block in range(blocks) for head in range(2)]
    upcoming = score(*tasks[0])
    kept = None
    for place, (block, head) in enumerate(tasks):
        scores = upcoming
        if place + 1 < len(tasks):
            upcoming = score(*tasks[place + 1])
        top = functools.reduce(jnp.maximum, scores)
        top = jnp.max(top, axis=1, keepdims=True)
        weights = [jnp.exp(piece - top) for piece in scores]
        total = jnp.sum(functools.reduce(jnp.add, weights), axis=1, keepdims=True)
        mixed = functools.reduce(
            jnp.add,
            [
                dot(weight.astype(BF16), head_part(part(other, 2), head))
                for other, weight in enumerate(weights)
            ],
        )
        mixed = mixed / total
        if head == 0:
            kept = mixed
        else:
            out[span(block), :] = (kept + mixed).astype(BF16)
    split_halves(out, core, out_own, out_other)


def attend_forward(info, qkv_own, qkv_other):
    rows, width = qkv_own.shape[0], qkv_own.shape[1] // 3
    taken = pl.BlockSpec((rows, 3 * LANES), lambda pair: (0, pair))
    given = pl.BlockSpec((rows, LANES), lambda pair: (0, pair))
    shape = jax.ShapeDtypeStruct((rows, width), BF16)
    return pl.pallas_call(
        attend_forward_kernel,
        grid=(width // LANES,),
        in_specs=[smem(), taken, taken],
        out_specs=[given, given],
        out_shape=[shape, shape],
        scratch_shapes=[
            pltpu.VMEM((2 * rows, 3 * LANES), BF16),
            pltpu.VMEM((2 * rows, LANES), BF16),
        ],
        compiler_params=limit(32),
        cost_estimate=cost(0.1),
        name="attend_forward",
    )(info, qkv_own, qkv_other)


def attend_backward_kernel(
    info,
    qkv_own,
    qkv_other,
    grad_own,
    grad_other,
    back_own,
    back_other,
    sums,
    qkv,
    grad,
    back,
    key_sum,
    value_sum,
):
    length, core = info[0], info[1]
    blocks = qkv.shape[0] // BLOCK
    fill_halves(qkv, core, qkv_own, qkv_other)
    fill_halves(grad, core, grad_own, grad_other)
    key_sum[...] = jnp.zeros_like(key_sum)
    value_sum[...] = jnp.zeros_like(value_sum)
    eighth = jnp.asarray(0.125, BF16)

    def part(block, which):
        return qkv[span(block), span(which, LANES)]

    column = lax.broadcasted_iota(jnp.int32, (1, BLOCK), 1)
    row = lax.broadcasted_iota(jnp.int32, (BLOCK, 1), 0)

    def products(block, head):
        query = head_part(part(block, 0), head) * eighth
        mixed = head_part(grad[span(block), :], head)
        last = jnp.minimum(column + block * BLOCK, length - 1)
        scores, grads = [], []
        for other in range(block + 1):
            piece = dot(part(other, 1), query, NT)
            if other == block or (other + 1) * BLOCK > LEN_MIN:
                piece = jnp.where(row + other * BLOCK <= last, piece, MASKED)
            scores.append(piece)
            grads.append(dot(part(other, 2), mixed, NT))
        return query, mixed, scores, grads

    tasks = [(block, head) for block in range(blocks) for head in range(2)]
    upcoming = products(*tasks[0])
    kept = None
    for place, (block, head) in enumerate(tasks):
        query, mixed, scores, grads = upcoming
        if place + 1 < len(tasks):
            upcoming = products(*tasks[place + 1])
        top = jnp.max(functools.reduce(jnp.maximum, scores), axis=0, keepdims=True)
        weights = [jnp.exp(piece - top) for piece in scores]
        total = jnp.sum(functools.reduce(jnp.add, weights), axis=0, keepdims=True)
        inverse = 1.0 / total
        weights = [weight * inverse for weight in weights]
        products_sum = functools.reduce(jnp.add, [w * g for w, g in zip(weights, grads)])
        inner = jnp.sum(products_sum, axis=0, keepdims=True)
        query_sum = None
        for other in range(block + 1):
            weight = weights[other]
            change = (weight * (grads[other] - inner)).astype(BF16)
            value_sum[span(other), :] += dot(weight.astype(BF16), mixed)
            key_sum[span(other), :] += dot(change, query)
            piece = dot(change, head_part(part(other, 1), head) * eighth, TN)
            query_sum = piece if query_sum is None else query_sum + piece
        if head == 0:
            kept = query_sum
        else:
            back[span(block), span(0, LANES)] = (kept + query_sum).astype(BF16)
    back[:, span(1, LANES)] = key_sum[...].astype(BF16)
    back[:, span(2, LANES)] = value_sum[...].astype(BF16)
    split_halves(back, core, back_own, back_other)
    sums[...] = jnp.sum(back[...].astype(F32), axis=0, keepdims=True)


def attend_backward(pair, info, qkv_own, qkv_other, grad_own, grad_other):
    rows = grad_own.shape[0]
    qkv_spec = pl.BlockSpec((rows, 3 * LANES), lambda step: (0, pair))
    grad_spec = pl.BlockSpec((rows, LANES), lambda step: (0, pair))
    shape = jax.ShapeDtypeStruct((rows, 3 * LANES), BF16)
    return pl.pallas_call(
        attend_backward_kernel,
        grid=(1,),
        in_specs=[smem(), qkv_spec, qkv_spec, grad_spec, grad_spec],
        out_specs=[vmem(), vmem(), vmem()],
        out_shape=[shape, shape, jax.ShapeDtypeStruct((1, 3 * LANES), F32)],
        scratch_shapes=[
            pltpu.VMEM((2 * rows, 3 * LANES), BF16),
            pltpu.VMEM((2 * rows, LANES), BF16),
            pltpu.VMEM((2 * rows, 3 * LANES), BF16),
            pltpu.VMEM((2 * rows, LANES), F32),
            pltpu.VMEM((2 * rows, LANES), F32),
        ],
        compiler_params=limit(32),
        cost_estimate=cost(13),
        name=f"attend_backward_{pair}",
    )(info, qkv_own, qkv_other, grad_own, grad_other)


def feed_kernel(two, grad, weight, bias, active, grad_pre, mlp, back, bias_sum):
    hidden = active.shape[1]
    slope = math.sqrt(2.0 / math.pi)
    cubic = slope * 0.044715
    for chunk in range(hidden // BLOCK):
        here = span(chunk)
        there = slice(hidden + chunk * BLOCK, hidden + (chunk + 1) * BLOCK)
        pre = dot(two[...], weight[:, here]) + bias[:, here]
        grad_active = dot(grad[...], weight[:, there])
        square = pre * pre
        half = 0.5 + 0.5 * jnp.tanh(pre * (slope + cubic * square))
        value = pre * half
        change = half + (value - value * half) * (2.0 * slope + (6.0 * cubic) * square)
        active[:, here] = value.astype(BF16)
        low = (grad_active * change).astype(BF16)
        grad_pre[:, here] = low
        bias_sum[:, here] = jnp.sum(low.astype(F32), axis=0, keepdims=True)
    for chunk in range(mlp.shape[1] // BLOCK):
        here = span(chunk)
        back[:, here] = dot(grad_pre[...], weight[here, :hidden], NT).astype(back.dtype)
        mlp[:, here] = dot(active[...], weight[here, hidden : 2 * hidden], NT).astype(mlp.dtype)


def feed(two, grad, weight, bias, result, name):
    rows, width = two.shape
    hidden = bias.shape[1]
    low = jax.ShapeDtypeStruct((rows, hidden), BF16)
    terms = jax.ShapeDtypeStruct((rows, width), result)
    return pl.pallas_call(
        feed_kernel,
        in_specs=[vmem()] * 4,
        out_specs=[vmem()] * 5,
        out_shape=[low, low, terms, terms, jax.ShapeDtypeStruct((1, hidden), F32)],
        compiler_params=limit(24),
        cost_estimate=cost(12),
        name=name,
    )(two, grad, weight, bias)


def weight_grads_kernel(count, shard, order, *refs):
    lefts_own, lefts_other = refs[:count], refs[count : 2 * count]
    rights_own, rights_other = refs[2 * count : 3 * count], refs[3 * count : 4 * count]
    out, total = refs[4 * count], refs[4 * count + 1]
    first = 0
    for term in range(count):
        columns = rights_own[term].shape[1]
        for chunk in range(total.shape[0] // BLOCK):
            here = span(chunk)
            piece = dot(lefts_own[term][:, here], rights_own[term][...], TN)
            piece += dot(lefts_other[term][:, here], rights_other[term][...], TN)
            total[here, first : first + columns] = piece.astype(BF16)
        first += columns
    if shard is None:
        out[...] = total[...]
        return
    for place in range(total.shape[0] // shard):
        start = pl.multiple_of(order[place] * shard, 16)
        out[span(place, shard), :] = total[pl.ds(start, shard), :]


def weight_grads(order, terms, name):
    width = terms[0][0].shape[1]
    columns = sum(term[2].shape[1] for term in terms)
    shard = None if order is None else width // order.shape[0]
    order = jnp.zeros((1,), jnp.int32) if order is None else order
    operands = [term[kind] for kind in range(4) for term in terms]
    return pl.pallas_call(
        functools.partial(weight_grads_kernel, len(terms), shard),
        in_specs=[smem()] + [vmem()] * len(operands),
        out_specs=vmem(),
        out_shape=jax.ShapeDtypeStruct((width, columns), BF16),
        scratch_shapes=[pltpu.VMEM((width, columns), BF16)],
        compiler_params=limit(24),
        cost_estimate=cost(0.1),
        name=name,
    )(order, *operands)


def norm_back_kernel(values, back_own, back_received, extra, gain, low, sums):
    for chunk in range(values.shape[0] // BLOCK):
        here = span(chunk)
        normed, inverse = norm_stats(values[here, :].astype(F32))
        grad = back_own[here, :].astype(F32) + back_received[here, :].astype(F32)
        scaled = grad * gain[...]
        added = extra[here, :].astype(F32)
        result = added + inverse * (
            scaled
            - jnp.mean(scaled, axis=-1, keepdims=True)
            - normed * jnp.mean(scaled * normed, axis=-1, keepdims=True)
        )
        rounded = result.astype(BF16)
        low[here, :] = rounded
        for place, item in enumerate((added, grad * normed, grad, rounded.astype(F32))):
            item = jnp.sum(item, axis=0, keepdims=True)
            if chunk == 0:
                sums[place : place + 1, :] = item
            else:
                sums[place : place + 1, :] += item


def norm_back(values, back_own, back_received, extra, gain, name):
    shapes = [
        jax.ShapeDtypeStruct(values.shape, BF16),
        jax.ShapeDtypeStruct((8, values.shape[1]), F32),
    ]
    return pl.pallas_call(
        norm_back_kernel,
        in_specs=[vmem()] * 5,
        out_specs=[vmem()] * len(shapes),
        out_shape=shapes,
        compiler_params=limit(16),
        cost_estimate=cost(0.1),
        name=name,
    )(values, back_own, back_received, extra, gain[None])


def early_kernel(info, sums, up_own, up_other, out):
    core = info[1]
    half = out.shape[1]
    for place in range(4):
        for side in range(2):
            out[2 * place + side : 2 * place + side + 1, :] = sums[place : place + 1, span(side, half)]
    for place in range(4):
        item = up_own[:, span(place, half)] + up_other[:, span(place, half)]
        out[8 + place : 9 + place, :] = jnp.where(core == 0, item, 0.0)
        out[12 + place : 13 + place, :] = jnp.where(core == 0, 0.0, item)


def late_kernel(info, sums, *refs):
    core = info[1]
    pairs, out = refs[:-1], refs[-1]
    half = out.shape[1]
    out[...] = jnp.zeros_like(out)
    for place in range(2):
        for side in range(2):
            out[2 * place + side : 2 * place + side + 1, :] = sums[place + 1 : place + 2, span(side, half)]
    for index, pair in enumerate(pairs):
        here = span(index, LANES)
        for place, which in enumerate((0, 2)):
            item = pair[:, span(which, LANES)]
            first = 4 + 2 * place
            out[first : first + 1, here] = jnp.where(core == 0, item, 0.0)
            out[first + 1 : first + 2, here] = jnp.where(core == 0, 0.0, item)


def pack(kernel, info, operands, half, name):
    return pl.pallas_call(
        kernel,
        in_specs=[smem()] + [vmem()] * len(operands),
        out_specs=vmem(),
        out_shape=jax.ShapeDtypeStruct((16, half), F32),
        cost_estimate=cost(0.1),
        name=name,
    )(info, *operands)


def place_kernel(shard, order, *refs):
    pieces, out = refs[:-1], refs[-1]
    place = 0
    for piece in pieces:
        for step in range(piece.shape[0] // shard):
            start = pl.multiple_of(order[place] * shard, 16)
            out[pl.ds(start, shard), :] = piece[span(step, shard), :]
            place += 1


def place_blocks(order, pieces):
    shard, columns = pieces[0].shape
    return pl.pallas_call(
        functools.partial(place_kernel, shard),
        in_specs=[smem()] + [vmem()] * len(pieces),
        out_specs=vmem(),
        out_shape=jax.ShapeDtypeStruct((shard * order.shape[0], columns), BF16),
        cost_estimate=cost(0.1),
        name="place_blocks",
    )(order, *pieces)


class Cube:
    def __init__(self, shard_rows):
        self.shard_rows = shard_rows
        self.zy = lax.axis_size("zy")
        self.cores = lax.axis_size("core")
        self.size = self.zy * lax.axis_size("x")
        self.bits = self.size.bit_length() - 1
        self.direct = self.size == 1 << self.bits and self.bits >= 2 and shard_rows % 16 == 0
        outer = list(range(self.bits - 1, 1, -1))
        self.dims = [outer + [0, 1], outer + [1, 0]]
        if self.direct:
            masks = [
                [sum(1 << dims[step] for step in range(self.bits) if place >> step & 1) for place in range(self.size)]
                for dims in self.dims
            ]
            mine = lax.axis_index("zy") * 2 + lax.axis_index("x")
            core = lax.axis_index("core")
            chosen = jnp.where(core == 0, jnp.array(masks[0], jnp.int32), jnp.array(masks[1], jnp.int32))
            self.order = jnp.bitwise_xor(mine.astype(jnp.int32), chosen)
        else:
            blocks = shard_rows * self.size // 48
            self.order = jnp.arange(blocks, dtype=jnp.int32)

    def send(self, values, step):
        pairs = []
        for zy in range(self.zy):
            for core in range(self.cores):
                for x in range(2):
                    other = (zy * 2 + x) ^ (1 << self.dims[core][step])
                    pairs.append(((zy * 2 + core) * 2 + x, (other // 2 * 2 + core) * 2 + other % 2))
        return lax.ppermute(values, ("zy", "core", "x"), pairs)

    def joined(self, pieces):
        return pieces[0] if len(pieces) == 1 else jnp.concatenate(pieces, axis=0)

    def grow(self, pieces, payload=None):
        payload = self.joined(pieces) if payload is None else payload
        return pieces + [self.send(payload, len(pieces) - 1)]

    def finish(self, pieces):
        if not self.direct:
            return lax.all_gather(pieces[0], ("zy", "x"), axis=0, tiled=True)
        return place_blocks(self.order, pieces)

    def payload(self, values):
        return values[values.shape[0] // 2 :]

    def reduce_send(self, payload, step):
        return self.send(payload, self.bits - 1 - step)

    def merge(self, values, received):
        return (values[: values.shape[0] // 2].astype(F32) + received.astype(F32)).astype(BF16)

    def scatter(self, values):
        return lax.psum_scatter(values, ("zy", "x"), scatter_dimension=0, tiled=True)

    def total(self, values):
        if not self.direct:
            return lax.psum(values, ("zy", "core", "x"))
        for step in range(self.bits):
            values = values + self.send(values, step)
        return values + exchange(values)


def swap_small(values):
    return lax.ppermute(values, ("core", "x"), [(0, 0), (1, 2), (2, 1), (3, 3)])


def swap_send(values):
    return lax.ppermute(values, ("core", "x"), [(1, 2), (2, 1)])


def swap_pick(values, received):
    return jnp.where(lax.axis_index("core") == lax.axis_index("x"), values, received)


def swap(values):
    return swap_pick(values, swap_send(values))


def exchange(values):
    return lax.ppermute(values, "core", [(0, 1), (1, 0)])


def tie(values, other):
    return lax.optimization_barrier((values, other))


def shards(
    hidden_in,
    seq_lens,
    ln1_gain,
    ln1_bias,
    w_qkv,
    bias_qv,
    w_out,
    bias_out,
    ln2_gain,
    ln2_bias,
    w_up,
    bias_up,
    w_down,
    bias_down,
    grad_out,
):
    core = lax.axis_index("core")
    group = ("zy", "x")
    rows, width = hidden_in.shape
    shard_rows = w_up.shape[0]
    head_cols = w_qkv.shape[2]
    hidden_cols = w_up.shape[1]
    pairs = head_cols // LANES
    qkv_cols = 3 * head_cols
    cube = Cube(shard_rows)

    qkv_shard = w_qkv.reshape(3, shard_rows, pairs, LANES).transpose(1, 2, 0, 3).reshape(shard_rows, qkv_cols)
    shard = swap(jnp.concatenate([qkv_shard, w_out.T, w_up, w_down.T], axis=1))
    attn_cols = qkv_cols + head_cols
    hidden_in, shard = tie(hidden_in, shard)
    residual_low = swap(hidden_in)
    attn_pieces = [shard[:, :attn_cols]]
    rest_weights = lax.all_gather(shard[:, attn_cols:], group, axis=0, tiled=True)
    length = swap_small(seq_lens)[0]
    if cube.direct:
        for step in range(cube.bits):
            payload = cube.joined(attn_pieces)
            if step == cube.bits - 2:
                payload, residual_low = tie(payload, residual_low)
            attn_pieces = cube.grow(attn_pieces, payload)
    attn_weights = cube.finish(attn_pieces)
    qkv_weight, out_weight = attn_weights[:, :qkv_cols], attn_weights[:, qkv_cols:]
    grad_low = swap(grad_out)
    info = jnp.stack([length, core.astype(jnp.int32)])

    residual = residual_low.astype(F32)
    unit_one, _ = norm_stats(residual)
    norm_own = (unit_one * ln1_gain + ln1_bias).astype(BF16)
    norm_other = exchange(norm_own)
    bias_here = lax.dynamic_slice_in_dim(bias_qv, core * head_cols, head_cols, 1)
    qkv_bias = jnp.stack([bias_here[0], jnp.zeros((head_cols,), F32), bias_here[1]])
    qkv_bias = qkv_bias.reshape(3, pairs, LANES).transpose(1, 0, 2).reshape(qkv_cols)
    qkv_own = (dot(norm_own, qkv_weight) + qkv_bias).astype(BF16)
    qkv_other = (dot(norm_other, qkv_weight) + qkv_bias).astype(BF16)
    mixed_own, mixed_other = attend_forward(info, qkv_own, qkv_other)
    attn_received = exchange(dot(mixed_other, out_weight, NT).astype(BF16))
    hidden = residual + (dot(mixed_own, out_weight, NT) + attn_received.astype(F32)) + bias_out
    rest_weights, hidden = tie(rest_weights, hidden)
    unit_two, _ = norm_stats(hidden)
    two_own = (unit_two * ln2_gain + ln2_bias).astype(BF16)
    two_other = exchange(two_own)
    bias_up_here = lax.dynamic_slice_in_dim(bias_up, core * hidden_cols, hidden_cols, 0)[None]

    slots = core * rows + jnp.arange(rows, dtype=jnp.int32)
    grad_own = jnp.where((slots < length)[:, None], grad_low, jnp.zeros_like(grad_low))
    grad_other = exchange(grad_own)

    active_other, grad_pre_other, mlp_other, back_two_other, up_sum_other = feed(
        two_other, grad_other, rest_weights, bias_up_here, BF16, "feed_other"
    )
    back_two_received = exchange(back_two_other)
    mlp_received = exchange(mlp_other)
    active_own, grad_pre_own, mlp_own, back_two_own, up_sum_own = feed(
        two_own, grad_own, rest_weights, bias_up_here, BF16, "feed_own"
    )
    mlp_sum = mlp_own.astype(F32) + mlp_received.astype(F32)
    layer_here = (hidden + mlp_sum + bias_down).astype(BF16)
    layer_there = swap_send(layer_here)

    up_grads = weight_grads(
        cube.order, [(two_own, two_other, grad_pre_own, grad_pre_other)], "up_grads"
    )
    if cube.direct:
        payload, back_two_own = tie(cube.payload(up_grads), back_two_own)
        up_received = cube.reduce_send(payload, 0)
    attn_grad_own, sums = norm_back(
        hidden, back_two_own, back_two_received, grad_own, ln2_gain, "norm_two_back"
    )
    attn_grad_other = exchange(attn_grad_own)
    first_grads = weight_grads(
        cube.order,
        [
            (grad_own, grad_other, active_own, active_other),
            (attn_grad_own, attn_grad_other, mixed_own, mixed_other),
        ],
        "down_out_grads",
    )
    grad_mixed_own = dot(attn_grad_own, out_weight).astype(BF16)
    grad_mixed_other = dot(attn_grad_other, out_weight).astype(BF16)
    early = pack(early_kernel, info, [sums, up_sum_own, up_sum_other], width // 2, "early_sums")
    if cube.direct:
        up_received, first_grads = tie(up_received, first_grads)
        early = early.astype(BF16)
    else:
        early = cube.total(early)
        first_grads = cube.scatter(first_grads)
        up_grads = cube.scatter(up_grads)

    def finish_step(grads, small, received):
        grads = cube.merge(grads, received[:-16])
        small = (small.astype(F32) + received[-16:, : small.shape[1]].astype(F32)).astype(BF16)
        return grads, small

    backs_own, backs_other, back_sums = [], [], []
    grad_pair = (grad_mixed_own, grad_mixed_other)
    steps = cube.bits if cube.direct else 0
    last_grads, pending = None, None
    for pair in range(max(pairs + 1, steps)):
        if pending is not None:
            first_grads, early = finish_step(first_grads, early, pending)
            pending = None
        received = None
        if pair < steps:
            padding = ((0, 0), (0, first_grads.shape[1] - early.shape[1]))
            payload = jnp.concatenate([cube.payload(first_grads), jnp.pad(early, padding)], axis=0)
            payload, grad_pair = tie(payload, grad_pair)
            received = cube.reduce_send(payload, pair)
        if pair < pairs:
            back_own, back_other, back_sum = attend_backward(pair, info, qkv_own, qkv_other, *grad_pair)
            if received is not None:
                received, back_own = tie(received, back_own)
            backs_own.append(back_own)
            backs_other.append(back_other)
            back_sums.append(back_sum)
        if pair == pairs:
            back_own = jnp.concatenate(backs_own, axis=1)
            back_other = jnp.concatenate(backs_other, axis=1)
            last_grads = weight_grads(
                cube.order, [(norm_own, norm_other, back_own, back_other)], "last_weight_grads"
            )
            if cube.direct:
                payload, back_other = tie(cube.payload(last_grads), back_other)
                last_received = cube.reduce_send(payload, 0)
            layer_there, back_other = tie(layer_there, back_other)
            layer_out = swap_pick(layer_here, layer_there)
            back_one_received = exchange(project(back_other, qkv_weight, "back_one_other"))
            grad_input, sums = norm_back(
                residual_low,
                project(back_own, qkv_weight, "back_one_own"),
                back_one_received,
                attn_grad_own,
                ln1_gain,
                "norm_one_back",
            )
        if received is not None and pair == pairs:
            pending = received
            received = None
        if received is not None:
            first_grads = cube.merge(first_grads, received[:-16])
            if pair == 0:
                up_grads = cube.merge(up_grads, up_received)
                first_grads = jnp.concatenate([up_grads, first_grads], axis=1)
            early = (early.astype(F32) + received[-16:, : early.shape[1]].astype(F32)).astype(BF16)
    if not cube.direct:
        first_grads = jnp.concatenate([up_grads, first_grads], axis=1)
    late = pack(late_kernel, info, [sums] + back_sums, width // 2, "late_sums")
    if cube.direct:
        late = late + cube.reduce_send(late, 0)
        last_received, grad_input = tie(last_received, grad_input)
    final_low = swap(grad_input)
    if cube.direct:
        last_grads = cube.merge(last_grads, last_received)
        late = late.astype(BF16)
        for step in range(1, steps):
            padding = ((0, 0), (0, qkv_cols - late.shape[1]))
            payload = jnp.concatenate([cube.payload(last_grads), jnp.pad(late, padding)], axis=0)
            received = cube.reduce_send(payload, step)
            if step == steps - 1:
                received, final_low = tie(received, final_low)
                if pending is not None:
                    received, pending = tie(received, pending)
            last_grads = cube.merge(last_grads, received[:-16])
            late = (late.astype(F32) + received[-16:, : late.shape[1]].astype(F32)).astype(BF16)
        if pending is not None:
            first_grads, early = finish_step(first_grads, early, pending)
        both = jnp.concatenate([late, early], axis=1).astype(F32)
        both = both + exchange(both)
        late, early = both[:, : late.shape[1]], both[:, late.shape[1] :]
    else:
        last_grads = cube.scatter(last_grads)
        late = cube.total(late)
    done_grads = swap(jnp.concatenate([first_grads, last_grads], axis=1))
    done_grads, last_grads = done_grads[:, :-qkv_cols], done_grads[:, -qkv_cols:]
    grad_input = final_low.astype(F32)

    early = early.reshape(-1)
    down_bias, gain_two, shift_two, out_bias, up_bias = jnp.split(early, [width * n for n in range(1, 5)])
    late = late.reshape(-1)[: 4 * width]
    gain_one, shift_one, qv_bias = jnp.split(late, [width, 2 * width])
    grad_w_qkv = last_grads.reshape(shard_rows, pairs, 3, LANES).transpose(2, 0, 1, 3)
    grad_w_qkv = grad_w_qkv.reshape(3, shard_rows, head_cols).astype(F32)
    grad_w_up = done_grads[:, :hidden_cols].astype(F32)
    grad_w_down = done_grads[:, hidden_cols : 2 * hidden_cols].T.astype(F32)
    grad_w_out = done_grads[:, 2 * hidden_cols :].T.astype(F32)
    return (
        layer_out,
        grad_input,
        gain_one,
        shift_one,
        grad_w_qkv,
        qv_bias.reshape(2, width),
        grad_w_out,
        out_bias,
        gain_two,
        shift_two,
        grad_w_up,
        up_bias,
        grad_w_down,
        down_bias,
    )


def solution(mesh):
    cores = 2
    devices = mesh.devices
    inner = Mesh(devices.reshape(devices.shape[0] // cores, cores, devices.shape[1]), ("zy", "core", "x"))
    dp = ("zy", "core")
    token = P(("zy", "core", "x"), None)
    in_specs = (
        token,
        P(dp),
        P(),
        P(),
        P(None, dp, "x"),
        P(),
        P("x", dp),
        P(),
        P(),
        P(),
        P(dp, "x"),
        P(),
        P("x", dp),
        P(),
        token,
    )
    out_specs = (
        token,
        token,
        P(),
        P(),
        P(None, dp, "x"),
        P(),
        P("x", dp),
        P(),
        P(),
        P(),
        P(dp, "x"),
        P(),
        P("x", dp),
        P(),
    )
    return jax.shard_map(shards, mesh=inner, in_specs=in_specs, out_specs=out_specs, check_vma=False)
```

```python
import functools
import math

import jax
import jax.numpy as jnp
from jax import lax
from jax.experimental import pallas as pl
from jax.experimental.pallas import tpu as pltpu
from jax.sharding import Mesh, PartitionSpec as P

HD = 64
LEN_MIN = 864
EPS = 1e-05
LANES = 128
BLOCK = 256
MASKED = -1000000000.0
F32 = jnp.float32
BF16 = jnp.bfloat16
NN = (((1,), (0,)), ((), ()))
NT = (((1,), (1,)), ((), ()))
TN = (((0,), (0,)), ((), ()))


def dot(left, right, dims=NN):
    return lax.dot_general(left, right, dims, preferred_element_type=F32)


def norm_stats(values):
    center = values - jnp.mean(values, axis=-1, keepdims=True)
    inverse = lax.rsqrt(jnp.mean(center * center, axis=-1, keepdims=True) + EPS)
    return center * inverse, inverse


def head_part(values, head):
    lane = lax.broadcasted_iota(jnp.int32, (1, LANES), 1)
    keep = (lane < HD) if head == 0 else (lane >= HD)
    return jnp.where(keep, values, jnp.zeros_like(values))


def lane_block(first):
    return pl.ds(pl.multiple_of(first, LANES), LANES)


def row_half(index, rows):
    return pl.ds(pl.multiple_of(index * rows, rows), rows)


def span(block, size=BLOCK):
    return slice(block * size, (block + 1) * size)


def vmem():
    return pl.BlockSpec(memory_space=pltpu.VMEM)


def smem():
    return pl.BlockSpec(memory_space=pltpu.SMEM)


def limit(mib):
    return pltpu.CompilerParams(vmem_limit_bytes=mib * 1024 * 1024)


def project_kernel(left, weight, out):
    out[...] = dot(left[...], weight[...], NT).astype(out.dtype)


def project(left, weight, name):
    return pl.pallas_call(
        project_kernel,
        in_specs=[vmem()] * 2,
        out_specs=vmem(),
        out_shape=jax.ShapeDtypeStruct((left.shape[0], weight.shape[0]), BF16),
        compiler_params=limit(16),
        cost_estimate=cost(0.1),
        name=name,
    )(left, weight)


def cost(microseconds):
    return pl.CostEstimate(flops=int(microseconds * 1.1e9), transcendentals=0, bytes_accessed=1)


def fill_halves(target, core, own, other):
    rows = own.shape[0]
    target[row_half(core, rows), :] = own[...]
    target[row_half(1 - core, rows), :] = other[...]


def split_halves(source, core, own, other):
    rows = own.shape[0]
    own[...] = source[row_half(core, rows), :]
    other[...] = source[row_half(1 - core, rows), :]


def attend_forward_kernel(info, qkv_own, qkv_other, out_own, out_other, qkv, out):
    length, core = info[0], info[1]
    blocks = qkv.shape[0] // BLOCK
    fill_halves(qkv, core, qkv_own, qkv_other)

    def part(block, which):
        return qkv[span(block), span(which, LANES)]

    column = lax.broadcasted_iota(jnp.int32, (1, BLOCK), 1)
    row = lax.broadcasted_iota(jnp.int32, (BLOCK, 1), 0)

    def score(block, head):
        query = head_part(part(block, 0), head) * jnp.asarray(0.125, BF16)
        last = jnp.minimum(row + block * BLOCK, length - 1)
        scores = []
        for other in range(block + 1):
            piece = dot(query, part(other, 1), NT)
            if other == block or (other + 1) * BLOCK > LEN_MIN:
                piece = jnp.where(column + other * BLOCK <= last, piece, MASKED)
            scores.append(piece)
        return scores

    tasks = [(block, head) for block in range(blocks) for head in range(2)]
    upcoming = score(*tasks[0])
    kept = None
    for place, (block, head) in enumerate(tasks):
        scores = upcoming
        if place + 1 < len(tasks):
            upcoming = score(*tasks[place + 1])
        top = functools.reduce(jnp.maximum, scores)
        top = jnp.max(top, axis=1, keepdims=True)
        weights = [jnp.exp(piece - top) for piece in scores]
        total = jnp.sum(functools.reduce(jnp.add, weights), axis=1, keepdims=True)
        mixed = functools.reduce(
            jnp.add,
            [
                dot(weight.astype(BF16), head_part(part(other, 2), head))
                for other, weight in enumerate(weights)
            ],
        )
        mixed = mixed / total
        if head == 0:
            kept = mixed
        else:
            out[span(block), :] = (kept + mixed).astype(BF16)
    split_halves(out, core, out_own, out_other)


def attend_forward(info, qkv_own, qkv_other):
    rows, width = qkv_own.shape[0], qkv_own.shape[1] // 3
    taken = pl.BlockSpec((rows, 3 * LANES), lambda pair: (0, pair))
    given = pl.BlockSpec((rows, LANES), lambda pair: (0, pair))
    shape = jax.ShapeDtypeStruct((rows, width), BF16)
    return pl.pallas_call(
        attend_forward_kernel,
        grid=(width // LANES,),
        in_specs=[smem(), taken, taken],
        out_specs=[given, given],
        out_shape=[shape, shape],
        scratch_shapes=[
            pltpu.VMEM((2 * rows, 3 * LANES), BF16),
            pltpu.VMEM((2 * rows, LANES), BF16),
        ],
        compiler_params=limit(32),
        cost_estimate=cost(0.1),
        name="attend_forward",
    )(info, qkv_own, qkv_other)


def attend_backward_kernel(
    info,
    qkv_own,
    qkv_other,
    grad_own,
    grad_other,
    back_own,
    back_other,
    sums,
    qkv,
    grad,
    back,
    key_sum,
    value_sum,
):
    length, core = info[0], info[1]
    blocks = qkv.shape[0] // BLOCK
    fill_halves(qkv, core, qkv_own, qkv_other)
    fill_halves(grad, core, grad_own, grad_other)
    key_sum[...] = jnp.zeros_like(key_sum)
    value_sum[...] = jnp.zeros_like(value_sum)
    eighth = jnp.asarray(0.125, BF16)

    def part(block, which):
        return qkv[span(block), span(which, LANES)]

    column = lax.broadcasted_iota(jnp.int32, (1, BLOCK), 1)
    row = lax.broadcasted_iota(jnp.int32, (BLOCK, 1), 0)

    def products(block, head):
        query = head_part(part(block, 0), head) * eighth
        mixed = head_part(grad[span(block), :], head)
        last = jnp.minimum(column + block * BLOCK, length - 1)
        scores, grads = [], []
        for other in range(block + 1):
            piece = dot(part(other, 1), query, NT)
            if other == block or (other + 1) * BLOCK > LEN_MIN:
                piece = jnp.where(row + other * BLOCK <= last, piece, MASKED)
            scores.append(piece)
            grads.append(dot(part(other, 2), mixed, NT))
        return query, mixed, scores, grads

    tasks = [(block, head) for block in range(blocks) for head in range(2)]
    upcoming = products(*tasks[0])
    kept = None
    for place, (block, head) in enumerate(tasks):
        query, mixed, scores, grads = upcoming
        if place + 1 < len(tasks):
            upcoming = products(*tasks[place + 1])
        top = jnp.max(functools.reduce(jnp.maximum, scores), axis=0, keepdims=True)
        weights = [jnp.exp(piece - top) for piece in scores]
        total = jnp.sum(functools.reduce(jnp.add, weights), axis=0, keepdims=True)
        inverse = 1.0 / total
        weights = [weight * inverse for weight in weights]
        products_sum = functools.reduce(jnp.add, [w * g for w, g in zip(weights, grads)])
        inner = jnp.sum(products_sum, axis=0, keepdims=True)
        query_sum = None
        for other in range(block + 1):
            weight = weights[other]
            change = (weight * (grads[other] - inner)).astype(BF16)
            value_sum[span(other), :] += dot(weight.astype(BF16), mixed)
            key_sum[span(other), :] += dot(change, query)
            piece = dot(change, head_part(part(other, 1), head) * eighth, TN)
            query_sum = piece if query_sum is None else query_sum + piece
        if head == 0:
            kept = query_sum
        else:
            back[span(block), span(0, LANES)] = (kept + query_sum).astype(BF16)
    back[:, span(1, LANES)] = key_sum[...].astype(BF16)
    back[:, span(2, LANES)] = value_sum[...].astype(BF16)
    split_halves(back, core, back_own, back_other)
    sums[...] = jnp.sum(back[...].astype(F32), axis=0, keepdims=True)


def attend_backward(pair, info, qkv_own, qkv_other, grad_own, grad_other):
    rows = grad_own.shape[0]
    qkv_spec = pl.BlockSpec((rows, 3 * LANES), lambda step: (0, pair))
    grad_spec = pl.BlockSpec((rows, LANES), lambda step: (0, pair))
    shape = jax.ShapeDtypeStruct((rows, 3 * LANES), BF16)
    return pl.pallas_call(
        attend_backward_kernel,
        grid=(1,),
        in_specs=[smem(), qkv_spec, qkv_spec, grad_spec, grad_spec],
        out_specs=[vmem(), vmem(), vmem()],
        out_shape=[shape, shape, jax.ShapeDtypeStruct((1, 3 * LANES), F32)],
        scratch_shapes=[
            pltpu.VMEM((2 * rows, 3 * LANES), BF16),
            pltpu.VMEM((2 * rows, LANES), BF16),
            pltpu.VMEM((2 * rows, 3 * LANES), BF16),
            pltpu.VMEM((2 * rows, LANES), F32),
            pltpu.VMEM((2 * rows, LANES), F32),
        ],
        compiler_params=limit(32),
        cost_estimate=cost(13),
        name=f"attend_backward_{pair}",
    )(info, qkv_own, qkv_other, grad_own, grad_other)


def feed_kernel(two, grad, weight, bias, active, grad_pre, mlp, back, bias_sum):
    hidden = active.shape[1]
    slope = math.sqrt(2.0 / math.pi)
    cubic = slope * 0.044715
    for chunk in range(hidden // BLOCK):
        here = span(chunk)
        there = slice(hidden + chunk * BLOCK, hidden + (chunk + 1) * BLOCK)
        pre = dot(two[...], weight[:, here]) + bias[:, here]
        grad_active = dot(grad[...], weight[:, there])
        square = pre * pre
        half = 0.5 + 0.5 * jnp.tanh(pre * (slope + cubic * square))
        value = pre * half
        change = half + (value - value * half) * (2.0 * slope + (6.0 * cubic) * square)
        active[:, here] = value.astype(BF16)
        low = (grad_active * change).astype(BF16)
        grad_pre[:, here] = low
        bias_sum[:, here] = jnp.sum(low.astype(F32), axis=0, keepdims=True)
    for chunk in range(mlp.shape[1] // BLOCK):
        here = span(chunk)
        back[:, here] = dot(grad_pre[...], weight[here, :hidden], NT).astype(back.dtype)
        mlp[:, here] = dot(active[...], weight[here, hidden : 2 * hidden], NT).astype(mlp.dtype)


def feed(two, grad, weight, bias, result, name):
    rows, width = two.shape
    hidden = bias.shape[1]
    low = jax.ShapeDtypeStruct((rows, hidden), BF16)
    terms = jax.ShapeDtypeStruct((rows, width), result)
    return pl.pallas_call(
        feed_kernel,
        in_specs=[vmem()] * 4,
        out_specs=[vmem()] * 5,
        out_shape=[low, low, terms, terms, jax.ShapeDtypeStruct((1, hidden), F32)],
        compiler_params=limit(24),
        cost_estimate=cost(12),
        name=name,
    )(two, grad, weight, bias)


def weight_grads_kernel(count, shard, order, *refs):
    lefts_own, lefts_other = refs[:count], refs[count : 2 * count]
    rights_own, rights_other = refs[2 * count : 3 * count], refs[3 * count : 4 * count]
    out, total = refs[4 * count], refs[4 * count + 1]
    first = 0
    for term in range(count):
        columns = rights_own[term].shape[1]
        for chunk in range(total.shape[0] // BLOCK):
            here = span(chunk)
            piece = dot(lefts_own[term][:, here], rights_own[term][...], TN)
            piece += dot(lefts_other[term][:, here], rights_other[term][...], TN)
            total[here, first : first + columns] = piece.astype(BF16)
        first += columns
    if shard is None:
        out[...] = total[...]
        return
    for place in range(total.shape[0] // shard):
        start = pl.multiple_of(order[place] * shard, 16)
        out[span(place, shard), :] = total[pl.ds(start, shard), :]


def weight_grads(order, terms, name):
    width = terms[0][0].shape[1]
    columns = sum(term[2].shape[1] for term in terms)
    shard = None if order is None else width // order.shape[0]
    order = jnp.zeros((1,), jnp.int32) if order is None else order
    operands = [term[kind] for kind in range(4) for term in terms]
    return pl.pallas_call(
        functools.partial(weight_grads_kernel, len(terms), shard),
        in_specs=[smem()] + [vmem()] * len(operands),
        out_specs=vmem(),
        out_shape=jax.ShapeDtypeStruct((width, columns), BF16),
        scratch_shapes=[pltpu.VMEM((width, columns), BF16)],
        compiler_params=limit(24),
        cost_estimate=cost(0.1),
        name=name,
    )(order, *operands)


def norm_back_kernel(values, back_own, back_received, extra, gain, low, sums):
    for chunk in range(values.shape[0] // BLOCK):
        here = span(chunk)
        normed, inverse = norm_stats(values[here, :].astype(F32))
        grad = back_own[here, :].astype(F32) + back_received[here, :].astype(F32)
        scaled = grad * gain[...]
        added = extra[here, :].astype(F32)
        result = added + inverse * (
            scaled
            - jnp.mean(scaled, axis=-1, keepdims=True)
            - normed * jnp.mean(scaled * normed, axis=-1, keepdims=True)
        )
        rounded = result.astype(BF16)
        low[here, :] = rounded
        for place, item in enumerate((added, grad * normed, grad, rounded.astype(F32))):
            item = jnp.sum(item, axis=0, keepdims=True)
            if chunk == 0:
                sums[place : place + 1, :] = item
            else:
                sums[place : place + 1, :] += item


def norm_back(values, back_own, back_received, extra, gain, name):
    shapes = [
        jax.ShapeDtypeStruct(values.shape, BF16),
        jax.ShapeDtypeStruct((8, values.shape[1]), F32),
    ]
    return pl.pallas_call(
        norm_back_kernel,
        in_specs=[vmem()] * 5,
        out_specs=[vmem()] * len(shapes),
        out_shape=shapes,
        compiler_params=limit(16),
        cost_estimate=cost(0.1),
        name=name,
    )(values, back_own, back_received, extra, gain[None])


def early_kernel(info, sums, up_own, up_other, out):
    core = info[1]
    half = out.shape[1]
    for place in range(4):
        for side in range(2):
            out[2 * place + side : 2 * place + side + 1, :] = sums[place : place + 1, span(side, half)]
    for place in range(4):
        item = up_own[:, span(place, half)] + up_other[:, span(place, half)]
        out[8 + place : 9 + place, :] = jnp.where(core == 0, item, 0.0)
        out[12 + place : 13 + place, :] = jnp.where(core == 0, 0.0, item)


def late_kernel(info, sums, *refs):
    core = info[1]
    pairs, out = refs[:-1], refs[-1]
    half = out.shape[1]
    out[...] = jnp.zeros_like(out)
    for place in range(2):
        for side in range(2):
            out[2 * place + side : 2 * place + side + 1, :] = sums[place + 1 : place + 2, span(side, half)]
    for index, pair in enumerate(pairs):
        here = span(index, LANES)
        for place, which in enumerate((0, 2)):
            item = pair[:, span(which, LANES)]
            first = 4 + 2 * place
            out[first : first + 1, here] = jnp.where(core == 0, item, 0.0)
            out[first + 1 : first + 2, here] = jnp.where(core == 0, 0.0, item)


def pack(kernel, info, operands, half, name):
    return pl.pallas_call(
        kernel,
        in_specs=[smem()] + [vmem()] * len(operands),
        out_specs=vmem(),
        out_shape=jax.ShapeDtypeStruct((16, half), F32),
        cost_estimate=cost(0.1),
        name=name,
    )(info, *operands)


def place_kernel(shard, order, *refs):
    pieces, out = refs[:-1], refs[-1]
    place = 0
    for piece in pieces:
        for step in range(piece.shape[0] // shard):
            start = pl.multiple_of(order[place] * shard, 16)
            out[pl.ds(start, shard), :] = piece[span(step, shard), :]
            place += 1


def place_blocks(order, pieces):
    shard, columns = pieces[0].shape
    return pl.pallas_call(
        functools.partial(place_kernel, shard),
        in_specs=[smem()] + [vmem()] * len(pieces),
        out_specs=vmem(),
        out_shape=jax.ShapeDtypeStruct((shard * order.shape[0], columns), BF16),
        cost_estimate=cost(0.1),
        name="place_blocks",
    )(order, *pieces)


class Cube:
    def __init__(self, shard_rows):
        self.shard_rows = shard_rows
        self.zy = lax.axis_size("zy")
        self.cores = lax.axis_size("core")
        self.size = self.zy * lax.axis_size("x")
        self.bits = self.size.bit_length() - 1
        self.direct = self.size == 1 << self.bits and self.bits >= 2 and shard_rows % 16 == 0
        outer = list(range(self.bits - 1, 1, -1))
        self.dims = [outer + [0, 1], outer + [1, 0]]
        if self.direct:
            masks = [
                [sum(1 << dims[step] for step in range(self.bits) if place >> step & 1) for place in range(self.size)]
                for dims in self.dims
            ]
            mine = lax.axis_index("zy") * 2 + lax.axis_index("x")
            core = lax.axis_index("core")
            chosen = jnp.where(core == 0, jnp.array(masks[0], jnp.int32), jnp.array(masks[1], jnp.int32))
            self.order = jnp.bitwise_xor(mine.astype(jnp.int32), chosen)
        else:
            blocks = shard_rows * self.size // 48
            self.order = jnp.arange(blocks, dtype=jnp.int32)

    def send(self, values, step):
        pairs = []
        for zy in range(self.zy):
            for core in range(self.cores):
                for x in range(2):
                    other = (zy * 2 + x) ^ (1 << self.dims[core][step])
                    pairs.append(((zy * 2 + core) * 2 + x, (other // 2 * 2 + core) * 2 + other % 2))
        return lax.ppermute(values, ("zy", "core", "x"), pairs)

    def joined(self, pieces):
        return pieces[0] if len(pieces) == 1 else jnp.concatenate(pieces, axis=0)

    def grow(self, pieces, payload=None):
        payload = self.joined(pieces) if payload is None else payload
        return pieces + [self.send(payload, len(pieces) - 1)]

    def finish(self, pieces):
        if not self.direct:
            return lax.all_gather(pieces[0], ("zy", "x"), axis=0, tiled=True)
        return place_blocks(self.order, pieces)

    def payload(self, values):
        return values[values.shape[0] // 2 :]

    def reduce_send(self, payload, step):
        return self.send(payload, self.bits - 1 - step)

    def merge(self, values, received):
        return (values[: values.shape[0] // 2].astype(F32) + received.astype(F32)).astype(BF16)

    def scatter(self, values):
        return lax.psum_scatter(values, ("zy", "x"), scatter_dimension=0, tiled=True)

    def total(self, values):
        if not self.direct:
            return lax.psum(values, ("zy", "core", "x"))
        for step in range(self.bits):
            values = values + self.send(values, step)
        return values + exchange(values)


def swap_small(values):
    return lax.ppermute(values, ("core", "x"), [(0, 0), (1, 2), (2, 1), (3, 3)])


def swap_send(values):
    return lax.ppermute(values, ("core", "x"), [(1, 2), (2, 1)])


def swap_pick(values, received):
    return jnp.where(lax.axis_index("core") == lax.axis_index("x"), values, received)


def swap(values):
    return swap_pick(values, swap_send(values))


def exchange(values):
    return lax.ppermute(values, "core", [(0, 1), (1, 0)])


def tie(values, other):
    return lax.optimization_barrier((values, other))


def shards(
    hidden_in,
    seq_lens,
    ln1_gain,
    ln1_bias,
    w_qkv,
    bias_qv,
    w_out,
    bias_out,
    ln2_gain,
    ln2_bias,
    w_up,
    bias_up,
    w_down,
    bias_down,
    grad_out,
):
    core = lax.axis_index("core")
    group = ("zy", "x")
    rows, width = hidden_in.shape
    shard_rows = w_up.shape[0]
    head_cols = w_qkv.shape[2]
    hidden_cols = w_up.shape[1]
    pairs = head_cols // LANES
    qkv_cols = 3 * head_cols
    cube = Cube(shard_rows)

    qkv_shard = w_qkv.reshape(3, shard_rows, pairs, LANES).transpose(1, 2, 0, 3).reshape(shard_rows, qkv_cols)
    shard = swap(jnp.concatenate([qkv_shard, w_out.T, w_up, w_down.T], axis=1))
    attn_cols = qkv_cols + head_cols
    hidden_in, shard = tie(hidden_in, shard)
    residual_low = swap(hidden_in)
    attn_pieces = [shard[:, :attn_cols]]
    rest_weights = lax.all_gather(shard[:, attn_cols:], group, axis=0, tiled=True)
    length = swap_small(seq_lens)[0]
    if cube.direct:
        for step in range(cube.bits):
            payload = cube.joined(attn_pieces)
            if step == cube.bits - 2:
                payload, residual_low = tie(payload, residual_low)
            attn_pieces = cube.grow(attn_pieces, payload)
    grad_out, attn_pieces[-1] = tie(grad_out, attn_pieces[-1])
    attn_weights = cube.finish(attn_pieces)
    qkv_weight, out_weight = attn_weights[:, :qkv_cols], attn_weights[:, qkv_cols:]
    grad_low = swap(grad_out)
    info = jnp.stack([length, core.astype(jnp.int32)])

    residual = residual_low.astype(F32)
    unit_one, _ = norm_stats(residual)
    norm_own = (unit_one * ln1_gain + ln1_bias).astype(BF16)
    norm_other = exchange(norm_own)
    bias_here = lax.dynamic_slice_in_dim(bias_qv, core * head_cols, head_cols, 1)
    qkv_bias = jnp.stack([bias_here[0], jnp.zeros((head_cols,), F32), bias_here[1]])
    qkv_bias = qkv_bias.reshape(3, pairs, LANES).transpose(1, 0, 2).reshape(qkv_cols)
    qkv_own = (dot(norm_own, qkv_weight) + qkv_bias).astype(BF16)
    qkv_other = (dot(norm_other, qkv_weight) + qkv_bias).astype(BF16)
    mixed_own, mixed_other = attend_forward(info, qkv_own, qkv_other)
    attn_received = exchange(dot(mixed_other, out_weight, NT).astype(BF16))
    hidden = residual + (dot(mixed_own, out_weight, NT) + attn_received.astype(F32)) + bias_out
    rest_weights, hidden = tie(rest_weights, hidden)
    unit_two, _ = norm_stats(hidden)
    two_own = (unit_two * ln2_gain + ln2_bias).astype(BF16)
    two_other = exchange(two_own)
    bias_up_here = lax.dynamic_slice_in_dim(bias_up, core * hidden_cols, hidden_cols, 0)[None]

    slots = core * rows + jnp.arange(rows, dtype=jnp.int32)
    grad_own = jnp.where((slots < length)[:, None], grad_low, jnp.zeros_like(grad_low))
    grad_other = exchange(grad_own)

    active_other, grad_pre_other, mlp_other, back_two_other, up_sum_other = feed(
        two_other, grad_other, rest_weights, bias_up_here, BF16, "feed_other"
    )
    back_two_received = exchange(back_two_other)
    mlp_received = exchange(mlp_other)
    active_own, grad_pre_own, mlp_own, back_two_own, up_sum_own = feed(
        two_own, grad_own, rest_weights, bias_up_here, BF16, "feed_own"
    )
    mlp_sum = mlp_own.astype(F32) + mlp_received.astype(F32)
    layer_here = (hidden + mlp_sum + bias_down).astype(BF16)
    layer_there = swap_send(layer_here)

    up_grads = weight_grads(
        cube.order, [(two_own, two_other, grad_pre_own, grad_pre_other)], "up_grads"
    )
    if cube.direct:
        payload, back_two_own = tie(cube.payload(up_grads), back_two_own)
        up_received = cube.reduce_send(payload, 0)
    attn_grad_own, sums = norm_back(
        hidden, back_two_own, back_two_received, grad_own, ln2_gain, "norm_two_back"
    )
    attn_grad_other = exchange(attn_grad_own)
    first_grads = weight_grads(
        cube.order,
        [
            (grad_own, grad_other, active_own, active_other),
            (attn_grad_own, attn_grad_other, mixed_own, mixed_other),
        ],
        "down_out_grads",
    )
    grad_mixed_own = dot(attn_grad_own, out_weight).astype(BF16)
    grad_mixed_other = dot(attn_grad_other, out_weight).astype(BF16)
    early = pack(early_kernel, info, [sums, up_sum_own, up_sum_other], width // 2, "early_sums")
    if cube.direct:
        up_received, first_grads = tie(up_received, first_grads)
        early = early.astype(BF16)
    else:
        early = cube.total(early)
        first_grads = cube.scatter(first_grads)
        up_grads = cube.scatter(up_grads)

    def finish_step(grads, small, received):
        grads = cube.merge(grads, received[:-16])
        small = (small.astype(F32) + received[-16:, : small.shape[1]].astype(F32)).astype(BF16)
        return grads, small

    backs_own, backs_other, back_sums = [], [], []
    grad_pair = (grad_mixed_own, grad_mixed_other)
    steps = cube.bits if cube.direct else 0
    last_grads, pending = None, None
    for pair in range(max(pairs + 1, steps)):
        if pending is not None:
            first_grads, early = finish_step(first_grads, early, pending)
            pending = None
        received = None
        if pair < steps:
            padding = ((0, 0), (0, first_grads.shape[1] - early.shape[1]))
            payload = jnp.concatenate([cube.payload(first_grads), jnp.pad(early, padding)], axis=0)
            payload, grad_pair = tie(payload, grad_pair)
            received = cube.reduce_send(payload, pair)
        if pair < pairs:
            back_own, back_other, back_sum = attend_backward(pair, info, qkv_own, qkv_other, *grad_pair)
            if received is not None:
                received, back_own = tie(received, back_own)
            backs_own.append(back_own)
            backs_other.append(back_other)
            back_sums.append(back_sum)
        if pair == pairs:
            back_own = jnp.concatenate(backs_own, axis=1)
            back_other = jnp.concatenate(backs_other, axis=1)
            last_grads = weight_grads(
                cube.order, [(norm_own, norm_other, back_own, back_other)], "last_weight_grads"
            )
            if cube.direct:
                payload, back_other = tie(cube.payload(last_grads), back_other)
                last_received = cube.reduce_send(payload, 0)
            layer_there, back_other = tie(layer_there, back_other)
            layer_out = swap_pick(layer_here, layer_there)
            back_one_received = exchange(project(back_other, qkv_weight, "back_one_other"))
            grad_input, sums = norm_back(
                residual_low,
                project(back_own, qkv_weight, "back_one_own"),
                back_one_received,
                attn_grad_own,
                ln1_gain,
                "norm_one_back",
            )
        if received is not None and pair == pairs:
            pending = received
            received = None
        if received is not None:
            first_grads = cube.merge(first_grads, received[:-16])
            if pair == 0:
                up_grads = cube.merge(up_grads, up_received)
                first_grads = jnp.concatenate([up_grads, first_grads], axis=1)
            early = (early.astype(F32) + received[-16:, : early.shape[1]].astype(F32)).astype(BF16)
    if not cube.direct:
        first_grads = jnp.concatenate([up_grads, first_grads], axis=1)
    late = pack(late_kernel, info, [sums] + back_sums, width // 2, "late_sums")
    if cube.direct:
        late = late + cube.reduce_send(late, 0)
        last_received, grad_input = tie(last_received, grad_input)
    final_low = swap(grad_input)
    if cube.direct:
        last_grads = cube.merge(last_grads, last_received)
        late = late.astype(BF16)
        for step in range(1, steps):
            padding = ((0, 0), (0, qkv_cols - late.shape[1]))
            payload = jnp.concatenate([cube.payload(last_grads), jnp.pad(late, padding)], axis=0)
            received = cube.reduce_send(payload, step)
            if step == steps - 1:
                received, final_low = tie(received, final_low)
                if pending is not None:
                    received, pending = tie(received, pending)
            last_grads = cube.merge(last_grads, received[:-16])
            late = (late.astype(F32) + received[-16:, : late.shape[1]].astype(F32)).astype(BF16)
        if pending is not None:
            first_grads, early = finish_step(first_grads, early, pending)
        both = jnp.concatenate([late, early], axis=1).astype(F32)
        both = both + exchange(both)
        late, early = both[:, : late.shape[1]], both[:, late.shape[1] :]
    else:
        last_grads = cube.scatter(last_grads)
        late = cube.total(late)
    done_grads = swap(jnp.concatenate([first_grads, last_grads], axis=1))
    done_grads, last_grads = done_grads[:, :-qkv_cols], done_grads[:, -qkv_cols:]
    grad_input = final_low.astype(F32)

    early = early.reshape(-1)
    down_bias, gain_two, shift_two, out_bias, up_bias = jnp.split(early, [width * n for n in range(1, 5)])
    late = late.reshape(-1)[: 4 * width]
    gain_one, shift_one, qv_bias = jnp.split(late, [width, 2 * width])
    grad_w_qkv = last_grads.reshape(shard_rows, pairs, 3, LANES).transpose(2, 0, 1, 3)
    grad_w_qkv = grad_w_qkv.reshape(3, shard_rows, head_cols).astype(F32)
    grad_w_up = done_grads[:, :hidden_cols].astype(F32)
    grad_w_down = done_grads[:, hidden_cols : 2 * hidden_cols].T.astype(F32)
    grad_w_out = done_grads[:, 2 * hidden_cols :].T.astype(F32)
    return (
        layer_out,
        grad_input,
        gain_one,
        shift_one,
        grad_w_qkv,
        qv_bias.reshape(2, width),
        grad_w_out,
        out_bias,
        gain_two,
        shift_two,
        grad_w_up,
        up_bias,
        grad_w_down,
        down_bias,
    )


def solution(mesh):
    cores = 2
    devices = mesh.devices
    inner = Mesh(devices.reshape(devices.shape[0] // cores, cores, devices.shape[1]), ("zy", "core", "x"))
    dp = ("zy", "core")
    token = P(("zy", "core", "x"), None)
    in_specs = (
        token,
        P(dp),
        P(),
        P(),
        P(None, dp, "x"),
        P(),
        P("x", dp),
        P(),
        P(),
        P(),
        P(dp, "x"),
        P(),
        P("x", dp),
        P(),
        token,
    )
    out_specs = (
        token,
        token,
        P(),
        P(),
        P(None, dp, "x"),
        P(),
        P("x", dp),
        P(),
        P(),
        P(),
        P(dp, "x"),
        P(),
        P("x", dp),
        P(),
    )
    return jax.shard_map(shards, mesh=inner, in_specs=in_specs, out_specs=out_specs, check_vma=False)
```
